32 devices in a mesh: gx: 4 (over z), gy: 4 (over y, x), gz: 2 (over core).
Axes of the slice: x: 2, y: 2, z: 4, core: 2. Of those that a mesh axis runs over, the one named last changes fastest.
Arguments:
- electric: float32 [3, 32, 64, 256], P(None, 'gx', 'gy', 'gz'), may hold values from -6 to 6
- permittivity_class: int32 [32, 64, 256], P('gx', 'gy', 'gz'), may hold values from 0 to 3
- cell_index: int32 [4, 64, 128], P('gx', ('gy', 'gz')), may hold values from 0 to 16384, as said below
- polarization: float32 [2, 3, 4, 64, 128], P(None, None, 'gx', ('gy', 'gz')), may hold values from -3 to 3
- populations: float32 [2, 4, 64, 128], P(None, 'gx', ('gy', 'gz')), may hold values from 0.05 to 0.45
- resonance: float32 [4, 64, 128], P('gx', ('gy', 'gz')), may hold values from 0.5 to 1.5
- dephasing: float32 [4, 64, 128], P('gx', ('gy', 'gz')), may hold values from 0.05 to 0.8
- coupling: float32 [4, 64, 128], P('gx', ('gy', 'gz')), may hold values from 0.1 to 1
- pump_rate: float32 [4, 64, 128], P('gx', ('gy', 'gz')), may hold values from 0.02 to 0.4
Outputs:
- electric_out: float32 [3, 32, 64, 256], P(None, 'gx', 'gy', 'gz')
- magnetic_out: float32 [3, 32, 64, 256], P(None, 'gx', 'gy', 'gz')
- polarization_out: float32 [2, 3, 4, 64, 128], P(None, None, 'gx', ('gy', 'gz'))
- populations_out: float32 [2, 4, 64, 128], P(None, 'gx', ('gy', 'gz'))
The draws below stay inside these ranges and needn't reach their ends.
Inputs may be any that keep to these rules, and one draw needn't show every extreme that they name: `cell_index`: A value below 16384 names the local cell (x 16 + y) * 128 + z of the target block; 16384 marks an empty slot. Every owner's buckets toward the devices of one index of gy, drawn from the seed, are full; each other bucket has an empty last slot.
All inputs are finite; a program needn't handle non-finite values.
Results may differ from the reference program's by a relative error of at most 0.0001.
Values sent between devices are 32-bit elements; how exact they have to be, the bound alone decides.
No kernel may reach another device: no remote copies, remote signals or barrier semaphores. Data moves between devices by JAX's collectives and lax.ppermute only.
A program may use at most 64 MiB of HBM per device.

```python
import math
import jax
import jax.numpy as jnp
from jax import lax

CX = 8
CY = 16
CZ = 128
STEPS = 4
SLOT = 128
NX = 32
NY = 64
NZ = 256
PEERS = 8
CELLS = 16384
N_GX = 4
N_GY = 4
N_GZ = 2


def draw_cell_index(key, part):
    slab_key = jax.random.fold_in(key, 11)
    live_key = jax.random.fold_in(key, 23)
    cell_key = jax.random.fold_in(key, 37)
    slab_row = jax.random.randint(slab_key, (), 0, N_GY)
    shape = (N_GX, PEERS * PEERS, SLOT)
    target = lax.broadcasted_iota(jnp.int32, shape, 1) % PEERS
    position = lax.broadcasted_iota(jnp.int32, shape, 2)
    in_slab = target // N_GZ == slab_row
    chosen = (jax.random.randint(live_key, shape, 0, 4) == 0) & (position < SLOT - 1)
    live = in_slab | chosen
    cells = jax.random.randint(cell_key, shape, 0, CELLS)
    return jnp.where(live, cells, CELLS).astype(jnp.int32)


def place_ends(entries, stream_key, smallest, largest):
    longest = entries.shape.index(max(entries.shape))
    spots = []
    for shift in (0, 1):
        where = [jax.random.randint(jax.random.fold_in(stream_key, axis), (), 0, length) for axis, length in enumerate(entries.shape)]
        where[longest] = (where[longest] + shift) % entries.shape[longest]
        spots.append(tuple(where))
    return entries.at[spots[0]].set(smallest).at[spots[1]].set(largest)


def level_of(rng, shape, pieces, least, top_value):
    gain = 1.0
    for axis_at, blocks in pieces:
        steps = jax.random.uniform(jax.random.fold_in(jax.random.fold_in(rng, 6), axis_at), (blocks,), jnp.float32, least / len(pieces), top_value / len(pieces))
        gain = gain * jnp.repeat(jnp.exp(steps), shape[axis_at] // blocks).reshape((-1,) + (1,) * (len(shape) - 1 - axis_at))
    return gain


def centred(stream_key, extent, scale, reach, pieces=(), dtype=jnp.bfloat16):
    loudness = level_of(stream_key, extent, pieces, -0.22, 0.18) if pieces else 1.0
    array = jax.random.normal(stream_key, extent, jnp.float32) * scale * loudness
    return jnp.minimum(jnp.maximum(array, -reach), reach).astype(dtype)


def setup_inputs(seed: int = 0) -> dict:
    keys = jax.random.split(jax.random.key(seed), 10)
    electric = centred(keys[0], (3, NX, NY, NZ), 1.0, 6.0, ((1, 4), (2, 4), (3, 2)), jnp.float32)
    permittivity_class = place_ends(jax.random.randint(keys[1], (NX, NY, NZ), 0, 4), jax.random.fold_in(keys[1], 1), 0, 3).astype(jnp.int32)
    cell_index = draw_cell_index(jax.random.fold_in(keys[9], 71), 0)
    polarization = centred(keys[3], (2, 3, N_GX, PEERS * PEERS, SLOT), 0.5, 3.0, ((2, 4), (3, 8)), jnp.float32)
    populations = jnp.clip(0.05 + 0.39999999 * jax.random.uniform(keys[4], (2, N_GX, PEERS * PEERS, SLOT), jnp.float32) ** level_of(keys[4], (2, N_GX, PEERS * PEERS, SLOT), ((1, 4), (2, 8)), -0.2, 0.2), 0.05, 0.45)
    resonance = jnp.clip(jnp.exp(math.log(1.5) - 1.0986123 * jax.random.uniform(keys[5], (N_GX, PEERS * PEERS, SLOT), jnp.float32) ** level_of(keys[5], (N_GX, PEERS * PEERS, SLOT), ((0, 4), (1, 8)), -0.2, 0.2)), 0.5, 1.5)
    dephasing = jnp.clip(jnp.exp(math.log(0.8) - 2.7725887 * jax.random.uniform(keys[6], (N_GX, PEERS * PEERS, SLOT), jnp.float32) ** level_of(keys[6], (N_GX, PEERS * PEERS, SLOT), ((0, 4), (1, 8)), -0.2, 0.2)), 0.05, 0.8)
    coupling = jnp.clip(jnp.exp(math.log(1.0) - 2.3025851 * jax.random.uniform(keys[7], (N_GX, PEERS * PEERS, SLOT), jnp.float32) ** level_of(keys[7], (N_GX, PEERS * PEERS, SLOT), ((0, 4), (1, 8)), -0.2, 0.2)), 0.1, 1.0)
    pump_rate = jnp.clip(jnp.exp(math.log(0.4) - 2.9957323 * jax.random.uniform(keys[8], (N_GX, PEERS * PEERS, SLOT), jnp.float32) ** level_of(keys[8], (N_GX, PEERS * PEERS, SLOT), ((0, 4), (1, 8)), -0.2, 0.2)), 0.02, 0.4)
    return {"electric": electric, "permittivity_class": permittivity_class, "cell_index": cell_index, "polarization": polarization, "populations": populations, "resonance": resonance, "dephasing": dephasing, "coupling": coupling, "pump_rate": pump_rate}


time_step = 0.5
pump_decay = 0.2
upper_decay = 0.02
work_share = 0.05
class_permittivity = (1.0, 2.1, 6.0, 12.25)


def inverse_permittivity(classes):
    inverse = jnp.zeros(classes.shape, jnp.float32)
    for number, epsilon in enumerate(class_permittivity):
        inverse = inverse + jnp.where(classes == number, 1.0 / epsilon, 0.0)
    return inverse


def combine_curl(along_x, along_y, along_z):
    return jnp.stack([along_y[2] - along_z[1], along_z[0] - along_x[2], along_x[1] - along_y[0]])


def curl_forward(electric):
    padded = jnp.pad(electric, ((0, 0), (0, 1), (0, 1), (0, 1)))
    return combine_curl(padded[:, 1:, :-1, :-1] - electric, padded[:, :-1, 1:, :-1] - electric, padded[:, :-1, :-1, 1:] - electric)


def curl_backward(magnetic):
    padded = jnp.pad(magnetic, ((0, 0), (1, 0), (1, 0), (1, 0)))
    return combine_curl(magnetic - padded[:, :-1, 1:, 1:], magnetic - padded[:, 1:, :-1, 1:], magnetic - padded[:, 1:, 1:, :-1])


def bloch_update(sample, current, previous, upper, pumped, resonance, dephasing, coupling, pump_rate):
    lower = 1.0 - upper - pumped
    damping = 0.5 * time_step * dephasing
    stiffness = (resonance * time_step) * (resonance * time_step)
    advanced = ((2.0 - stiffness) * current - (1.0 - damping) * previous + coupling * (time_step * time_step) * (lower - upper) * sample) / (1.0 + damping)
    work = jnp.sum(sample * (advanced - previous), axis=0) / (2.0 * time_step)
    pumped_next = pumped + time_step * (pump_rate * lower - pump_decay * pumped)
    upper_next = upper + time_step * (pump_decay * pumped - upper_decay * upper + work_share * work / resonance)
    return advanced, current, upper_next, pumped_next


def reference(electric, permittivity_class, cell_index, polarization, populations, resonance, dephasing, coupling, pump_rate):
    inverse = inverse_permittivity(permittivity_class)
    blocks = cell_index.reshape(N_GX, PEERS, PEERS, SLOT)
    owner_x = lax.broadcasted_iota(jnp.int32, blocks.shape, 0)
    target = lax.broadcasted_iota(jnp.int32, blocks.shape, 2)
    target_y = target // N_GZ
    target_z = target % N_GZ
    live = blocks < CELLS
    local = jnp.minimum(blocks, CELLS - 1)
    local_x = local // (CY * CZ)
    local_y = (local // CZ) % CY
    local_z = local % CZ
    global_cell = ((owner_x * CX + local_x) * NY + target_y * CY + local_y) * NZ + target_z * CZ + local_z
    flat_index = global_cell.reshape(-1).astype(jnp.int32)
    dropped = jnp.where(live, global_cell, NX * NY * NZ).reshape(-1).astype(jnp.int32)
    weight = live.reshape(-1).astype(jnp.float32)
    current = polarization[0].reshape(3, -1)
    previous = polarization[1].reshape(3, -1)
    upper = populations[0].reshape(-1)
    pumped = populations[1].reshape(-1)
    freq = resonance.reshape(-1)
    dephase = dephasing.reshape(-1)
    strength = coupling.reshape(-1)
    pumping = pump_rate.reshape(-1)
    magnetic = jnp.zeros_like(electric)
    for repeat in range(STEPS):
        magnetic = magnetic - time_step * curl_forward(electric)
        sample = electric.reshape(3, -1)[:, flat_index] * weight
        advanced, previous, upper, pumped = bloch_update(sample, current, previous, upper, pumped, freq, dephase, strength, pumping)
        change = advanced - previous
        current = advanced
        source = jnp.zeros((3, NX * NY * NZ), jnp.float32).at[:, dropped].add(change, mode="drop").reshape(electric.shape)
        electric = electric + inverse * (time_step * curl_backward(magnetic) - source)
    polar_out = jnp.stack([current, previous]).reshape(polarization.shape)
    popul_out = jnp.stack([upper, pumped]).reshape(populations.shape)
    return (electric, magnetic, polar_out, popul_out)
```

```python
import functools

import jax
import jax.numpy as jnp
from jax import lax
from jax.experimental import pallas as pl
from jax.experimental.pallas import tpu as pltpu
from jax.sharding import PartitionSpec as P

STEPS = 4
TIME_STEP = 0.5
PUMP_DECAY = 0.2
UPPER_DECAY = 0.02
WORK_SHARE = 0.05
CLASS_PERMITTIVITY = (1.0, 2.1, 6.0, 12.25)

WIDTHS = (STEPS,) * 3 + (STEPS - 1,) * 4 + (STEPS - 2,) * 4 + (STEPS - 3,) * 9
FIELDS = len(WIDTHS)
ALL_WIDTHS = WIDTHS + (STEPS,)
BASES = tuple(sum(ALL_WIDTHS[:i]) for i in range(FIELDS + 1))
LAYERS = sum(ALL_WIDTHS)
LANE_BASES = tuple(2 * sum(WIDTHS[:i]) for i in range(FIELDS))
LANES = 128
VMEM_LIMIT = 56 * 1024 * 1024


def inverse_permittivity(classes):
    inverse = jnp.zeros(classes.shape, jnp.float32)
    for number, epsilon in enumerate(CLASS_PERMITTIVITY):
        inverse = jnp.where(classes == number, 1.0 / epsilon, inverse)
    return inverse


def halves(value):
    high = value.astype(jnp.bfloat16)
    low = (value - high.astype(jnp.float32)).astype(jnp.bfloat16)
    return high, low


def write_one_hots(index, row_hot, depth_hot, rows, depth):
    shift = depth.bit_length() - 1
    buckets, slots = index.shape
    for b in range(buckets):
        row = lax.shift_right_logical(index[b : b + 1], shift)
        deep = lax.bitwise_and(index[b : b + 1], depth - 1)
        rows_at = lax.broadcasted_iota(jnp.int32, (rows, slots), 0)
        deep_at = lax.broadcasted_iota(jnp.int32, (depth, slots), 0)
        hot = jnp.where(rows_at == row, 1.0, 0.0).astype(jnp.bfloat16)
        span = slice(b * slots, (b + 1) * slots)
        row_hot[0:rows, span] = hot
        row_hot[rows : 2 * rows, span] = hot
        depth_hot[:, span] = jnp.where(deep_at == deep, 1.0, 0.0).astype(jnp.bfloat16)


def gather_cells(cells, index, row_hot, depth):
    buckets, slots = index.shape
    parts = []
    for block in cells:
        high, low = halves(block.T)
        parts.append(jnp.concatenate([high, low], axis=1))
    left = jnp.concatenate(parts, axis=0)
    samples = [[], [], []]
    group = 2 if buckets % 2 == 0 else 1
    for start in range(0, buckets, group):
        span = slice(start * slots, (start + group) * slots)
        picked = jnp.dot(left, row_hot[:, span], preferred_element_type=jnp.float32)
        for b in range(start, start + group):
            deep = lax.bitwise_and(index[b : b + 1], depth - 1)
            hit = lax.broadcasted_iota(jnp.int32, (depth, slots), 0) == deep
            for c in range(3):
                part = picked[c * depth : (c + 1) * depth, (b - start) * slots : (b - start + 1) * slots]
                samples[c].append(jnp.sum(jnp.where(hit, part, 0.0), axis=0, keepdims=True))
    return [jnp.concatenate(rows, axis=0) for rows in samples]


def flat_row(value):
    buckets = value.shape[0]
    return jnp.concatenate([value[b : b + 1] for b in range(buckets)], axis=1)


def scatter_cells(values, row_hot, depth_hot, rows):
    hot = row_hot[0:rows, :]
    hot = jnp.concatenate([hot, hot], axis=1)
    deep = depth_hot[...]
    out = []
    for value in values:
        high, low = halves(flat_row(value))
        spread = jnp.concatenate([deep * high, deep * low], axis=1)
        out.append(
            lax.dot_general(
                hot, spread, (((1,), (1,)), ((), ())), preferred_element_type=jnp.float32
            )
        )
    return out


def emitter_constants(arrived):
    freq, dephase, strength, pumping = [arrived[:, f, :] for f in range(8, 12)]
    damping = 0.5 * TIME_STEP * dephase
    stiffness = freq * TIME_STEP * (freq * TIME_STEP)
    scale = 1.0 + damping
    keep = (2.0 - stiffness) / scale
    back = (1.0 - damping) / scale
    drive = strength * (TIME_STEP * TIME_STEP) / scale
    share = WORK_SHARE / freq
    return keep, back, drive, share, pumping


def bloch_step(sample, current, previous, upper, pumped, constants):
    keep, back, drive, share, pumping = constants
    lower = 1.0 - upper - pumped
    push = drive * (lower - upper)
    advanced = [keep * c - back * p + push * s for c, p, s in zip(current, previous, sample)]
    work = sum(s * (a - p) for s, a, p in zip(sample, advanced, previous)) / (2.0 * TIME_STEP)
    pumped_next = pumped + TIME_STEP * (pumping * lower - PUMP_DECAY * pumped)
    upper_next = upper + TIME_STEP * (
        PUMP_DECAY * pumped - UPPER_DECAY * upper + share * work
    )
    return advanced, current, upper_next, pumped_next


def pack_kernel(index, polar, popul, freq, dephase, strength, pumping, out):
    for i in range(2):
        for c in range(3):
            out[:, 3 * i + c, :] = polar[i, c, 0]
    for i in range(2):
        out[:, 6 + i, :] = popul[i, 0]
    for f, source in enumerate((freq, dephase, strength, pumping)):
        out[:, 8 + f, :] = source[0]
    out[:, 12, :] = index[0].astype(jnp.float32)


def first_kernel(arrived, electric, classes, fields, strip, states, row_hot, depth_hot):
    _, nx, ny, depth = electric.shape
    rows = nx * ny
    index = arrived[:, 12, :].astype(jnp.int32)
    write_one_hots(index, row_hot, depth_hot, rows, depth)
    for c in range(3):
        fields[c] = electric[c].reshape(rows, depth)
    fields[3] = inverse_permittivity(classes[...].reshape(rows, depth))
    sample = gather_cells([fields[c] for c in range(3)], index, row_hot, depth)
    constants = emitter_constants(arrived)
    keep, back, drive, share, pumping = constants
    start = [arrived[:, c, :] for c in range(3)]
    before = [arrived[:, 3 + c, :] for c in range(3)]
    now, _, upper, pumped = bloch_step(
        sample, start, before, arrived[:, 6, :], arrived[:, 7, :], constants
    )
    for c in range(3):
        states[c] = now[c]
        states[3 + c] = start[c]
    states[6] = upper
    states[7] = pumped
    lower = 1.0 - upper - pumped
    push = drive * (lower - upper)
    pumped_after = pumped + TIME_STEP * (pumping * lower - PUMP_DECAY * pumped)
    upper_free = upper + TIME_STEP * (PUMP_DECAY * pumped - UPPER_DECAY * upper)
    free = [keep * n - back * s for n, s in zip(now, start)]
    values = [n - s for n, s in zip(now, start)]
    values += [f - n for f, n in zip(free, now)]
    values.append(push)
    values += [(keep - 1.0) * f - back * n for f, n in zip(free, now)]
    values.append((keep - 1.0) * push)
    values.append(drive * (1.0 - pumped_after - 2.0 * upper_free))
    values += [-drive * share * (f - s) for f, s in zip(free, start)]
    values.append(-drive * share * push)
    for number, block in enumerate(scatter_cells(values, row_hot, depth_hot, rows)):
        fields[4 + number] = block
    lane = lax.broadcasted_iota(jnp.int32, (rows, depth), 1)
    packed = jnp.zeros((rows, depth), jnp.float32)
    for f, width in enumerate(WIDTHS):
        at = LANE_BASES[f]
        turned = pltpu.roll(fields[f], (at + width) % depth, 1)
        packed = jnp.where((lane >= at) & (lane < at + 2 * width), turned, packed)
    strip[...] = packed


def faces_x_kernel(nx, ny, count_z, fields, *refs):
    from_low, from_high, strip, low, high = refs
    rows, depth = strip.shape
    lane = lax.broadcasted_iota(jnp.int32, (rows, depth), 1)
    top = jnp.zeros((rows, depth), jnp.bool_)
    for f, width in enumerate(WIDTHS):
        at = LANE_BASES[f]
        top = top | ((lane >= at) & (lane < at + width))
    me = lax.axis_index("gz")
    strip[...] = jnp.where(
        top,
        jnp.where(me > 0, from_low[...], 0.0),
        jnp.where(me < count_z - 1, from_high[...], 0.0),
    )
    for f, width in enumerate(ALL_WIDTHS):
        source = fields.at[f] if f < FIELDS else strip
        for d in range(width):
            low[BASES[f] + d] = source[d * ny : (d + 1) * ny, :]
            high[BASES[f] + d] = source[(nx - 1 - d) * ny : (nx - d) * ny, :]


def faces_y_kernel(nx, ny, fields, strip, halo_low, halo_high, low, high):
    for f, width in enumerate(ALL_WIDTHS):
        source = fields.at[f] if f < FIELDS else strip
        for d in range(width):
            for face, y in ((low, d), (high, ny - 1 - d)):
                at = BASES[f] + d
                face[at, 0:nx, :] = source[pl.ds(y, nx, stride=ny), :]
                if width < STEPS:
                    face[at, nx : nx + 2 * STEPS, :] = jnp.zeros(
                        (2 * STEPS, face.shape[2]), jnp.float32
                    )
                for e in range(width):
                    face[at, nx + e : nx + e + 1, :] = halo_high[BASES[f] + e, y : y + 1, :]
                    last = nx + 2 * STEPS - 1 - e
                    face[at, last : last + 1, :] = halo_low[BASES[f] + e, y : y + 1, :]


def steps_kernel(
    fields, strip, x_low, x_high, y_low, y_high, arrived, states,
    electric, magnetic, result,
    wide, wide_strip, field, row_hot, depth_hot,
):
    _, nx, ny, depth = electric.shape
    rows = nx * ny
    ex, ey, ez = nx + 2 * STEPS, ny + 2 * STEPS, 2 * depth

    for f, width in enumerate(ALL_WIDTHS):
        source = fields.at[f] if f < FIELDS else strip
        target = wide.at[f] if f < FIELDS else wide_strip
        target[STEPS : STEPS + nx, 0:ny, 0:depth] = source[...].reshape(nx, ny, depth)
        target[:, ny : ny + 2 * STEPS, 0:depth] = jnp.zeros((ex, 2 * STEPS, depth), jnp.float32)
        for d in range(width):
            at = BASES[f] + d
            target[STEPS - 1 - d, 0:ny, 0:depth] = x_low[at]
            target[STEPS + nx + d, 0:ny, 0:depth] = x_high[at]
            for halo, y in ((y_low, ey - 1 - d), (y_high, ny + d)):
                for x in range(ex):
                    row = (x - STEPS) % ex
                    target[x, y : y + 1, 0:depth] = halo[at, row : row + 1, :]

    def spread(x, carry):
        value = wide_strip[x]
        for f, width in enumerate(WIDTHS):
            wide[f, x, :, depth:ez] = pltpu.roll(
                value, (-(LANE_BASES[f] + width)) % depth, 1
            )
        return carry

    lax.fori_loop(0, ex, spread, 0)
    row_at = lax.broadcasted_iota(jnp.int32, (ey, ez), 0)
    lane_at = lax.broadcasted_iota(jnp.int32, (ey, ez), 1)
    outside = ((row_at >= ey - STEPS) & (lax.axis_index("gy") == 0)) | (
        (lane_at >= ez - STEPS) & (lax.axis_index("gz") == 0)
    )
    inside = jnp.where(outside, 0.0, 1.0)
    first_x = lax.axis_index("gx") == 0

    index = arrived[:, 12, :].astype(jnp.int32)
    write_one_hots(index, row_hot, depth_hot, rows, depth)
    constants = emitter_constants(arrived)
    current = [states[c] for c in range(3)]
    previous = [states[3 + c] for c in range(3)]
    upper = states[6]
    pumped = states[7]

    def up_y(v):
        return pltpu.roll(v, ey - 1, 0)

    def up_z(v):
        return pltpu.roll(v, ez - 1, 1)

    def down_y(v):
        return pltpu.roll(v, 1, 0)

    def down_z(v):
        return pltpu.roll(v, 1, 1)

    def advance_magnetic(step, x):
        e0, e1, e2 = wide[0, x], wide[1, x], wide[2, x]
        f1, f2 = wide[1, x + 1], wide[2, x + 1]
        curl = (
            (up_y(e2) - e2) - (up_z(e1) - e1),
            (up_z(e0) - e0) - (f2 - e2),
            (f1 - e1) - (up_y(e0) - e0),
        )
        mask = inside * jnp.where(first_x & (x < STEPS), 0.0, 1.0)
        for c in range(3):
            change = -TIME_STEP * curl[c]
            if step > 1:
                change = field[c, x] + change
            field[c, x] = change * mask

    def advance_electric(step, x):
        m0, m1, m2 = field[0, x], field[1, x], field[2, x]
        l1, l2 = field[1, x - 1], field[2, x - 1]
        curl = (
            (m2 - down_y(m2)) - (m1 - down_z(m1)),
            (m0 - down_z(m0)) - (m2 - l2),
            (m1 - l1) - (m0 - down_y(m0)),
        )
        old = [wide[c, x] for c in range(3)]
        if step == 2:
            gain = wide[10, x]
            source = [wide[7 + c, x] + gain * old[c] for c in range(3)]
            ratio = wide[14, x]
            for c in range(3):
                wide[11 + c, x] = wide[11 + c, x] + ratio * old[c]
            square = old[0] * old[0] + old[1] * old[1] + old[2] * old[2]
            wide[15, x] = (
                wide[15, x]
                + (wide[16, x] * old[0] + wide[17, x] * old[1] + wide[18, x] * old[2])
                + wide[19, x] * square
            )
        elif step == 3:
            gain = wide[15, x]
            source = [wide[11 + c, x] + gain * old[c] for c in range(3)]
        else:
            source = [wide[4 + c, x] for c in range(3)]
        inverse = wide[3, x]
        for c in range(3):
            wide[c, x] = old[c] + inverse * (TIME_STEP * curl[c] - source[c])

    for step in range(1, STEPS + 1):
        if step > 1:
            cells = [
                wide[c, STEPS : STEPS + nx, 0:ny, 0:depth].reshape(rows, depth) for c in range(3)
            ]
            sample = gather_cells(cells, index, row_hot, depth)
            advanced, previous, upper, pumped = bloch_step(
                sample, current, previous, upper, pumped, constants
            )
            if step == STEPS:
                change = [a - c for a, c in zip(advanced, current)]
                for c, block in enumerate(scatter_cells(change, row_hot, depth_hot, rows)):
                    wide[4 + c, STEPS : STEPS + nx, 0:ny, 0:depth] = block.reshape(nx, ny, depth)
            current = advanced
        advance_magnetic(step, step - 1)

        def body(x, carry, step=step):
            advance_magnetic(step, x)
            advance_electric(step, x)
            return carry

        lax.fori_loop(step, ex - step, body, 0)
    for c in range(3):
        electric[c] = wide[c, STEPS : STEPS + nx, 0:ny, 0:depth]
        magnetic[c] = field[c, STEPS : STEPS + nx, 0:ny, 0:depth]
        result[:, c, :] = current[c]
        result[:, 3 + c, :] = previous[c]
    result[:, 6, :] = upper
    result[:, 7, :] = pumped


def call(kernel, out_shapes, scratch=()):
    return pl.pallas_call(
        kernel,
        out_shape=[jax.ShapeDtypeStruct(s, jnp.float32) for s in out_shapes],
        scratch_shapes=list(scratch),
        compiler_params=pltpu.CompilerParams(vmem_limit_bytes=VMEM_LIMIT),
    )


def shifted(value, axis, step):
    count = lax.axis_size(axis)
    pairs = [(i, i + step) for i in range(count) if 0 <= i + step < count]
    return lax.ppermute(value, axis, pairs)


def shards(
    electric, permittivity_class, cell_index, polarization, populations,
    resonance, dephasing, coupling, pump_rate,
):
    _, nx, ny, depth = electric.shape
    rows = nx * ny
    _, buckets, slots = cell_index.shape
    ex, ey, ez = nx + 2 * STEPS, ny + 2 * STEPS, 2 * depth
    hots = [
        pltpu.VMEM((2 * rows, buckets * slots), jnp.bfloat16),
        pltpu.VMEM((depth, buckets * slots), jnp.bfloat16),
    ]
    (packed,) = call(pack_kernel, [(buckets, 13, slots)])(
        cell_index, polarization, populations, resonance, dephasing, coupling, pump_rate
    )
    arrived = lax.all_to_all(packed, ("gy", "gz"), split_axis=0, concat_axis=0, tiled=True)
    fields, strip, states = call(
        first_kernel,
        [(FIELDS, rows, depth), (rows, depth), (8, buckets, slots)],
        hots,
    )(arrived, electric, permittivity_class)
    count_z = lax.axis_size("gz")
    if count_z == 2:
        from_low = from_high = lax.ppermute(strip, "gz", [(0, 1), (1, 0)])
    else:
        from_low = shifted(strip, "gz", 1)
        from_high = shifted(strip, "gz", -1)
    strip, face_low, face_high = call(
        functools.partial(faces_x_kernel, nx, ny, count_z),
        [(rows, depth), (LAYERS, ny, depth), (LAYERS, ny, depth)],
    )(fields, from_low, from_high)
    x_low = shifted(face_high, "gx", 1)
    x_high = shifted(face_low, "gx", -1)
    face_low, face_high = call(
        functools.partial(faces_y_kernel, nx, ny), [(LAYERS, ex, depth)] * 2
    )(fields, strip, x_low, x_high)
    y_low = shifted(face_high, "gy", 1)
    y_high = shifted(face_low, "gy", -1)
    electric, magnetic, result = call(
        steps_kernel,
        [electric.shape, electric.shape, (buckets, 8, slots)],
        [
            pltpu.VMEM((FIELDS, ex, ey, ez), jnp.float32),
            pltpu.VMEM((ex, ey, depth), jnp.float32),
            pltpu.VMEM((3, ex, ey, ez), jnp.float32),
        ]
        + hots,
    )(fields, strip, x_low, x_high, y_low, y_high, arrived, states)
    home = lax.all_to_all(result, ("gy", "gz"), split_axis=0, concat_axis=0, tiled=True)
    home = jnp.moveaxis(home, 1, 0)
    polar_out = home[0:6].reshape(polarization.shape)
    popul_out = home[6:8].reshape(populations.shape)
    return (electric, magnetic, polar_out, popul_out)


def solution(mesh):
    owners = P("gx", ("gy", "gz"), None)
    return jax.shard_map(
        shards,
        mesh=mesh,
        in_specs=(
            P(None, "gx", "gy", "gz"),
            P("gx", "gy", "gz"),
            owners,
            P(None, None, "gx", ("gy", "gz"), None),
            P(None, "gx", ("gy", "gz"), None),
            owners,
            owners,
            owners,
            owners,
        ),
        out_specs=(
            P(None, "gx", "gy", "gz"),
            P(None, "gx", "gy", "gz"),
            P(None, None, "gx", ("gy", "gz"), None),
            P(None, "gx", ("gy", "gz"), None),
        ),
        check_vma=False,
    )
```

```python
import functools

import jax
import jax.numpy as jnp
from jax import lax
from jax.experimental import pallas as pl
from jax.experimental.pallas import tpu as pltpu
from jax.sharding import PartitionSpec as P

STEPS = 4
TIME_STEP = 0.5
PUMP_DECAY = 0.2
UPPER_DECAY = 0.02
WORK_SHARE = 0.05
CLASS_PERMITTIVITY = (1.0, 2.1, 6.0, 12.25)

WIDTHS = (STEPS,) * 3 + (STEPS - 1,) * 4 + (STEPS - 2,) * 4 + (STEPS - 3,) * 9
FIELDS = len(WIDTHS)
ALL_WIDTHS = WIDTHS + (STEPS,)
VECTORS = (0, 4, 7, 11)
LANE_BASES = tuple(2 * sum(WIDTHS[:i]) for i in range(FIELDS))
LANES = 128
VMEM_LIMIT = 56 * 1024 * 1024


def layer_list(skip_axis):
    layers = []
    for f, width in enumerate(ALL_WIDTHS):
        unused = skip_axis is not None and f - skip_axis in VECTORS
        layers += [(f, d) for d in range(width - 1 if unused else width)]
    return layers


LAYERS_LOW = (layer_list(0), layer_list(1))
LAYERS_HIGH = layer_list(None)


def corner_rows(layers, halo_sign):
    out = []
    for f, d in layers:
        width = ALL_WIDTHS[f]
        for side in (-1, 1):
            reach = width - d if side != halo_sign else width - 1 - d
            for e in range(reach):
                known = LAYERS_HIGH if side < 0 else LAYERS_LOW[0]
                if (f, e) in known:
                    out.append((f, d, side, e))
    return out


def face_rows(layers, halo_sign, nx):
    count = len(layers) * nx + len(corner_rows(layers, halo_sign))
    return -(-count // 8) * 8


def inverse_permittivity(classes):
    inverse = jnp.zeros(classes.shape, jnp.float32)
    for number, epsilon in enumerate(CLASS_PERMITTIVITY):
        inverse = jnp.where(classes == number, 1.0 / epsilon, inverse)
    return inverse


def halves(value):
    high = value.astype(jnp.bfloat16)
    low = (value - high.astype(jnp.float32)).astype(jnp.bfloat16)
    return high, low


def write_one_hots(index, row_hot, depth_hot, rows, depth):
    shift = depth.bit_length() - 1
    buckets, slots = index.shape
    for b in range(buckets):
        row = lax.shift_right_logical(index[b : b + 1], shift)
        deep = lax.bitwise_and(index[b : b + 1], depth - 1)
        rows_at = lax.broadcasted_iota(jnp.int32, (rows, slots), 0)
        deep_at = lax.broadcasted_iota(jnp.int32, (depth, slots), 0)
        hot = jnp.where(rows_at == row, 1.0, 0.0).astype(jnp.bfloat16)
        span = slice(b * slots, (b + 1) * slots)
        row_hot[0:rows, span] = hot
        row_hot[rows : 2 * rows, span] = hot
        depth_hot[:, span] = jnp.where(deep_at == deep, 1.0, 0.0).astype(jnp.bfloat16)


def gather_cells(cells, index, row_hot, depth):
    buckets, slots = index.shape
    parts = []
    for block in cells:
        high, low = halves(block.T)
        parts.append(jnp.concatenate([high, low], axis=1))
    left = jnp.concatenate(parts, axis=0)
    samples = [[], [], []]
    group = 2 if buckets % 2 == 0 else 1
    for start in range(0, buckets, group):
        span = slice(start * slots, (start + group) * slots)
        picked = jnp.dot(left, row_hot[:, span], preferred_element_type=jnp.float32)
        for b in range(start, start + group):
            deep = lax.bitwise_and(index[b : b + 1], depth - 1)
            hit = lax.broadcasted_iota(jnp.int32, (depth, slots), 0) == deep
            for c in range(3):
                part = picked[c * depth : (c + 1) * depth, (b - start) * slots : (b - start + 1) * slots]
                samples[c].append(jnp.sum(jnp.where(hit, part, 0.0), axis=0, keepdims=True))
    return [jnp.concatenate(rows, axis=0) for rows in samples]


def flat_row(value):
    buckets = value.shape[0]
    return jnp.concatenate([value[b : b + 1] for b in range(buckets)], axis=1)


def scatter_cells(values, row_hot, depth_hot, rows):
    hot = row_hot[0:rows, :]
    hot = jnp.concatenate([hot, hot], axis=1)
    deep = depth_hot[...]
    out = []
    for value in values:
        high, low = halves(flat_row(value))
        spread = jnp.concatenate([deep * high, deep * low], axis=1)
        out.append(
            lax.dot_general(
                hot, spread, (((1,), (1,)), ((), ())), preferred_element_type=jnp.float32
            )
        )
    return out


def emitter_constants(arrived):
    freq, dephase, strength, pumping = [arrived[:, f, :] for f in range(8, 12)]
    damping = 0.5 * TIME_STEP * dephase
    stiffness = freq * TIME_STEP * (freq * TIME_STEP)
    scale = 1.0 + damping
    keep = (2.0 - stiffness) / scale
    back = (1.0 - damping) / scale
    drive = strength * (TIME_STEP * TIME_STEP) / scale
    share = WORK_SHARE / freq
    return keep, back, drive, share, pumping


def bloch_step(sample, current, previous, upper, pumped, constants):
    keep, back, drive, share, pumping = constants
    lower = 1.0 - upper - pumped
    push = drive * (lower - upper)
    advanced = [keep * c - back * p + push * s for c, p, s in zip(current, previous, sample)]
    work = sum(s * (a - p) for s, a, p in zip(sample, advanced, previous)) / (2.0 * TIME_STEP)
    pumped_next = pumped + TIME_STEP * (pumping * lower - PUMP_DECAY * pumped)
    upper_next = upper + TIME_STEP * (
        PUMP_DECAY * pumped - UPPER_DECAY * upper + share * work
    )
    return advanced, current, upper_next, pumped_next


def pack_kernel(index, polar, popul, freq, dephase, strength, pumping, out):
    for i in range(2):
        for c in range(3):
            out[:, 3 * i + c, :] = polar[i, c, 0]
    for i in range(2):
        out[:, 6 + i, :] = popul[i, 0]
    for f, source in enumerate((freq, dephase, strength, pumping)):
        out[:, 8 + f, :] = source[0]
    out[:, 12, :] = index[0].astype(jnp.float32)


def first_kernel(arrived, electric, classes, fields, strip, states, row_hot, depth_hot):
    _, nx, ny, depth = electric.shape
    rows = nx * ny
    index = arrived[:, 12, :].astype(jnp.int32)
    write_one_hots(index, row_hot, depth_hot, rows, depth)
    for c in range(3):
        fields[c] = electric[c].reshape(rows, depth)
    fields[3] = inverse_permittivity(classes[...].reshape(rows, depth))
    sample = gather_cells([fields[c] for c in range(3)], index, row_hot, depth)
    constants = emitter_constants(arrived)
    keep, back, drive, share, pumping = constants
    start = [arrived[:, c, :] for c in range(3)]
    before = [arrived[:, 3 + c, :] for c in range(3)]
    now, _, upper, pumped = bloch_step(
        sample, start, before, arrived[:, 6, :], arrived[:, 7, :], constants
    )
    for c in range(3):
        states[c] = now[c]
        states[3 + c] = start[c]
    states[6] = upper
    states[7] = pumped
    lower = 1.0 - upper - pumped
    push = drive * (lower - upper)
    pumped_after = pumped + TIME_STEP * (pumping * lower - PUMP_DECAY * pumped)
    upper_free = upper + TIME_STEP * (PUMP_DECAY * pumped - UPPER_DECAY * upper)
    free = [keep * n - back * s for n, s in zip(now, start)]
    values = [n - s for n, s in zip(now, start)]
    values += [f - n for f, n in zip(free, now)]
    values.append(push)
    values += [(keep - 1.0) * f - back * n for f, n in zip(free, now)]
    values.append((keep - 1.0) * push)
    values.append(drive * (1.0 - pumped_after - 2.0 * upper_free))
    values += [-drive * share * (f - s) for f, s in zip(free, start)]
    values.append(-drive * share * push)
    for number, block in enumerate(scatter_cells(values, row_hot, depth_hot, rows)):
        fields[4 + number] = block
    lane = lax.broadcasted_iota(jnp.int32, (rows, depth), 1)
    packed = jnp.zeros((rows, depth), jnp.float32)
    for f, width in enumerate(WIDTHS):
        at = LANE_BASES[f]
        turned = pltpu.roll(fields[f], (at + width) % depth, 1)
        packed = jnp.where((lane >= at) & (lane < at + 2 * width), turned, packed)
    strip[...] = packed


def faces_x_kernel(nx, ny, count_z, fields, *refs):
    from_low, from_high, strip, low, high = refs
    rows, depth = strip.shape
    lane = lax.broadcasted_iota(jnp.int32, (rows, depth), 1)
    top = jnp.zeros((rows, depth), jnp.bool_)
    for f, width in enumerate(WIDTHS):
        at = LANE_BASES[f]
        top = top | ((lane >= at) & (lane < at + width))
    me = lax.axis_index("gz")
    strip[...] = jnp.where(
        top,
        jnp.where(me > 0, from_low[...], 0.0),
        jnp.where(me < count_z - 1, from_high[...], 0.0),
    )
    for at, (f, d) in enumerate(LAYERS_LOW[0]):
        source = fields.at[f] if f < FIELDS else strip
        low[at] = source[d * ny : (d + 1) * ny, :]
    for at, (f, d) in enumerate(LAYERS_HIGH):
        source = fields.at[f] if f < FIELDS else strip
        high[at] = source[(nx - 1 - d) * ny : (nx - d) * ny, :]


def faces_y_kernel(nx, ny, fields, strip, halo_low, halo_high, low, high):
    for face, layers, sign in ((low, LAYERS_LOW[1], -1), (high, LAYERS_HIGH, 1)):
        for at, (f, d) in enumerate(layers):
            source = fields.at[f] if f < FIELDS else strip
            y = d if sign < 0 else ny - 1 - d
            face[at * nx : (at + 1) * nx, :] = source[pl.ds(y, nx, stride=ny), :]
        for row, (f, d, side, e) in enumerate(corner_rows(layers, -sign)):
            y = d if sign < 0 else ny - 1 - d
            if side < 0:
                value = halo_low[LAYERS_HIGH.index((f, e)), y : y + 1, :]
            else:
                value = halo_high[LAYERS_LOW[0].index((f, e)), y : y + 1, :]
            at = len(layers) * nx + row
            face[at : at + 1, :] = value


def steps_kernel(
    fields, strip, x_low, x_high, y_low, y_high, arrived, states,
    electric, magnetic, result,
    wide, wide_strip, field, row_hot, depth_hot,
):
    _, nx, ny, depth = electric.shape
    rows = nx * ny
    ex, ey, ez = nx + 2 * STEPS, ny + 2 * STEPS, 2 * depth

    def target(f):
        return wide.at[f] if f < FIELDS else wide_strip

    for f in range(FIELDS + 1):
        source = fields.at[f] if f < FIELDS else strip
        target(f)[STEPS : STEPS + nx, 0:ny, 0:depth] = source[...].reshape(nx, ny, depth)
        target(f)[:, ny : ny + 2 * STEPS, 0:depth] = jnp.zeros((ex, 2 * STEPS, depth), jnp.float32)
    for at, (f, d) in enumerate(LAYERS_HIGH):
        target(f)[STEPS - 1 - d, 0:ny, 0:depth] = x_low[at]
    for at, (f, d) in enumerate(LAYERS_LOW[0]):
        target(f)[STEPS + nx + d, 0:ny, 0:depth] = x_high[at]
    for halo, layers, sign in ((y_low, LAYERS_HIGH, -1), (y_high, LAYERS_LOW[1], 1)):
        for at, (f, d) in enumerate(layers):
            y = ey - 1 - d if sign < 0 else ny + d
            for x in range(nx):
                target(f)[STEPS + x, y : y + 1, 0:depth] = halo[at * nx + x : at * nx + x + 1, :]
        for row, (f, d, side, e) in enumerate(corner_rows(layers, sign)):
            y = ey - 1 - d if sign < 0 else ny + d
            x = STEPS - 1 - e if side < 0 else STEPS + nx + e
            at = len(layers) * nx + row
            target(f)[x, y : y + 1, 0:depth] = halo[at : at + 1, :]

    for x in range(ex):
        value = wide_strip[x]
        for f, width in enumerate(WIDTHS):
            wide[f, x, :, depth:ez] = pltpu.roll(
                value, (-(LANE_BASES[f] + width)) % depth, 1
            )
    row_at = lax.broadcasted_iota(jnp.int32, (ey, ez), 0)
    lane_at = lax.broadcasted_iota(jnp.int32, (ey, ez), 1)
    outside = ((row_at >= ey - STEPS) & (lax.axis_index("gy") == 0)) | (
        (lane_at >= ez - STEPS) & (lax.axis_index("gz") == 0)
    )
    inside = jnp.where(outside, 0.0, 1.0)
    first_x = lax.axis_index("gx") == 0

    index = arrived[:, 12, :].astype(jnp.int32)
    write_one_hots(index, row_hot, depth_hot, rows, depth)
    constants = emitter_constants(arrived)
    current = [states[c] for c in range(3)]
    previous = [states[3 + c] for c in range(3)]
    upper = states[6]
    pumped = states[7]

    def up_y(v):
        return pltpu.roll(v, ey - 1, 0)

    def up_z(v):
        return pltpu.roll(v, ez - 1, 1)

    def down_y(v):
        return pltpu.roll(v, 1, 0)

    def down_z(v):
        return pltpu.roll(v, 1, 1)

    def advance_magnetic(step, x):
        e0, e1, e2 = wide[0, x], wide[1, x], wide[2, x]
        f1, f2 = wide[1, x + 1], wide[2, x + 1]
        curl = (
            (up_y(e2) - e2) - (up_z(e1) - e1),
            (up_z(e0) - e0) - (f2 - e2),
            (f1 - e1) - (up_y(e0) - e0),
        )
        mask = inside * jnp.where(first_x, 0.0, 1.0) if x < STEPS else inside
        for c in range(3):
            change = -TIME_STEP * curl[c]
            if step > 1:
                change = field[c, x] + change
            field[c, x] = change * mask

    def advance_electric(step, x):
        m0, m1, m2 = field[0, x], field[1, x], field[2, x]
        l1, l2 = field[1, x - 1], field[2, x - 1]
        curl = (
            (m2 - down_y(m2)) - (m1 - down_z(m1)),
            (m0 - down_z(m0)) - (m2 - l2),
            (m1 - l1) - (m0 - down_y(m0)),
        )
        old = [wide[c, x] for c in range(3)]
        if step == 2:
            gain = wide[10, x]
            source = [wide[7 + c, x] + gain * old[c] for c in range(3)]
            ratio = wide[14, x]
            for c in range(3):
                wide[11 + c, x] = wide[11 + c, x] + ratio * old[c]
            square = old[0] * old[0] + old[1] * old[1] + old[2] * old[2]
            wide[15, x] = (
                wide[15, x]
                + (wide[16, x] * old[0] + wide[17, x] * old[1] + wide[18, x] * old[2])
                + wide[19, x] * square
            )
        elif step == 3:
            gain = wide[15, x]
            source = [wide[11 + c, x] + gain * old[c] for c in range(3)]
        else:
            source = [wide[4 + c, x] for c in range(3)]
        inverse = wide[3, x]
        for c in range(3):
            wide[c, x] = old[c] + inverse * (TIME_STEP * curl[c] - source[c])

    for step in range(1, STEPS + 1):
        if step > 1:
            cells = [
                wide[c, STEPS : STEPS + nx, 0:ny, 0:depth].reshape(rows, depth) for c in range(3)
            ]
            sample = gather_cells(cells, index, row_hot, depth)
            advanced, previous, upper, pumped = bloch_step(
                sample, current, previous, upper, pumped, constants
            )
            if step == STEPS:
                change = [a - c for a, c in zip(advanced, current)]
                for c, block in enumerate(scatter_cells(change, row_hot, depth_hot, rows)):
                    wide[4 + c, STEPS : STEPS + nx, 0:ny, 0:depth] = block.reshape(nx, ny, depth)
            current = advanced
        advance_magnetic(step, step - 1)

        for x in range(step, ex - step):
            advance_magnetic(step, x)
            advance_electric(step, x)
    for c in range(3):
        electric[c] = wide[c, STEPS : STEPS + nx, 0:ny, 0:depth]
        magnetic[c] = field[c, STEPS : STEPS + nx, 0:ny, 0:depth]
        result[:, c, :] = current[c]
        result[:, 3 + c, :] = previous[c]
    result[:, 6, :] = upper
    result[:, 7, :] = pumped


def call(kernel, out_shapes, scratch=(), final=0):
    shapes = [
        jax.ShapeDtypeStruct(s, jnp.float32) if i < final else pltpu.VMEM(s, jnp.float32)
        for i, s in enumerate(out_shapes)
    ]
    return pl.pallas_call(
        kernel,
        out_shape=shapes,
        scratch_shapes=list(scratch),
        compiler_params=pltpu.CompilerParams(vmem_limit_bytes=VMEM_LIMIT),
    )


def near(*values):
    return [pltpu.with_memory_space_constraint(v, pltpu.VMEM) for v in values]


def shifted(value, axis, step):
    count = lax.axis_size(axis)
    pairs = [(i, i + step) for i in range(count) if 0 <= i + step < count]
    return lax.ppermute(value, axis, pairs)


def shards(
    electric, permittivity_class, cell_index, polarization, populations,
    resonance, dephasing, coupling, pump_rate,
):
    _, nx, ny, depth = electric.shape
    rows = nx * ny
    _, buckets, slots = cell_index.shape
    ex, ey, ez = nx + 2 * STEPS, ny + 2 * STEPS, 2 * depth
    hots = [
        pltpu.VMEM((2 * rows, buckets * slots), jnp.bfloat16),
        pltpu.VMEM((depth, buckets * slots), jnp.bfloat16),
    ]
    (packed,) = call(pack_kernel, [(buckets, 13, slots)])(
        cell_index, polarization, populations, resonance, dephasing, coupling, pump_rate
    )
    arrived = lax.all_to_all(packed, ("gy", "gz"), split_axis=0, concat_axis=0, tiled=True)
    (arrived,) = near(arrived)
    fields, strip, states = call(
        first_kernel,
        [(FIELDS, rows, depth), (rows, depth), (8, buckets, slots)],
        hots,
    )(arrived, electric, permittivity_class)
    fields, strip, states = near(fields, strip, states)
    count_z = lax.axis_size("gz")
    if count_z == 2:
        from_low = from_high = lax.ppermute(strip, "gz", [(0, 1), (1, 0)])
    else:
        from_low = shifted(strip, "gz", 1)
        from_high = shifted(strip, "gz", -1)
    strip, face_low, face_high = call(
        functools.partial(faces_x_kernel, nx, ny, count_z),
        [(rows, depth), (len(LAYERS_LOW[0]), ny, depth), (len(LAYERS_HIGH), ny, depth)],
    )(fields, *near(from_low, from_high))
    (strip,) = near(strip)
    x_low = shifted(face_high, "gx", 1)
    x_high = shifted(face_low, "gx", -1)
    x_low, x_high = near(x_low, x_high)
    face_low, face_high = call(
        functools.partial(faces_y_kernel, nx, ny),
        [
            (face_rows(LAYERS_LOW[1], 1, nx), depth),
            (face_rows(LAYERS_HIGH, -1, nx), depth),
        ],
    )(fields, strip, x_low, x_high)
    y_low = shifted(face_high, "gy", 1)
    y_high = shifted(face_low, "gy", -1)
    y_low, y_high = near(y_low, y_high)
    electric, magnetic, result = call(
        steps_kernel,
        [electric.shape, electric.shape, (buckets, 8, slots)],
        [
            pltpu.VMEM((FIELDS, ex, ey, ez), jnp.float32),
            pltpu.VMEM((ex, ey, depth), jnp.float32),
            pltpu.VMEM((3, ex, ey, ez), jnp.float32),
        ]
        + hots,
        final=2,
    )(fields, strip, x_low, x_high, y_low, y_high, arrived, states)
    home = lax.all_to_all(result, ("gy", "gz"), split_axis=0, concat_axis=0, tiled=True)
    home = jnp.moveaxis(home, 1, 0)
    polar_out = home[0:6].reshape(polarization.shape)
    popul_out = home[6:8].reshape(populations.shape)
    return (electric, magnetic, polar_out, popul_out)


def solution(mesh):
    owners = P("gx", ("gy", "gz"), None)
    return jax.shard_map(
        shards,
        mesh=mesh,
        in_specs=(
            P(None, "gx", "gy", "gz"),
            P("gx", "gy", "gz"),
            owners,
            P(None, None, "gx", ("gy", "gz"), None),
            P(None, "gx", ("gy", "gz"), None),
            owners,
            owners,
            owners,
            owners,
        ),
        out_specs=(
            P(None, "gx", "gy", "gz"),
            P(None, "gx", "gy", "gz"),
            P(None, None, "gx", ("gy", "gz"), None),
            P(None, "gx", ("gy", "gz"), None),
        ),
        check_vma=False,
    )
```

```python
import functools

import jax
import jax.numpy as jnp
from jax import lax
from jax.experimental import pallas as pl
from jax.experimental.pallas import tpu as pltpu
from jax.sharding import PartitionSpec as P

STEPS = 4
TIME_STEP = 0.5
PUMP_DECAY = 0.2
UPPER_DECAY = 0.02
WORK_SHARE = 0.05
CLASS_PERMITTIVITY = (1.0, 2.1, 6.0, 12.25)

WIDTHS = (STEPS,) * 3 + (STEPS - 1,) * 4 + (STEPS - 2,) * 4 + (STEPS - 3,) * 9
FIELDS = len(WIDTHS)
GRID = 4
ALL_WIDTHS = WIDTHS + (STEPS,)
VECTORS = (0, 4, 7, 11)
LANE_BASES = tuple(2 * sum(WIDTHS[:i]) for i in range(FIELDS))
LANES = 128
VMEM_LIMIT = 24 * 1024 * 1024
HIGH_LIMIT = 56 * 1024 * 1024


def layer_list(skip_axis):
    layers = []
    for f, width in enumerate(ALL_WIDTHS):
        unused = skip_axis is not None and f - skip_axis in VECTORS
        layers += [(f, d) for d in range(width - 1 if unused else width)]
    return layers


LAYERS_LOW = (layer_list(0), layer_list(1))
LAYERS_HIGH = layer_list(None)


def corner_rows(layers, halo_sign):
    out = []
    for f, d in layers:
        width = ALL_WIDTHS[f]
        for side in (-1, 1):
            reach = width - d if side != halo_sign else width - 1 - d
            for e in range(reach):
                known = LAYERS_HIGH if side < 0 else LAYERS_LOW[0]
                if (f, e) in known:
                    out.append((f, d, side, e))
    return out


def corner_shape(layers, halo_sign, depth):
    return (-(-len(corner_rows(layers, halo_sign)) // 8) * 8, depth)


def inverse_permittivity(classes):
    inverse = jnp.zeros(classes.shape, jnp.float32)
    for number, epsilon in enumerate(CLASS_PERMITTIVITY):
        inverse = jnp.where(classes == number, 1.0 / epsilon, inverse)
    return inverse


def halves(value):
    high = value.astype(jnp.bfloat16)
    low = (value - high.astype(jnp.float32)).astype(jnp.bfloat16)
    return high, low


def write_one_hots(index, row_hot, depth_hot, rows, depth):
    shift = depth.bit_length() - 1
    buckets, slots = index.shape
    for b in range(buckets):
        row = lax.shift_right_logical(index[b : b + 1], shift)
        deep = lax.bitwise_and(index[b : b + 1], depth - 1)
        rows_at = lax.broadcasted_iota(jnp.int32, (rows, slots), 0)
        deep_at = lax.broadcasted_iota(jnp.int32, (depth, slots), 0)
        hot = jnp.where(rows_at == row, 1.0, 0.0).astype(jnp.bfloat16)
        span = slice(b * slots, (b + 1) * slots)
        row_hot[0:rows, span] = hot
        row_hot[rows : 2 * rows, span] = hot
        depth_hot[:, span] = jnp.where(deep_at == deep, 1.0, 0.0).astype(jnp.bfloat16)


def cell_halves(cells):
    parts = []
    for block in cells:
        parts.append(jnp.concatenate(halves(block.T), axis=1))
    return jnp.concatenate(parts, axis=0)


def gather_cells(left, index, row_hot, depth):
    buckets, slots = index.shape
    samples = [[], [], []]
    group = 2 if buckets % 2 == 0 else 1
    for start in range(0, buckets, group):
        span = slice(start * slots, (start + group) * slots)
        picked = jnp.dot(left, row_hot[:, span], preferred_element_type=jnp.float32)
        for b in range(start, start + group):
            deep = lax.bitwise_and(index[b : b + 1], depth - 1)
            hit = lax.broadcasted_iota(jnp.int32, (depth, slots), 0) == deep
            for c in range(3):
                part = picked[c * depth : (c + 1) * depth, (b - start) * slots : (b - start + 1) * slots]
                samples[c].append(jnp.sum(jnp.where(hit, part, 0.0), axis=0, keepdims=True))
    return [jnp.concatenate(rows, axis=0) for rows in samples]


def flat_row(value):
    buckets = value.shape[0]
    return jnp.concatenate([value[b : b + 1] for b in range(buckets)], axis=1)


def scatter_cells(values, row_hot, depth_hot, rows):
    hot = row_hot[0:rows, :]
    hot = jnp.concatenate([hot, hot], axis=1)
    deep = depth_hot[...]
    out = []
    for value in values:
        high, low = halves(flat_row(value))
        spread = jnp.concatenate([deep * high, deep * low], axis=1)
        out.append(
            lax.dot_general(
                hot, spread, (((1,), (1,)), ((), ())), preferred_element_type=jnp.float32
            )
        )
    return out


def emitter_constants(arrived):
    freq, dephase, strength, pumping = [arrived[:, f, :] for f in range(8, 12)]
    damping = 0.5 * TIME_STEP * dephase
    stiffness = freq * TIME_STEP * (freq * TIME_STEP)
    scale = 1.0 + damping
    keep = (2.0 - stiffness) / scale
    back = (1.0 - damping) / scale
    drive = strength * (TIME_STEP * TIME_STEP) / scale
    share = WORK_SHARE / freq
    return keep, back, drive, share, pumping


def bloch_step(sample, current, previous, upper, pumped, constants):
    keep, back, drive, share, pumping = constants
    lower = 1.0 - upper - pumped
    push = drive * (lower - upper)
    advanced = [keep * c - back * p + push * s for c, p, s in zip(current, previous, sample)]
    work = sum(s * (a - p) for s, a, p in zip(sample, advanced, previous)) / (2.0 * TIME_STEP)
    pumped_next = pumped + TIME_STEP * (pumping * lower - PUMP_DECAY * pumped)
    upper_next = upper + TIME_STEP * (
        PUMP_DECAY * pumped - UPPER_DECAY * upper + share * work
    )
    return advanced, current, upper_next, pumped_next


def pack_kernel(index, polar, popul, freq, dephase, strength, pumping, out):
    for i in range(2):
        for c in range(3):
            out[:, 3 * i + c, :] = polar[i, c, 0]
    for i in range(2):
        out[:, 6 + i, :] = popul[i, 0]
    for f, source in enumerate((freq, dephase, strength, pumping)):
        out[:, 8 + f, :] = source[0]
    out[:, 12, :] = index[0].astype(jnp.float32)


def source_of(base, coefs, strip, f):
    if f < GRID:
        return base.at[f]
    return coefs.at[f - GRID] if f < FIELDS else strip


def base_kernel(electric, classes, base, left):
    _, nx, ny, depth = electric.shape
    rows = nx * ny
    for c in range(3):
        base[c] = electric[c].reshape(rows, depth)
    base[3] = inverse_permittivity(classes[...].reshape(rows, depth)) * -(TIME_STEP**2)
    left[...] = cell_halves([base[c] for c in range(3)])


def first_kernel(arrived, base, left, coefs, strip, states, row_hot, depth_hot):
    _, rows, depth = base.shape
    index = arrived[:, 12, :].astype(jnp.int32)
    write_one_hots(index, row_hot, depth_hot, rows, depth)
    sample = gather_cells(left[...], index, row_hot, depth)
    constants = emitter_constants(arrived)
    keep, back, drive, share, pumping = constants
    start = [arrived[:, c, :] for c in range(3)]
    before = [arrived[:, 3 + c, :] for c in range(3)]
    now, _, upper, pumped = bloch_step(
        sample, start, before, arrived[:, 6, :], arrived[:, 7, :], constants
    )
    for c in range(3):
        states[c] = now[c]
        states[3 + c] = start[c]
    states[6] = upper
    states[7] = pumped
    lower = 1.0 - upper - pumped
    push = drive * (lower - upper)
    pumped_after = pumped + TIME_STEP * (pumping * lower - PUMP_DECAY * pumped)
    upper_free = upper + TIME_STEP * (PUMP_DECAY * pumped - UPPER_DECAY * upper)
    free = [keep * n - back * s for n, s in zip(now, start)]
    values = [n - s for n, s in zip(now, start)]
    values += [f - n for f, n in zip(free, now)]
    values.append(push)
    values += [(keep - 1.0) * f - back * n for f, n in zip(free, now)]
    values.append((keep - 1.0) * push)
    values.append(drive * (1.0 - pumped_after - 2.0 * upper_free))
    values += [-drive * share * (f - s) for f, s in zip(free, start)]
    values.append(-drive * share * push)
    values = [value * (1.0 / TIME_STEP**2) for value in values]
    for number, block in enumerate(scatter_cells(values, row_hot, depth_hot, rows)):
        coefs[number] = block
    lane = lax.broadcasted_iota(jnp.int32, (rows, depth), 1)
    packed = jnp.zeros((rows, depth), jnp.float32)
    for f, width in enumerate(WIDTHS):
        at = LANE_BASES[f]
        turned = pltpu.roll(source_of(base, coefs, strip, f)[...], (at + width) % depth, 1)
        packed = jnp.where((lane >= at) & (lane < at + 2 * width), turned, packed)
    strip[...] = packed


def faces_kernel(nx, ny, count_z, base, coefs, from_low, from_high, strip, x_low, x_high, y_low, y_high):
    rows, depth = strip.shape
    lane = lax.broadcasted_iota(jnp.int32, (rows, depth), 1)
    top = jnp.zeros((rows, depth), jnp.bool_)
    for f, width in enumerate(WIDTHS):
        at = LANE_BASES[f]
        top = top | ((lane >= at) & (lane < at + width))
    me = lax.axis_index("gz")
    strip[...] = jnp.where(
        top,
        jnp.where(me > 0, from_low[...], 0.0),
        jnp.where(me < count_z - 1, from_high[...], 0.0),
    )

    def source(f):
        return source_of(base, coefs, strip, f)

    for at, (f, d) in enumerate(LAYERS_LOW[0]):
        x_low[at] = source(f)[d * ny : (d + 1) * ny, :]
    for at, (f, d) in enumerate(LAYERS_HIGH):
        x_high[at] = source(f)[(nx - 1 - d) * ny : (nx - d) * ny, :]
    for at, (f, d) in enumerate(LAYERS_LOW[1]):
        y_low[at] = source(f)[pl.ds(d, nx, stride=ny), :]
    for at, (f, d) in enumerate(LAYERS_HIGH):
        y_high[at] = source(f)[pl.ds(ny - 1 - d, nx, stride=ny), :]


def corners_kernel(halo_low, halo_high, low, high):
    ny = halo_low.shape[1]
    for face, layers, sign in ((low, LAYERS_LOW[1], -1), (high, LAYERS_HIGH, 1)):
        for row, (f, d, side, e) in enumerate(corner_rows(layers, -sign)):
            y = d if sign < 0 else ny - 1 - d
            if side < 0:
                value = halo_low[LAYERS_HIGH.index((f, e)), y : y + 1, :]
            else:
                value = halo_high[LAYERS_LOW[0].index((f, e)), y : y + 1, :]
            face[row : row + 1, :] = value


def place(cells, wide, wide_strip, f):
    if f < 3:
        return cells.at[f]
    return wide.at[f - 3] if f < FIELDS else wide_strip


def assemble_kernel(
    base, coefs, strip, x_low, x_high, y_low, y_high, cells, wide, wide_strip
):
    _, ny, depth = x_low.shape
    nx = y_low.shape[1]
    ex, ey, ez = nx + 2 * STEPS, ny + 2 * STEPS, 2 * depth
    for f in range(FIELDS + 1):
        source = source_of(base, coefs, strip, f)
        target = place(cells, wide, wide_strip, f)
        target[STEPS : STEPS + nx, 0:ny, 0:depth] = source[...].reshape(nx, ny, depth)
        target[:, ny:ey, 0:depth] = jnp.zeros((ex, 2 * STEPS, depth), jnp.float32)
    for at, (f, d) in enumerate(LAYERS_HIGH):
        place(cells, wide, wide_strip, f)[STEPS - 1 - d, 0:ny, 0:depth] = x_low[at]
    for at, (f, d) in enumerate(LAYERS_LOW[0]):
        place(cells, wide, wide_strip, f)[STEPS + nx + d, 0:ny, 0:depth] = x_high[at]
    for halo, layers, sign in ((y_low, LAYERS_HIGH, -1), (y_high, LAYERS_LOW[1], 1)):
        for at, (f, d) in enumerate(layers):
            y = ey - 1 - d if sign < 0 else ny + d
            for x in range(nx):
                place(cells, wide, wide_strip, f)[STEPS + x, y : y + 1, 0:depth] = halo[at, x : x + 1, :]
    for x in range(ex):
        value = wide_strip[x]
        for f, width in enumerate(WIDTHS):
            place(cells, wide, wide_strip, f)[x, :, depth:ez] = pltpu.roll(
                value, (-(LANE_BASES[f] + width)) % depth, 1
            )


def rolls(ey, ez):
    return (
        lambda v: pltpu.roll(v, ey - 1, 0),
        lambda v: pltpu.roll(v, ez - 1, 1),
        lambda v: pltpu.roll(v, 1, 0),
        lambda v: pltpu.roll(v, 1, 1),
    )


def inside_mask(ey, ez):
    row_at = lax.broadcasted_iota(jnp.int32, (ey, ez), 0)
    lane_at = lax.broadcasted_iota(jnp.int32, (ey, ez), 1)
    outside = ((row_at >= ey - STEPS) & (lax.axis_index("gy") == 0)) | (
        (lane_at >= ez - STEPS) & (lax.axis_index("gz") == 0)
    )
    return jnp.where(outside, 0.0, 1.0)


def advance_magnetic(cells, field, inside, step, x):
    _, _, ey, ez = cells.shape
    up_y, up_z, _, _ = rolls(ey, ez)
    e0, e1, e2 = cells[0, x], cells[1, x], cells[2, x]
    f1, f2 = cells[1, x + 1], cells[2, x + 1]
    curl = (
        (up_y(e2) - e2) - (up_z(e1) - e1),
        (up_z(e0) - e0) - (f2 - e2),
        (f1 - e1) - (up_y(e0) - e0),
    )
    mask = inside
    if x < STEPS:
        mask = inside * jnp.where(lax.axis_index("gx") == 0, 0.0, 1.0)
    for c in range(3):
        change = curl[c] * mask
        field[c, x] = field[c, x] + change if step > 1 else change


def backward_curl(field, x):
    _, _, ey, ez = field.shape
    _, _, down_y, down_z = rolls(ey, ez)
    m0, m1, m2 = field[0, x], field[1, x], field[2, x]
    l1, l2 = field[1, x - 1], field[2, x - 1]
    return (
        (m2 - down_y(m2)) - (m1 - down_z(m1)),
        (m0 - down_z(m0)) - (m2 - l2),
        (m1 - l1) - (m0 - down_y(m0)),
    )


def advance_electric(cells, wide, field, step, x):
    curl = backward_curl(field, x)
    old = [cells[c, x] for c in range(3)]
    if step == 2:
        gain = wide[7, x]
        source = [wide[4 + c, x] + gain * old[c] for c in range(3)]
        if STEPS - 2 < x < wide.shape[1] - STEPS + 1:
            ratio = wide[11, x]
            for c in range(3):
                wide[8 + c, x] = wide[8 + c, x] + ratio * old[c]
            square = old[0] * old[0] + old[1] * old[1] + old[2] * old[2]
            wide[12, x] = (
                wide[12, x]
                + (wide[13, x] * old[0] + wide[14, x] * old[1] + wide[15, x] * old[2])
                + wide[16, x] * square
            )
    elif step == 3:
        gain = wide[12, x]
        source = [wide[8 + c, x] + gain * old[c] for c in range(3)]
    else:
        source = [wide[1 + c, x] for c in range(3)]
    scale = wide[0, x]
    for c in range(3):
        cells[c, x] = old[c] + scale * (curl[c] + source[c])


def steps_kernel(
    c_low, c_high, _cells, _wide, wide_strip, row_hot, depth_hot, arrived, states,
    cells, wide, field, result, changes,
):
    _, ex, ey, ez = wide.shape
    nx, ny, depth = ex - 2 * STEPS, ey - 2 * STEPS, ez // 2
    rows = nx * ny
    for corner, layers, sign in ((c_low, LAYERS_HIGH, -1), (c_high, LAYERS_LOW[1], 1)):
        for row, (f, d, side, e) in enumerate(corner_rows(layers, sign)):
            y = ey - 1 - d if sign < 0 else ny + d
            x = STEPS - 1 - e if side < 0 else STEPS + nx + e
            place(cells, wide, wide_strip, f)[x, y : y + 1, 0:depth] = corner[row : row + 1, :]
    for x in (*range(STEPS), *range(STEPS + nx, ex)):
        value = wide_strip[x, ny:ey]
        for f, width in enumerate(WIDTHS):
            place(cells, wide, wide_strip, f)[x, ny:ey, depth:ez] = pltpu.roll(
                value, (-(LANE_BASES[f] + width)) % depth, 1
            )
    inside = inside_mask(ey, ez)
    index = arrived[:, 12, :].astype(jnp.int32)
    constants = emitter_constants(arrived)
    current = [states[c] for c in range(3)]
    previous = [states[3 + c] for c in range(3)]
    upper = states[6]
    pumped = states[7]
    for step in range(1, STEPS + 1):
        if step > 1:
            own = [
                cells[c, STEPS : STEPS + nx, 0:ny, 0:depth].reshape(rows, depth) for c in range(3)
            ]
            sample = gather_cells(cell_halves(own), index, row_hot, depth)
            advanced, previous, upper, pumped = bloch_step(
                sample, current, previous, upper, pumped, constants
            )
            if step == STEPS:
                change = [
                    (a - c) * (1.0 / TIME_STEP**2) for a, c in zip(advanced, current)
                ]
            current = advanced
        if step < STEPS:
            advance_magnetic(cells, field, inside, step, step - 1)
            for x in range(step, ex - step):
                advance_magnetic(cells, field, inside, step, x)
                advance_electric(cells, wide, field, step, x)
    for c in range(3):
        result[:, c, :] = current[c]
        result[:, 3 + c, :] = previous[c]
    result[:, 6, :] = upper
    result[:, 7, :] = pumped
    for c in range(3):
        changes[c] = change[c]


def last_kernel(cells, base, field, changes, row_hot, depth_hot, electric, magnetic):
    _, nx, ny, depth = electric.shape
    rows = nx * ny
    ey, ez = cells.shape[2:]
    sources = scatter_cells([changes[c] for c in range(3)], row_hot, depth_hot, rows)
    inside = inside_mask(ey, ez)
    advance_magnetic(cells, field, inside, STEPS, STEPS - 1)
    for x in range(STEPS, STEPS + nx):
        advance_magnetic(cells, field, inside, STEPS, x)
        curl = backward_curl(field, x)
        span = slice((x - STEPS) * ny, (x - STEPS + 1) * ny)
        scale = base[3, span]
        for c in range(3):
            own = curl[c][0:ny, 0:depth] + sources[c][span]
            electric[c, x - STEPS] = cells[c, x, 0:ny, 0:depth] + scale * own
            magnetic[c, x - STEPS] = field[c, x, 0:ny, 0:depth] * -TIME_STEP


def unpack_kernel(home, polar, popul):
    for i in range(2):
        for c in range(3):
            polar[i, c, 0] = home[:, 3 * i + c, :]
        popul[i, 0] = home[:, 6 + i, :]


def call(kernel, outs, final=(), aliases=None, limit=VMEM_LIMIT):
    shapes = [pltpu.VMEM(s[:-1], s[-1]) if isinstance(s[-1], type) else pltpu.VMEM(s, jnp.float32) for s in outs]
    shapes += [jax.ShapeDtypeStruct(s, jnp.float32) for s in final]
    return pl.pallas_call(
        kernel,
        out_shape=shapes,
        input_output_aliases=aliases or {},
        compiler_params=pltpu.CompilerParams(vmem_limit_bytes=limit),
    )


def near(*values):
    return [pltpu.with_memory_space_constraint(v, pltpu.VMEM) for v in values]


def shifted(value, axis, step):
    count = lax.axis_size(axis)
    pairs = [(i, i + step) for i in range(count) if 0 <= i + step < count]
    return lax.ppermute(value, axis, pairs)


def shards(
    electric, permittivity_class, cell_index, polarization, populations,
    resonance, dephasing, coupling, pump_rate,
):
    _, nx, ny, depth = electric.shape
    rows = nx * ny
    _, buckets, slots = cell_index.shape
    ex, ey, ez = nx + 2 * STEPS, ny + 2 * STEPS, 2 * depth
    hots = [
        (2 * rows, buckets * slots, jnp.bfloat16),
        (depth, buckets * slots, jnp.bfloat16),
    ]
    (packed,) = call(pack_kernel, [(buckets, 13, slots)], limit=HIGH_LIMIT)(
        cell_index, polarization, populations, resonance, dephasing, coupling, pump_rate
    )
    base, left = near(
        *call(
            base_kernel,
            [(GRID, rows, depth), (3 * depth, 2 * rows, jnp.bfloat16)],
            limit=HIGH_LIMIT,
        )(electric, permittivity_class)
    )
    arrived = lax.all_to_all(packed, ("gy", "gz"), split_axis=0, concat_axis=0, tiled=True)
    (arrived,) = near(arrived)
    coefs, strip, states, row_hot, depth_hot = near(
        *call(
            first_kernel,
            [(FIELDS - GRID, rows, depth), (rows, depth), (8, buckets, slots), *hots],
        )(arrived, base, left)
    )
    count_z = lax.axis_size("gz")
    if count_z == 2:
        from_low = from_high = lax.ppermute(strip, "gz", [(0, 1), (1, 0)])
    else:
        from_low = shifted(strip, "gz", 1)
        from_high = shifted(strip, "gz", -1)
    strip, *faces = call(
        functools.partial(faces_kernel, nx, ny, count_z),
        [
            (rows, depth),
            (len(LAYERS_LOW[0]), ny, depth),
            (len(LAYERS_HIGH), ny, depth),
            (len(LAYERS_LOW[1]), nx, depth),
            (len(LAYERS_HIGH), nx, depth),
        ],
    )(base, coefs, *near(from_low, from_high))
    (strip,) = near(strip)
    x_low, x_high = near(shifted(faces[1], "gx", 1), shifted(faces[0], "gx", -1))
    y_low, y_high = near(shifted(faces[3], "gy", 1), shifted(faces[2], "gy", -1))
    low, high = call(
        corners_kernel,
        [corner_shape(LAYERS_LOW[1], 1, depth), corner_shape(LAYERS_HIGH, -1, depth)],
    )(x_low, x_high)
    c_low, c_high = near(shifted(high, "gy", 1), shifted(low, "gy", -1))
    cells, wide, wide_strip = near(
        *call(
            assemble_kernel, [(3, ex, ey, ez), (FIELDS - 3, ex, ey, ez), (ex, ey, depth)]
        )(base, coefs, strip, x_low, x_high, y_low, y_high)
    )
    cells, _, field, result, changes = near(
        *call(
            steps_kernel,
            [
                cells.shape,
                wide.shape,
                (3, ex, ey, ez),
                (buckets, 8, slots),
                (3, buckets, slots),
            ],
            aliases={2: 0, 3: 1},
        )(c_low, c_high, cells, wide, wide_strip, row_hot, depth_hot, arrived, states)
    )
    home = lax.all_to_all(result, ("gy", "gz"), split_axis=0, concat_axis=0, tiled=True)
    electric, magnetic = call(last_kernel, [], [electric.shape, electric.shape])(
        cells, base, field, changes, row_hot, depth_hot
    )
    polar_out, popul_out = call(unpack_kernel, [], [polarization.shape, populations.shape])(
        *near(home)
    )
    return (electric, magnetic, polar_out, popul_out)


def solution(mesh):
    owners = P("gx", ("gy", "gz"), None)
    return jax.shard_map(
        shards,
        mesh=mesh,
        in_specs=(
            P(None, "gx", "gy", "gz"),
            P("gx", "gy", "gz"),
            owners,
            P(None, None, "gx", ("gy", "gz"), None),
            P(None, "gx", ("gy", "gz"), None),
            owners,
            owners,
            owners,
            owners,
        ),
        out_specs=(
            P(None, "gx", "gy", "gz"),
            P(None, "gx", "gy", "gz"),
            P(None, None, "gx", ("gy", "gz"), None),
            P(None, "gx", ("gy", "gz"), None),
        ),
        check_vma=False,
    )
```

```python
import functools

import jax
import jax.numpy as jnp
from jax import lax
from jax.experimental import pallas as pl
from jax.experimental.pallas import tpu as pltpu
from jax.sharding import PartitionSpec as P

STEPS = 4
TIME_STEP = 0.5
PUMP_DECAY = 0.2
UPPER_DECAY = 0.02
WORK_SHARE = 0.05
CLASS_PERMITTIVITY = (1.0, 2.1, 6.0, 12.25)

WIDTHS = (STEPS,) * 3 + (STEPS - 1,) * 4 + (STEPS - 2,) * 4 + (STEPS - 3,) * 9
FIELDS = len(WIDTHS)
GRID = 4
ALL_WIDTHS = WIDTHS + (STEPS,)
VECTORS = (0, 4, 7, 11)
LANE_BASES = tuple(2 * sum(WIDTHS[:i]) for i in range(FIELDS))
FOLDS = 2
LONG = pl.CostEstimate(flops=20_000_000_000, bytes_accessed=100_000_000, transcendentals=0)
VMEM_LIMIT = 24 * 1024 * 1024
HIGH_LIMIT = 56 * 1024 * 1024


def layer_list(skip_axis):
    layers = []
    for f, width in enumerate(ALL_WIDTHS):
        unused = skip_axis is not None and f - skip_axis in VECTORS
        layers += [(f, d) for d in range(width - 1 if unused else width)]
    return layers


LAYERS_LOW = (layer_list(0), layer_list(1))
LAYERS_HIGH = layer_list(None)


def corner_rows(layers, halo_sign):
    out = []
    furthest = 0 if halo_sign < 0 else 1
    for f, d in layers:
        width = ALL_WIDTHS[f]
        for side in (-1, 1):
            reach = width - d
            if side == halo_sign or any(
                f in (v, v + 1, v + 2) and f != v + furthest for v in VECTORS
            ):
                reach -= 1
            known = LAYERS_HIGH if side < 0 else LAYERS_LOW[1]
            out += [(f, d, side, e) for e in range(reach) if (f, e) in known]
    return out


def corner_shape(layers, halo_sign, depth):
    return (-(-len(corner_rows(layers, halo_sign)) // 8) * 8, depth)


def inverse_permittivity(classes):
    inverse = jnp.zeros(classes.shape, jnp.float32)
    for number, epsilon in enumerate(CLASS_PERMITTIVITY):
        inverse = jnp.where(classes == number, 1.0 / epsilon, inverse)
    return inverse


def halves(value):
    high = value.astype(jnp.bfloat16)
    low = (value - high.astype(jnp.float32)).astype(jnp.bfloat16)
    return high, low


def write_one_hots(index, row_hot, depth_hot, rows, depth):
    fold = depth // FOLDS
    shift = depth.bit_length() - 1
    buckets, slots = index.shape
    live = index < rows * depth
    part = lax.shift_right_logical(lax.bitwise_and(index, depth - 1), fold.bit_length() - 1)
    row = lax.shift_right_logical(index, shift) + part * rows
    row = jnp.where(live, row, -1)
    deep = lax.bitwise_and(index, fold - 1)
    rows_at = lax.broadcasted_iota(jnp.int32, (FOLDS * rows, slots), 0)
    deep_at = lax.broadcasted_iota(jnp.int32, (fold, slots), 0)
    for b in range(buckets):
        span = slice(b * slots, (b + 1) * slots)
        row_hot[:, span] = jnp.where(rows_at == row[b : b + 1], 1.0, 0.0).astype(jnp.bfloat16)
        depth_hot[:, span] = jnp.where(deep_at == deep[b : b + 1], 1.0, 0.0).astype(jnp.bfloat16)


def cell_halves(cells):
    parts = []
    for block in cells:
        turned = block.T
        fold = turned.shape[0] // FOLDS
        turned = [turned[i * fold : (i + 1) * fold] for i in range(FOLDS)]
        parts += halves(jnp.concatenate(turned, axis=1))
    return jnp.concatenate(parts, axis=0)


def gather_cells(left, index, row_hot, depth):
    buckets, slots = index.shape
    fold = depth // FOLDS
    size = 2 * fold
    samples = [[], [], []]
    group = 2 if buckets % 2 == 0 else 1
    place_at = lax.broadcasted_iota(jnp.int32, (size, slots), 0)
    place_at = lax.bitwise_and(place_at, fold - 1)
    for start in range(0, buckets, group):
        span = slice(start * slots, (start + group) * slots)
        picked = jnp.dot(left, row_hot[:, span], preferred_element_type=jnp.float32)
        for b in range(start, start + group):
            hit = place_at == lax.bitwise_and(index[b : b + 1], fold - 1)
            lanes = slice((b - start) * slots, (b - start + 1) * slots)
            for c in range(3):
                part = picked[c * size : (c + 1) * size, lanes]
                samples[c].append(jnp.sum(jnp.where(hit, part, 0.0), axis=0, keepdims=True))
    return [jnp.concatenate(rows, axis=0) for rows in samples]


def flat_row(value):
    buckets = value.shape[0]
    return jnp.concatenate([value[b : b + 1] for b in range(buckets)], axis=1)


def scatter_cells(values, row_hot, depth_hot, rows, group=4):
    hot = row_hot[...]
    deep = depth_hot[...]
    fold = deep.shape[0]
    out = []
    for start in range(0, len(values), group):
        some = [halves(flat_row(value)) for value in values[start : start + group]]
        total = 0.0
        for part in range(2):
            spread = jnp.concatenate([deep * pair[part] for pair in some], axis=0)
            total = total + lax.dot_general(
                spread, hot, (((1,), (1,)), ((), ())), preferred_element_type=jnp.float32
            )
        for i in range(len(some)):
            block = total[i * fold : (i + 1) * fold]
            block = [block[:, j * rows : (j + 1) * rows] for j in range(FOLDS)]
            out.append(jnp.concatenate(block, axis=0).T)
    return out


def emitter_constants(arrived):
    freq, dephase, strength, pumping = [arrived[:, f, :] for f in range(8, 12)]
    damping = 0.5 * TIME_STEP * dephase
    stiffness = freq * TIME_STEP * (freq * TIME_STEP)
    scale = 1.0 + damping
    keep = (2.0 - stiffness) / scale
    back = (1.0 - damping) / scale
    drive = strength * (TIME_STEP * TIME_STEP) / scale
    share = WORK_SHARE / freq
    return keep, back, drive, share, pumping


def bloch_step(sample, current, previous, upper, pumped, constants):
    keep, back, drive, share, pumping = constants
    lower = 1.0 - upper - pumped
    push = drive * (lower - upper)
    advanced = [keep * c - back * p + push * s for c, p, s in zip(current, previous, sample)]
    work = sum(s * (a - p) for s, a, p in zip(sample, advanced, previous)) / (2.0 * TIME_STEP)
    pumped_next = pumped + TIME_STEP * (pumping * lower - PUMP_DECAY * pumped)
    upper_next = upper + TIME_STEP * (
        PUMP_DECAY * pumped - UPPER_DECAY * upper + share * work
    )
    return advanced, current, upper_next, pumped_next


def pack_kernel(index, polar, popul, freq, dephase, strength, pumping, out):
    for i in range(2):
        for c in range(3):
            out[:, 3 * i + c, :] = polar[i, c, 0]
    for i in range(2):
        out[:, 6 + i, :] = popul[i, 0]
    for f, source in enumerate((freq, dephase, strength, pumping)):
        out[:, 8 + f, :] = source[0]
    out[:, 12, :] = index[0].astype(jnp.float32)


def source_of(base, coefs, strip, f):
    if f < GRID:
        return base.at[f]
    return coefs.at[f - GRID] if f < FIELDS else strip


def base_kernel(electric, classes, base, left):
    _, nx, ny, depth = electric.shape
    rows = nx * ny
    for c in range(3):
        base[c] = electric[c].reshape(rows, depth)
    base[3] = inverse_permittivity(classes[...].reshape(rows, depth)) * -(TIME_STEP**2)
    left[...] = cell_halves([base[c] for c in range(3)])


def first_kernel(arrived, base, left, coefs, strip, states, row_hot, depth_hot):
    _, rows, depth = base.shape
    index = arrived[:, 12, :].astype(jnp.int32)
    write_one_hots(index, row_hot, depth_hot, rows, depth)
    sample = gather_cells(left[...], index, row_hot, depth)
    constants = emitter_constants(arrived)
    keep, back, drive, share, pumping = constants
    start = [arrived[:, c, :] for c in range(3)]
    before = [arrived[:, 3 + c, :] for c in range(3)]
    now, _, upper, pumped = bloch_step(
        sample, start, before, arrived[:, 6, :], arrived[:, 7, :], constants
    )
    for c in range(3):
        states[c] = now[c]
        states[3 + c] = start[c]
    states[6] = upper
    states[7] = pumped
    lower = 1.0 - upper - pumped
    push = drive * (lower - upper)
    pumped_after = pumped + TIME_STEP * (pumping * lower - PUMP_DECAY * pumped)
    upper_free = upper + TIME_STEP * (PUMP_DECAY * pumped - UPPER_DECAY * upper)
    free = [keep * n - back * s for n, s in zip(now, start)]
    values = [n - s for n, s in zip(now, start)]
    values += [f - n for f, n in zip(free, now)]
    values.append(push)
    values += [(keep - 1.0) * f - back * n for f, n in zip(free, now)]
    values.append((keep - 1.0) * push)
    values.append(drive * (1.0 - pumped_after - 2.0 * upper_free))
    values += [-drive * share * (f - s) for f, s in zip(free, start)]
    values.append(-drive * share * push)
    values = [value * (1.0 / TIME_STEP**2) for value in values]
    for number, block in enumerate(scatter_cells(values, row_hot, depth_hot, rows)):
        coefs[number] = block
    lane = lax.broadcasted_iota(jnp.int32, (rows, depth), 1)
    packed = jnp.zeros((rows, depth), jnp.float32)
    for f, width in enumerate(WIDTHS):
        at = LANE_BASES[f]
        turned = pltpu.roll(source_of(base, coefs, strip, f)[...], (at + width) % depth, 1)
        packed = jnp.where((lane >= at) & (lane < at + 2 * width), turned, packed)
    strip[...] = packed


def faces_kernel(nx, ny, count_z, base, coefs, from_low, from_high, strip, x_low, x_high, y_low, y_high):
    rows, depth = strip.shape
    lane = lax.broadcasted_iota(jnp.int32, (rows, depth), 1)
    top = jnp.zeros((rows, depth), jnp.bool_)
    for f, width in enumerate(WIDTHS):
        at = LANE_BASES[f]
        top = top | ((lane >= at) & (lane < at + width))
    me = lax.axis_index("gz")
    strip[...] = jnp.where(
        top,
        jnp.where(me > 0, from_low[...], 0.0),
        jnp.where(me < count_z - 1, from_high[...], 0.0),
    )

    def source(f):
        return source_of(base, coefs, strip, f)

    for at, (f, d) in enumerate(LAYERS_LOW[0]):
        x_low[at] = source(f)[d * ny : (d + 1) * ny, :]
    for at, (f, d) in enumerate(LAYERS_HIGH):
        x_high[at] = source(f)[(nx - 1 - d) * ny : (nx - d) * ny, :]
    for at, (f, d) in enumerate(LAYERS_LOW[1]):
        y_low[at] = source(f)[pl.ds(d, nx, stride=ny), :]
    for at, (f, d) in enumerate(LAYERS_HIGH):
        y_high[at] = source(f)[pl.ds(ny - 1 - d, nx, stride=ny), :]


def corners_kernel(halo_low, halo_high, low, high):
    nx = halo_low.shape[1]
    for face, layers, sign in ((low, LAYERS_LOW[0], -1), (high, LAYERS_HIGH, 1)):
        for row, (f, d, side, e) in enumerate(corner_rows(layers, -sign)):
            x = d if sign < 0 else nx - 1 - d
            if side < 0:
                value = halo_low[LAYERS_HIGH.index((f, e)), x : x + 1, :]
            else:
                value = halo_high[LAYERS_LOW[1].index((f, e)), x : x + 1, :]
            face[row : row + 1, :] = value


def place(cells, wide, wide_strip, f):
    if f < 3:
        return cells.at[f]
    return wide.at[f - 3] if f < FIELDS else wide_strip


def spread_strip(cells, wide, wide_strip, x, y, count, fields):
    depth = wide_strip.shape[2]
    value = wide_strip[x, y : y + count]
    for f in fields:
        place(cells, wide, wide_strip, f)[x, y : y + count, depth : 2 * depth] = pltpu.roll(
            value, (-(LANE_BASES[f] + WIDTHS[f])) % depth, 1
        )


def assemble_kernel(
    base, coefs, strip, y_low, y_high, cells, wide, wide_strip, field, snaps
):
    _, nx, depth = y_low.shape
    _, ex, ey, ez = cells.shape
    ny = ey - 2 * STEPS
    for f in range(FIELDS + 1):
        source = source_of(base, coefs, strip, f)
        target = place(cells, wide, wide_strip, f)
        target[STEPS : STEPS + nx, 0:ny, 0:depth] = source[...].reshape(nx, ny, depth)
        target[STEPS : STEPS + nx, ny:ey, 0:depth] = jnp.zeros((nx, 2 * STEPS, depth), jnp.float32)
    for halo, layers, sign in ((y_low, LAYERS_HIGH, -1), (y_high, LAYERS_LOW[1], 1)):
        for at, (f, d) in enumerate(layers):
            y = ey - 1 - d if sign < 0 else ny + d
            for x in range(nx):
                place(cells, wide, wide_strip, f)[STEPS + x, y : y + 1, 0:depth] = halo[at, x : x + 1, :]
    for x in range(STEPS, STEPS + nx):
        spread_strip(cells, wide, wide_strip, x, 0, ey, range(FIELDS))
    inside = inside_mask(ey, ez)
    for step in range(1, STEPS):
        for x in range(STEPS + step - 1, STEPS + nx - step):
            advance_magnetic(cells, field, inside, step, x)
            if x >= STEPS + step:
                advance_electric(cells, wide, field, snaps, step, x)


def side_slabs(nx):
    for d in range(STEPS):
        fields = [f for f in range(FIELDS) if WIDTHS[f] > d]
        yield STEPS - 1 - d, fields
        yield STEPS + nx + d, fields


def sides_kernel(x_low, x_high, _cells, _wide, _strip, cells, wide, wide_strip):
    _, ny, depth = x_low.shape
    _, ex, ey, _ = cells.shape
    nx = ex - 2 * STEPS
    for at, (f, d) in enumerate(LAYERS_HIGH):
        place(cells, wide, wide_strip, f)[STEPS - 1 - d, 0:ny, 0:depth] = x_low[at]
    for at, (f, d) in enumerate(LAYERS_LOW[0]):
        place(cells, wide, wide_strip, f)[STEPS + nx + d, 0:ny, 0:depth] = x_high[at]
    for x, fields in side_slabs(nx):
        for f in (*fields, FIELDS):
            target = place(cells, wide, wide_strip, f)
            target[x, ny:ey, :] = jnp.zeros((2 * STEPS, target.shape[2]), jnp.float32)
        spread_strip(cells, wide, wide_strip, x, 0, ny, fields)


def rolls(ey, ez):
    return (
        lambda v: pltpu.roll(v, ey - 1, 0),
        lambda v: pltpu.roll(v, ez - 1, 1),
        lambda v: pltpu.roll(v, 1, 0),
        lambda v: pltpu.roll(v, 1, 1),
    )


def inside_mask(ey, ez):
    row_at = lax.broadcasted_iota(jnp.int32, (ey, ez), 0)
    lane_at = lax.broadcasted_iota(jnp.int32, (ey, ez), 1)
    outside = ((row_at >= ey - STEPS) & (lax.axis_index("gy") == 0)) | (
        (lane_at >= ez - STEPS) & (lax.axis_index("gz") == 0)
    )
    return jnp.where(outside, 0.0, 1.0)


def advance_magnetic(cells, field, inside, step, x):
    _, _, ey, ez = cells.shape
    up_y, up_z, _, _ = rolls(ey, ez)
    e0, e1, e2 = cells[0, x], cells[1, x], cells[2, x]
    f1, f2 = cells[1, x + 1], cells[2, x + 1]
    curl = (
        (up_y(e2) - e2) - (up_z(e1) - e1),
        (up_z(e0) - e0) - (f2 - e2),
        (f1 - e1) - (up_y(e0) - e0),
    )
    mask = inside
    if x < STEPS:
        mask = inside * jnp.where(lax.axis_index("gx") == 0, 0.0, 1.0)
    for c in range(3):
        change = curl[c] * mask
        field[c, x] = field[c, x] + change if step > 1 else change


def backward_curl(field, x):
    _, _, ey, ez = field.shape
    _, _, down_y, down_z = rolls(ey, ez)
    m0, m1, m2 = field[0, x], field[1, x], field[2, x]
    l1, l2 = field[1, x - 1], field[2, x - 1]
    return (
        (m2 - down_y(m2)) - (m1 - down_z(m1)),
        (m0 - down_z(m0)) - (m2 - l2),
        (m1 - l1) - (m0 - down_y(m0)),
    )


def advance_electric(cells, wide, field, snaps, step, x):
    curl = backward_curl(field, x)
    old = [cells[c, x] for c in range(3)]
    if step == 2:
        gain = wide[7, x]
        source = [wide[4 + c, x] + gain * old[c] for c in range(3)]
        if STEPS - 2 < x < wide.shape[1] - STEPS + 1:
            ratio = wide[11, x]
            for c in range(3):
                wide[8 + c, x] = wide[8 + c, x] + ratio * old[c]
            square = old[0] * old[0] + old[1] * old[1] + old[2] * old[2]
            wide[12, x] = (
                wide[12, x]
                + (wide[13, x] * old[0] + wide[14, x] * old[1] + wide[15, x] * old[2])
                + wide[16, x] * square
            )
    elif step == 3:
        gain = wide[12, x]
        source = [wide[8 + c, x] + gain * old[c] for c in range(3)]
    else:
        source = [wide[1 + c, x] for c in range(3)]
    scale = wide[0, x]
    _, rows, depth = snaps.shape
    ny = cells.shape[2] - 2 * STEPS
    at = (x - STEPS) * ny
    for c in range(3):
        new = old[c] + scale * (curl[c] + source[c])
        cells[c, x] = new
        if 0 <= at < rows:
            snaps[(step - 1) * 3 + c, at : at + ny, :] = new[0:ny, 0:depth]


def steps_kernel(
    c_low, c_high, _cells, _wide, _field, _snaps, wide_strip, row_hot, depth_hot,
    arrived, states, cells, wide, field, snaps, result, changes,
):
    _, ex, ey, ez = wide.shape
    nx, ny, depth = ex - 2 * STEPS, ey - 2 * STEPS, ez // 2
    rows = nx * ny
    for corner, layers, sign in ((c_low, LAYERS_HIGH, -1), (c_high, LAYERS_LOW[0], 1)):
        for row, (f, d, side, e) in enumerate(corner_rows(layers, sign)):
            x = STEPS - 1 - d if sign < 0 else STEPS + nx + d
            y = ey - 1 - e if side < 0 else ny + e
            place(cells, wide, wide_strip, f)[x, y : y + 1, 0:depth] = corner[row : row + 1, :]
    for x, fields in side_slabs(nx):
        fields = [f for f in fields if WIDTHS[f] > 1]
        spread_strip(cells, wide, wide_strip, x, ny, 2 * STEPS, fields)
    inside = inside_mask(ey, ez)
    index = arrived[:, 12, :].astype(jnp.int32)
    constants = emitter_constants(arrived)
    current = [states[c] for c in range(3)]
    previous = [states[3 + c] for c in range(3)]
    upper = states[6]
    pumped = states[7]
    for step in range(1, STEPS + 1):
        if step > 1:
            own = [snaps[(step - 2) * 3 + c] for c in range(3)]
            sample = gather_cells(cell_halves(own), index, row_hot, depth)
            advanced, previous, upper, pumped = bloch_step(
                sample, current, previous, upper, pumped, constants
            )
            if step == STEPS:
                change = [
                    (a - c) * (1.0 / TIME_STEP**2) for a, c in zip(advanced, current)
                ]
            current = advanced
        if step < STEPS:
            done = range(STEPS + step, STEPS + nx - step)
            for x in range(step - 1, ex - step):
                if x not in done and x + 1 not in done:
                    advance_magnetic(cells, field, inside, step, x)
                if x not in done and x >= step:
                    advance_electric(cells, wide, field, snaps, step, x)
    for c in range(3):
        result[:, c, :] = current[c]
        result[:, 3 + c, :] = previous[c]
    result[:, 6, :] = upper
    result[:, 7, :] = pumped
    for c in range(3):
        changes[c] = change[c]


def last_kernel(cells, base, field, changes, row_hot, depth_hot, electric, magnetic):
    _, nx, ny, depth = electric.shape
    rows = nx * ny
    ey, ez = cells.shape[2:]
    sources = scatter_cells([changes[c] for c in range(3)], row_hot, depth_hot, rows)
    inside = inside_mask(ey, ez)
    advance_magnetic(cells, field, inside, STEPS, STEPS - 1)
    for x in range(STEPS, STEPS + nx):
        advance_magnetic(cells, field, inside, STEPS, x)
        curl = backward_curl(field, x)
        span = slice((x - STEPS) * ny, (x - STEPS + 1) * ny)
        scale = base[3, span]
        for c in range(3):
            own = curl[c][0:ny, 0:depth] + sources[c][span]
            electric[c, x - STEPS] = cells[c, x, 0:ny, 0:depth] + scale * own
            magnetic[c, x - STEPS] = field[c, x, 0:ny, 0:depth] * -TIME_STEP


def unpack_kernel(home, polar, popul):
    for i in range(2):
        for c in range(3):
            polar[i, c, 0] = home[:, 3 * i + c, :]
        popul[i, 0] = home[:, 6 + i, :]


def call(kernel, outs, final=(), aliases=None, limit=VMEM_LIMIT, cost=None):
    shapes = [pltpu.VMEM(s[:-1], s[-1]) if isinstance(s[-1], type) else pltpu.VMEM(s, jnp.float32) for s in outs]
    shapes += [jax.ShapeDtypeStruct(s, jnp.float32) for s in final]
    return pl.pallas_call(
        kernel,
        out_shape=shapes,
        input_output_aliases=aliases or {},
        cost_estimate=cost,
        compiler_params=pltpu.CompilerParams(vmem_limit_bytes=limit),
    )


def near(*values):
    return [pltpu.with_memory_space_constraint(v, pltpu.VMEM) for v in values]


def shifted(value, axis, step):
    count = lax.axis_size(axis)
    pairs = [(i, i + step) for i in range(count) if 0 <= i + step < count]
    return lax.ppermute(value, axis, pairs)


def shards(
    electric, permittivity_class, cell_index, polarization, populations,
    resonance, dephasing, coupling, pump_rate,
):
    _, nx, ny, depth = electric.shape
    rows = nx * ny
    _, buckets, slots = cell_index.shape
    ex, ey, ez = nx + 2 * STEPS, ny + 2 * STEPS, 2 * depth
    hots = [
        (FOLDS * rows, buckets * slots, jnp.bfloat16),
        (depth // FOLDS, buckets * slots, jnp.bfloat16),
    ]
    (packed,) = call(pack_kernel, [(buckets, 13, slots)], limit=HIGH_LIMIT)(
        cell_index, polarization, populations, resonance, dephasing, coupling, pump_rate
    )
    base, left = near(
        *call(
            base_kernel,
            [(GRID, rows, depth), (6 * depth // FOLDS, FOLDS * rows, jnp.bfloat16)],
            limit=HIGH_LIMIT,
        )(electric, permittivity_class)
    )
    arrived = lax.all_to_all(packed, ("gy", "gz"), split_axis=0, concat_axis=0, tiled=True)
    (arrived,) = near(arrived)
    coefs, strip, states, row_hot, depth_hot = near(
        *call(
            first_kernel,
            [(FIELDS - GRID, rows, depth), (rows, depth), (8, buckets, slots), *hots],
        )(arrived, base, left)
    )
    count_z = lax.axis_size("gz")
    if count_z == 2:
        from_low = from_high = lax.ppermute(strip, "gz", [(0, 1), (1, 0)])
    else:
        from_low = shifted(strip, "gz", 1)
        from_high = shifted(strip, "gz", -1)
    strip, *faces = call(
        functools.partial(faces_kernel, nx, ny, count_z),
        [
            (rows, depth),
            (len(LAYERS_LOW[0]), ny, depth),
            (len(LAYERS_HIGH), ny, depth),
            (len(LAYERS_LOW[1]), nx, depth),
            (len(LAYERS_HIGH), nx, depth),
        ],
    )(base, coefs, *near(from_low, from_high))
    (strip,) = near(strip)
    x_low, x_high = near(shifted(faces[1], "gx", 1), shifted(faces[0], "gx", -1))
    y_low, y_high = near(shifted(faces[3], "gy", 1), shifted(faces[2], "gy", -1))
    low, high = call(
        corners_kernel,
        [corner_shape(LAYERS_LOW[0], 1, depth), corner_shape(LAYERS_HIGH, -1, depth)],
        cost=LONG,
    )(y_low, y_high)
    c_low, c_high = near(shifted(high, "gx", 1), shifted(low, "gx", -1))
    state = near(
        *call(
            assemble_kernel,
            [
                (3, ex, ey, ez),
                (FIELDS - 3, ex, ey, ez),
                (ex, ey, depth),
                (3, ex, ey, ez),
                (3 * (STEPS - 1), rows, depth),
            ],
        )(base, coefs, strip, y_low, y_high)
    )
    cells, wide, wide_strip, field, snaps = state
    cells, wide, wide_strip = near(
        *call(
            sides_kernel,
            [cells.shape, wide.shape, wide_strip.shape],
            aliases={2: 0, 3: 1, 4: 2},
        )(x_low, x_high, cells, wide, wide_strip)
    )
    cells, _, field, _, result, changes = near(
        *call(
            steps_kernel,
            [
                cells.shape,
                wide.shape,
                field.shape,
                snaps.shape,
                (buckets, 8, slots),
                (3, buckets, slots),
            ],
            aliases={2: 0, 3: 1, 4: 2, 5: 3},
        )(c_low, c_high, cells, wide, field, snaps, wide_strip, row_hot, depth_hot, arrived, states)
    )
    home = lax.all_to_all(result, ("gy", "gz"), split_axis=0, concat_axis=0, tiled=True)
    electric, magnetic = call(last_kernel, [], [electric.shape, electric.shape])(
        cells, base, field, changes, row_hot, depth_hot
    )
    polar_out, popul_out = call(unpack_kernel, [], [polarization.shape, populations.shape])(
        *near(home)
    )
    return (electric, magnetic, polar_out, popul_out)


def solution(mesh):
    owners = P("gx", ("gy", "gz"), None)
    return jax.shard_map(
        shards,
        mesh=mesh,
        in_specs=(
            P(None, "gx", "gy", "gz"),
            P("gx", "gy", "gz"),
            owners,
            P(None, None, "gx", ("gy", "gz"), None),
            P(None, "gx", ("gy", "gz"), None),
            owners,
            owners,
            owners,
            owners,
        ),
        out_specs=(
            P(None, "gx", "gy", "gz"),
            P(None, "gx", "gy", "gz"),
            P(None, None, "gx", ("gy", "gz"), None),
            P(None, "gx", ("gy", "gz"), None),
        ),
        check_vma=False,
    )
```

```python
import functools

import jax
import jax.numpy as jnp
from jax import lax
from jax.experimental import pallas as pl
from jax.experimental.pallas import tpu as pltpu
from jax.sharding import PartitionSpec as P

STEPS = 4
TIME_STEP = 0.5
PUMP_DECAY = 0.2
UPPER_DECAY = 0.02
WORK_SHARE = 0.05
CLASS_PERMITTIVITY = (1.0, 2.1, 6.0, 12.25)

WIDTHS = (STEPS,) * 3 + (STEPS - 1,) * 4 + (STEPS - 2,) * 4 + (STEPS - 3,) * 9
FIELDS = len(WIDTHS)
GRID = 4
VECTORS = (0, 4, 7, 11)
LANE_BASES = tuple(sum(WIDTHS[:i]) for i in range(FIELDS))
LAYER_LANES = tuple(sum(w for w in WIDTHS if w > d) for d in range(STEPS))
LAYER_BASES = tuple(sum(LAYER_LANES[:d]) for d in range(STEPS + 1))
FOLDS = 2
LONG = pl.CostEstimate(flops=20_000_000_000, bytes_accessed=100_000_000, transcendentals=0)
VMEM_LIMIT = 24 * 1024 * 1024
HIGH_LIMIT = 56 * 1024 * 1024


def layer_list(skip_axis, strips):
    layers = []
    for f, width in enumerate(WIDTHS):
        unused = skip_axis is not None and f - skip_axis in VECTORS
        layers += [(f, d) for d in range(width - 1 if unused else width)]
    return layers + [(FIELDS + i, 0) for i in range(strips)]


def low_layers(axis, strips):
    return layer_list(axis, strips)


def high_layers(strips):
    return layer_list(None, strips)


def corner_rows(halo_sign, strips):
    out = []
    furthest = 0 if halo_sign < 0 else 1
    known_x = high_layers(0) if halo_sign < 0 else low_layers(0, 0)
    for f, width in enumerate(WIDTHS + (STEPS,) * strips):
        for d in range(width):
            if f < FIELDS and (f, d) not in known_x:
                continue
            for side in (-1, 1):
                reach = width - d
                if side == halo_sign or any(
                    f in (v, v + 1, v + 2) and f != v + furthest for v in VECTORS
                ):
                    reach -= 1
                known = high_layers(0) if side < 0 else low_layers(1, 0)
                out += [
                    (f, d, side, e)
                    for e in range(reach)
                    if f >= FIELDS or (f, e) in known
                ]
    return out


def corner_shape(halo_sign, strips, depth):
    return (-(-len(corner_rows(halo_sign, strips)) // 8) * 8, depth)


def share_lanes(layers):
    lane = lax.broadcasted_iota(jnp.int32, layers[0].shape, 1)
    out = layers[0]
    for d in range(1, STEPS):
        turned = pltpu.roll(layers[d], LAYER_BASES[d], 1)
        out = jnp.where(lane >= LAYER_BASES[d], turned, out)
    return out


def layer_of_shared(shared, d):
    depth = shared.shape[1]
    return pltpu.roll(shared, depth - LAYER_BASES[d], 1) if d else shared


def inverse_permittivity(classes):
    inverse = jnp.zeros(classes.shape, jnp.float32)
    for number, epsilon in enumerate(CLASS_PERMITTIVITY):
        inverse = jnp.where(classes == number, 1.0 / epsilon, inverse)
    return inverse


def halves(value):
    high = value.astype(jnp.bfloat16)
    low = (value - high.astype(jnp.float32)).astype(jnp.bfloat16)
    return high, low


def write_one_hots(index, row_hot, depth_hot, rows, depth):
    fold = depth // FOLDS
    shift = depth.bit_length() - 1
    buckets, slots = index.shape
    live = index < rows * depth
    part = lax.shift_right_logical(lax.bitwise_and(index, depth - 1), fold.bit_length() - 1)
    row = lax.shift_right_logical(index, shift) + part * rows
    row = jnp.where(live, row, -1)
    deep = lax.bitwise_and(index, fold - 1)
    rows_at = lax.broadcasted_iota(jnp.int32, (FOLDS * rows, slots), 0)
    deep_at = lax.broadcasted_iota(jnp.int32, (fold, slots), 0)
    for b in range(buckets):
        span = slice(b * slots, (b + 1) * slots)
        row_hot[:, span] = jnp.where(rows_at == row[b : b + 1], 1.0, 0.0).astype(jnp.bfloat16)
        depth_hot[:, span] = jnp.where(deep_at == deep[b : b + 1], 1.0, 0.0).astype(jnp.bfloat16)


def cell_halves(cells):
    parts = []
    for block in cells:
        turned = block.T
        fold = turned.shape[0] // FOLDS
        turned = [turned[i * fold : (i + 1) * fold] for i in range(FOLDS)]
        parts += halves(jnp.concatenate(turned, axis=1))
    return jnp.concatenate(parts, axis=0)


def gather_cells(left, index, row_hot, depth):
    buckets, slots = index.shape
    fold = depth // FOLDS
    size = 2 * fold
    samples = [[], [], []]
    group = 2 if buckets % 2 == 0 else 1
    place_at = lax.broadcasted_iota(jnp.int32, (size, slots), 0)
    place_at = lax.bitwise_and(place_at, fold - 1)
    for start in range(0, buckets, group):
        span = slice(start * slots, (start + group) * slots)
        picked = jnp.dot(left, row_hot[:, span], preferred_element_type=jnp.float32)
        for b in range(start, start + group):
            hit = place_at == lax.bitwise_and(index[b : b + 1], fold - 1)
            lanes = slice((b - start) * slots, (b - start + 1) * slots)
            for c in range(3):
                part = picked[c * size : (c + 1) * size, lanes]
                samples[c].append(jnp.sum(jnp.where(hit, part, 0.0), axis=0, keepdims=True))
    return [jnp.concatenate(rows, axis=0) for rows in samples]


def flat_row(value):
    buckets = value.shape[0]
    return jnp.concatenate([value[b : b + 1] for b in range(buckets)], axis=1)


def scatter_cells(values, row_hot, depth_hot, rows, group=4):
    hot = row_hot[...]
    deep = depth_hot[...]
    fold = deep.shape[0]
    out = []
    for start in range(0, len(values), group):
        some = [halves(flat_row(value)) for value in values[start : start + group]]
        total = 0.0
        for part in range(2):
            spread = jnp.concatenate([deep * pair[part] for pair in some], axis=0)
            total = total + lax.dot_general(
                spread, hot, (((1,), (1,)), ((), ())), preferred_element_type=jnp.float32
            )
        for i in range(len(some)):
            block = total[i * fold : (i + 1) * fold]
            block = [block[:, j * rows : (j + 1) * rows] for j in range(FOLDS)]
            out.append(jnp.concatenate(block, axis=0).T)
    return out


def emitter_constants(arrived):
    freq, dephase, strength, pumping = [arrived[:, f, :] for f in range(8, 12)]
    damping = 0.5 * TIME_STEP * dephase
    stiffness = freq * TIME_STEP * (freq * TIME_STEP)
    scale = 1.0 + damping
    keep = (2.0 - stiffness) / scale
    back = (1.0 - damping) / scale
    drive = strength * (TIME_STEP * TIME_STEP) / scale
    share = WORK_SHARE / freq
    return keep, back, drive, share, pumping


def bloch_step(sample, current, previous, upper, pumped, constants):
    keep, back, drive, share, pumping = constants
    lower = 1.0 - upper - pumped
    push = drive * (lower - upper)
    advanced = [keep * c - back * p + push * s for c, p, s in zip(current, previous, sample)]
    work = sum(s * (a - p) for s, a, p in zip(sample, advanced, previous)) / (2.0 * TIME_STEP)
    pumped_next = pumped + TIME_STEP * (pumping * lower - PUMP_DECAY * pumped)
    upper_next = upper + TIME_STEP * (
        PUMP_DECAY * pumped - UPPER_DECAY * upper + share * work
    )
    return advanced, current, upper_next, pumped_next


def pack_kernel(
    electric, classes, index, polar, popul, freq, dephase, strength, pumping, out, base, left
):
    for i in range(2):
        for c in range(3):
            out[:, 3 * i + c, :] = polar[i, c, 0]
    for i in range(2):
        out[:, 6 + i, :] = popul[i, 0]
    for f, source in enumerate((freq, dephase, strength, pumping)):
        out[:, 8 + f, :] = source[0]
    out[:, 12, :] = index[0].astype(jnp.float32)
    _, nx, ny, depth = electric.shape
    rows = nx * ny
    for c in range(3):
        base[c] = electric[c].reshape(rows, depth)
    base[3] = inverse_permittivity(classes[...].reshape(rows, depth)) * -(TIME_STEP**2)
    left[...] = cell_halves([base[c] for c in range(3)])


def source_of(base, coefs, strip, f):
    if f < GRID:
        return base.at[f]
    return coefs.at[f - GRID] if f < FIELDS else strip.at[f - FIELDS]


def first_kernel(arrived, base, left, coefs, states, row_hot, depth_hot, *strip):
    _, rows, depth = base.shape
    index = arrived[:, 12, :].astype(jnp.int32)
    write_one_hots(index, row_hot, depth_hot, rows, depth)
    sample = gather_cells(left[...], index, row_hot, depth)
    constants = emitter_constants(arrived)
    keep, back, drive, share, pumping = constants
    start = [arrived[:, c, :] for c in range(3)]
    before = [arrived[:, 3 + c, :] for c in range(3)]
    now, _, upper, pumped = bloch_step(
        sample, start, before, arrived[:, 6, :], arrived[:, 7, :], constants
    )
    for c in range(3):
        states[c] = now[c]
        states[3 + c] = start[c]
    states[6] = upper
    states[7] = pumped
    lower = 1.0 - upper - pumped
    push = drive * (lower - upper)
    pumped_after = pumped + TIME_STEP * (pumping * lower - PUMP_DECAY * pumped)
    upper_free = upper + TIME_STEP * (PUMP_DECAY * pumped - UPPER_DECAY * upper)
    free = [keep * n - back * s for n, s in zip(now, start)]
    values = [n - s for n, s in zip(now, start)]
    values += [f - n for f, n in zip(free, now)]
    values.append(push)
    values += [(keep - 1.0) * f - back * n for f, n in zip(free, now)]
    values.append((keep - 1.0) * push)
    values.append(drive * (1.0 - pumped_after - 2.0 * upper_free))
    values += [-drive * share * (f - s) for f, s in zip(free, start)]
    values.append(-drive * share * push)
    values = [value * (1.0 / TIME_STEP**2) for value in values]
    for number, block in enumerate(scatter_cells(values, row_hot, depth_hot, rows)):
        coefs[number] = block
    lane = lax.broadcasted_iota(jnp.int32, (rows, depth), 1)
    strips = len(strip)
    for i in range(strips):
        top = 1 - i if strips > 1 else jnp.where(lax.axis_index("gz") == 0, 1, 0)
        packed = jnp.zeros((rows, depth), jnp.float32)
        for f, width in enumerate(WIDTHS):
            at = LANE_BASES[f]
            turned = pltpu.roll(source_of(base, coefs, None, f)[...], at + width * top, 1)
            packed = jnp.where((lane >= at) & (lane < at + width), turned, packed)
        strip[i][0] = packed


def join_kernel(first, second, out):
    out[0] = first[0]
    out[1] = second[0]


def faces_kernel(nx, ny, base, coefs, strip, y_low, y_high, x_low, x_high):
    strips = strip.shape[0]
    for face, layers, sign, axis in (
        (y_low, low_layers(1, strips), -1, 1),
        (y_high, high_layers(strips), 1, 1),
        (x_low, low_layers(0, strips), -1, 0),
        (x_high, high_layers(strips), 1, 0),
    ):

        def layer(f, d):
            source = source_of(base, coefs, strip, f)
            at = d if sign < 0 else (nx, ny)[axis] - 1 - d
            if axis == 1:
                return source[pl.ds(at, nx, stride=ny), :]
            return source[at * ny : (at + 1) * ny, :]

        for at, (f, d) in enumerate(layers):
            if f < FIELDS:
                face[at] = layer(f, d)
            else:
                face[at] = share_lanes([layer(f, i) for i in range(STEPS)])


def corners_kernel(strips, halo_low, halo_high, low, high):
    nx = halo_low.shape[1]
    for face, sign in ((low, -1), (high, 1)):
        for row, (f, d, side, e) in enumerate(corner_rows(-sign, strips)):
            x = d if sign < 0 else nx - 1 - d
            halo = halo_low if side < 0 else halo_high
            layers = high_layers(strips) if side < 0 else low_layers(1, strips)
            at = layers.index((f, e if f < FIELDS else 0))
            value = halo[at, x : x + 1, :]
            face[row : row + 1, :] = value if f < FIELDS else layer_of_shared(value, e)


def place(cells, wide, wide_strip, f):
    if f < 3:
        return cells.at[f]
    return wide.at[f - 3] if f < FIELDS else wide_strip.at[f - FIELDS]


def spread_strip(cells, wide, wide_strip, x, y, count, fields):
    strips, _, _, depth = wide_strip.shape
    values = [wide_strip[i, x, y : y + count] for i in range(strips)]
    upper = lax.broadcasted_iota(jnp.int32, (count, depth), 1) >= depth // 2
    low = lax.axis_index("gz") > 0
    for f in fields:
        at, width = LANE_BASES[f], WIDTHS[f]
        if strips == 1:
            shift = lax.bitwise_and(depth - at - jnp.where(low, width, 0), depth - 1)
            value = pltpu.roll(values[0], shift, 1)
            if f < GRID:
                value = jnp.where(upper == low, value, 0.0)
        else:
            value = jnp.where(
                upper,
                pltpu.roll(values[0], (depth - at - width) % depth, 1),
                pltpu.roll(values[1], (depth - at) % depth, 1),
            )
        place(cells, wide, wide_strip, f)[x, y : y + count, depth : 2 * depth] = value


def assemble_kernel(
    base, coefs, strip, y_low, y_high, cells, wide, wide_strip, field, snaps
):
    _, nx, depth = y_low.shape
    _, ex, ey, ez = cells.shape
    ny = ey - 2 * STEPS
    strips = strip.shape[0]
    for f in range(FIELDS + strips):
        source = source_of(base, coefs, strip, f)
        target = place(cells, wide, wide_strip, f)
        target[STEPS : STEPS + nx, 0:ny, 0:depth] = source[...].reshape(nx, ny, depth)
        target[STEPS : STEPS + nx, ny:ey, 0:depth] = jnp.zeros((nx, 2 * STEPS, depth), jnp.float32)
    for halo, layers, sign in (
        (y_low, high_layers(strips), -1),
        (y_high, low_layers(1, strips), 1),
    ):
        for at, (f, first) in enumerate(layers):
            target = place(cells, wide, wide_strip, f)
            for d in range(STEPS) if f >= FIELDS else (first,):
                y = ey - 1 - d if sign < 0 else ny + d
                value = halo[at] if f < FIELDS else layer_of_shared(halo[at], d)
                for x in range(nx):
                    target[STEPS + x, y : y + 1, 0:depth] = value[x : x + 1]
    for x in range(STEPS, STEPS + nx):
        spread_strip(cells, wide, wide_strip, x, 0, ey, range(FIELDS))
    inside = inside_mask(ey, ez)
    for step in range(1, STEPS):
        for x in range(STEPS + step - 1, STEPS + nx - step):
            advance_magnetic(cells, field, inside, step, x)
            if x >= STEPS + step:
                advance_electric(cells, wide, field, snaps, step, x)


def side_slabs(nx):
    for d in range(STEPS):
        fields = [f for f in range(FIELDS) if WIDTHS[f] > d]
        yield STEPS - 1 - d, fields
        yield STEPS + nx + d, fields


def sides_kernel(x_low, x_high, _cells, _wide, _strip, cells, wide, wide_strip):
    _, ny, depth = x_low.shape
    _, ex, ey, _ = cells.shape
    nx = ex - 2 * STEPS
    strips = wide_strip.shape[0]
    for halo, layers, sign in (
        (x_low, high_layers(strips), -1),
        (x_high, low_layers(0, strips), 1),
    ):
        for at, (f, first) in enumerate(layers):
            for d in range(STEPS) if f >= FIELDS else (first,):
                x = STEPS - 1 - d if sign < 0 else STEPS + nx + d
                value = halo[at] if f < FIELDS else layer_of_shared(halo[at], d)
                place(cells, wide, wide_strip, f)[x, 0:ny, 0:depth] = value
    for x, fields in side_slabs(nx):
        for f in (*fields, *range(FIELDS, FIELDS + strips)):
            target = place(cells, wide, wide_strip, f)
            target[x, ny:ey, :] = jnp.zeros((2 * STEPS, target.shape[2]), jnp.float32)
        spread_strip(cells, wide, wide_strip, x, 0, ny, fields)


def rolls(ey, ez):
    return (
        lambda v: pltpu.roll(v, ey - 1, 0),
        lambda v: pltpu.roll(v, ez - 1, 1),
        lambda v: pltpu.roll(v, 1, 0),
        lambda v: pltpu.roll(v, 1, 1),
    )


def inside_mask(ey, ez):
    row_at = lax.broadcasted_iota(jnp.int32, (ey, ez), 0)
    lane_at = lax.broadcasted_iota(jnp.int32, (ey, ez), 1)
    outside = ((row_at >= ey - STEPS) & (lax.axis_index("gy") == 0)) | (
        (lane_at >= ez - STEPS) & (lax.axis_index("gz") == 0)
    )
    return jnp.where(outside, 0.0, 1.0)


def advance_magnetic(cells, field, inside, step, x):
    _, _, ey, ez = cells.shape
    up_y, up_z, _, _ = rolls(ey, ez)
    e0, e1, e2 = cells[0, x], cells[1, x], cells[2, x]
    f1, f2 = cells[1, x + 1], cells[2, x + 1]
    curl = (
        (up_y(e2) - e2) - (up_z(e1) - e1),
        (up_z(e0) - e0) - (f2 - e2),
        (f1 - e1) - (up_y(e0) - e0),
    )
    mask = inside
    if x < STEPS:
        mask = inside * jnp.where(lax.axis_index("gx") == 0, 0.0, 1.0)
    for c in range(3):
        change = curl[c] * mask
        field[c, x] = field[c, x] + change if step > 1 else change


def backward_curl(field, x):
    _, _, ey, ez = field.shape
    _, _, down_y, down_z = rolls(ey, ez)
    m0, m1, m2 = field[0, x], field[1, x], field[2, x]
    l1, l2 = field[1, x - 1], field[2, x - 1]
    return (
        (m2 - down_y(m2)) - (m1 - down_z(m1)),
        (m0 - down_z(m0)) - (m2 - l2),
        (m1 - l1) - (m0 - down_y(m0)),
    )


def advance_electric(cells, wide, field, snaps, step, x):
    curl = backward_curl(field, x)
    old = [cells[c, x] for c in range(3)]
    if step == 2:
        gain = wide[7, x]
        source = [wide[4 + c, x] + gain * old[c] for c in range(3)]
        if STEPS - 2 < x < wide.shape[1] - STEPS + 1:
            ratio = wide[11, x]
            for c in range(3):
                wide[8 + c, x] = wide[8 + c, x] + ratio * old[c]
            square = old[0] * old[0] + old[1] * old[1] + old[2] * old[2]
            wide[12, x] = (
                wide[12, x]
                + (wide[13, x] * old[0] + wide[14, x] * old[1] + wide[15, x] * old[2])
                + wide[16, x] * square
            )
    elif step == 3:
        gain = wide[12, x]
        source = [wide[8 + c, x] + gain * old[c] for c in range(3)]
    else:
        source = [wide[1 + c, x] for c in range(3)]
    scale = wide[0, x]
    _, rows, depth = snaps.shape
    ny = cells.shape[2] - 2 * STEPS
    at = (x - STEPS) * ny
    for c in range(3):
        new = old[c] + scale * (curl[c] + source[c])
        cells[c, x] = new
        if 0 <= at < rows:
            snaps[(step - 1) * 3 + c, at : at + ny, :] = new[0:ny, 0:depth]


def steps_kernel(
    c_low, c_high, _cells, _wide, _field, _snaps, wide_strip, row_hot, depth_hot,
    arrived, states, cells, wide, field, snaps, result, changes,
):
    _, ex, ey, ez = wide.shape
    nx, ny, depth = ex - 2 * STEPS, ey - 2 * STEPS, ez // 2
    rows = nx * ny
    for corner, sign in ((c_low, -1), (c_high, 1)):
        for row, (f, d, side, e) in enumerate(corner_rows(sign, wide_strip.shape[0])):
            x = STEPS - 1 - d if sign < 0 else STEPS + nx + d
            y = ey - 1 - e if side < 0 else ny + e
            place(cells, wide, wide_strip, f)[x, y : y + 1, 0:depth] = corner[row : row + 1, :]
    for x, fields in side_slabs(nx):
        fields = [f for f in fields if WIDTHS[f] > 1]
        spread_strip(cells, wide, wide_strip, x, ny, 2 * STEPS, fields)
    inside = inside_mask(ey, ez)
    index = arrived[:, 12, :].astype(jnp.int32)
    constants = emitter_constants(arrived)
    current = [states[c] for c in range(3)]
    previous = [states[3 + c] for c in range(3)]
    upper = states[6]
    pumped = states[7]
    for step in range(1, STEPS + 1):
        if step > 1:
            own = [snaps[(step - 2) * 3 + c] for c in range(3)]
            sample = gather_cells(cell_halves(own), index, row_hot, depth)
            advanced, previous, upper, pumped = bloch_step(
                sample, current, previous, upper, pumped, constants
            )
            if step == STEPS:
                change = [
                    (a - c) * (1.0 / TIME_STEP**2) for a, c in zip(advanced, current)
                ]
            current = advanced
        if step < STEPS:
            done = range(STEPS + step, STEPS + nx - step)
            for x in range(step - 1, ex - step):
                if x not in done and x + 1 not in done:
                    advance_magnetic(cells, field, inside, step, x)
                if x not in done and x >= step:
                    advance_electric(cells, wide, field, snaps, step, x)
    for c in range(3):
        result[:, c, :] = current[c]
        result[:, 3 + c, :] = previous[c]
    result[:, 6, :] = upper
    result[:, 7, :] = pumped
    for c in range(3):
        changes[c] = change[c]


def last_kernel(cells, base, field, changes, row_hot, depth_hot, electric, magnetic):
    _, nx, ny, depth = electric.shape
    rows = nx * ny
    ey, ez = cells.shape[2:]
    sources = scatter_cells([changes[c] for c in range(3)], row_hot, depth_hot, rows)
    inside = inside_mask(ey, ez)
    advance_magnetic(cells, field, inside, STEPS, STEPS - 1)
    for x in range(STEPS, STEPS + nx):
        advance_magnetic(cells, field, inside, STEPS, x)
        curl = backward_curl(field, x)
        span = slice((x - STEPS) * ny, (x - STEPS + 1) * ny)
        scale = base[3, span]
        for c in range(3):
            own = curl[c][0:ny, 0:depth] + sources[c][span]
            electric[c, x - STEPS] = cells[c, x, 0:ny, 0:depth] + scale * own
            magnetic[c, x - STEPS] = field[c, x, 0:ny, 0:depth] * -TIME_STEP


def unpack_kernel(home, polar, popul):
    for i in range(2):
        for c in range(3):
            polar[i, c, 0] = home[:, 3 * i + c, :]
        popul[i, 0] = home[:, 6 + i, :]


def call(kernel, outs, final=(), aliases=None, limit=VMEM_LIMIT, cost=None):
    shapes = [pltpu.VMEM(s[:-1], s[-1]) if isinstance(s[-1], type) else pltpu.VMEM(s, jnp.float32) for s in outs]
    shapes += [jax.ShapeDtypeStruct(s, jnp.float32) for s in final]
    return pl.pallas_call(
        kernel,
        out_shape=shapes,
        input_output_aliases=aliases or {},
        cost_estimate=cost,
        compiler_params=pltpu.CompilerParams(vmem_limit_bytes=limit),
    )


def near(*values):
    return [pltpu.with_memory_space_constraint(v, pltpu.VMEM) for v in values]


def shifted(value, axis, step):
    count = lax.axis_size(axis)
    pairs = [(i, i + step) for i in range(count) if 0 <= i + step < count]
    return lax.ppermute(value, axis, pairs)


def shards(
    electric, permittivity_class, cell_index, polarization, populations,
    resonance, dephasing, coupling, pump_rate,
):
    _, nx, ny, depth = electric.shape
    rows = nx * ny
    _, buckets, slots = cell_index.shape
    ex, ey, ez = nx + 2 * STEPS, ny + 2 * STEPS, 2 * depth
    hots = [
        (FOLDS * rows, buckets * slots, jnp.bfloat16),
        (depth // FOLDS, buckets * slots, jnp.bfloat16),
    ]
    packed, base, left = near(
        *call(
            pack_kernel,
            [
                (buckets, 13, slots),
                (GRID, rows, depth),
                (6 * depth // FOLDS, FOLDS * rows, jnp.bfloat16),
            ],
            limit=HIGH_LIMIT,
        )(
            electric, permittivity_class, cell_index, polarization, populations,
            resonance, dephasing, coupling, pump_rate,
        )
    )
    arrived = lax.all_to_all(packed, ("gy", "gz"), split_axis=0, concat_axis=0, tiled=True)
    (arrived,) = near(arrived)
    strips = 1 if lax.axis_size("gz") == 2 else 2
    coefs, states, row_hot, depth_hot, *strip = near(
        *call(
            first_kernel,
            [
                (FIELDS - GRID, rows, depth),
                (8, buckets, slots),
                *hots,
                *[(1, rows, depth)] * strips,
            ],
        )(arrived, base, left)
    )
    if strips == 1:
        (strip,) = near(lax.ppermute(strip[0], "gz", [(0, 1), (1, 0)]))
    else:
        strip = near(shifted(strip[0], "gz", 1), shifted(strip[1], "gz", -1))
        (strip,) = near(*call(join_kernel, [(strips, rows, depth)])(*strip))
    high = len(high_layers(strips))
    faces = call(
        functools.partial(faces_kernel, nx, ny),
        [
            (len(low_layers(1, strips)), nx, depth),
            (high, nx, depth),
            (len(low_layers(0, strips)), ny, depth),
            (high, ny, depth),
        ],
    )(base, coefs, strip)
    y_low, y_high = near(shifted(faces[1], "gy", 1), shifted(faces[0], "gy", -1))
    x_low, x_high = near(shifted(faces[3], "gx", 1), shifted(faces[2], "gx", -1))
    low, high = call(
        functools.partial(corners_kernel, strips),
        [corner_shape(1, strips, depth), corner_shape(-1, strips, depth)],
        cost=LONG,
    )(y_low, y_high)
    c_low, c_high = near(shifted(high, "gx", 1), shifted(low, "gx", -1))
    state = near(
        *call(
            assemble_kernel,
            [
                (3, ex, ey, ez),
                (FIELDS - 3, ex, ey, ez),
                (strips, ex, ey, depth),
                (3, ex, ey, ez),
                (3 * (STEPS - 1), rows, depth),
            ],
        )(base, coefs, strip, y_low, y_high)
    )
    cells, wide, wide_strip, field, snaps = state
    cells, wide, wide_strip = near(
        *call(
            sides_kernel,
            [cells.shape, wide.shape, wide_strip.shape],
            aliases={2: 0, 3: 1, 4: 2},
        )(x_low, x_high, cells, wide, wide_strip)
    )
    cells, _, field, _, result, changes = near(
        *call(
            steps_kernel,
            [
                cells.shape,
                wide.shape,
                field.shape,
                snaps.shape,
                (buckets, 8, slots),
                (3, buckets, slots),
            ],
            aliases={2: 0, 3: 1, 4: 2, 5: 3},
        )(c_low, c_high, cells, wide, field, snaps, wide_strip, row_hot, depth_hot, arrived, states)
    )
    home = lax.all_to_all(result, ("gy", "gz"), split_axis=0, concat_axis=0, tiled=True)
    electric, magnetic = call(last_kernel, [], [electric.shape, electric.shape])(
        cells, base, field, changes, row_hot, depth_hot
    )
    polar_out, popul_out = call(unpack_kernel, [], [polarization.shape, populations.shape])(
        *near(home)
    )
    return (electric, magnetic, polar_out, popul_out)


def solution(mesh):
    owners = P("gx", ("gy", "gz"), None)
    return jax.shard_map(
        shards,
        mesh=mesh,
        in_specs=(
            P(None, "gx", "gy", "gz"),
            P("gx", "gy", "gz"),
            owners,
            P(None, None, "gx", ("gy", "gz"), None),
            P(None, "gx", ("gy", "gz"), None),
            owners,
            owners,
            owners,
            owners,
        ),
        out_specs=(
            P(None, "gx", "gy", "gz"),
            P(None, "gx", "gy", "gz"),
            P(None, None, "gx", ("gy", "gz"), None),
            P(None, "gx", ("gy", "gz"), None),
        ),
        check_vma=False,
    )
```

```python
import functools

import jax
import jax.numpy as jnp
from jax import lax
from jax.experimental import pallas as pl
from jax.experimental.pallas import tpu as pltpu
from jax.sharding import PartitionSpec as P

STEPS = 4
TIME_STEP = 0.5
PUMP_DECAY = 0.2
UPPER_DECAY = 0.02
WORK_SHARE = 0.05
CLASS_PERMITTIVITY = (1.0, 2.1, 6.0, 12.25)

WIDTHS = (STEPS,) * 3 + (STEPS - 1,) * 4 + (STEPS - 2,) * 4 + (STEPS - 3,) * 9
FIELDS = len(WIDTHS)
GRID = 4
VECTORS = (0, 4, 7, 11)
LANE_BASES = tuple(sum(WIDTHS[:i]) for i in range(FIELDS))
LAYER_LANES = tuple(sum(w for w in WIDTHS if w > d) for d in range(STEPS))
LAYER_BASES = tuple(sum(LAYER_LANES[:d]) for d in range(STEPS + 1))
FOLDS = 2
LONG = pl.CostEstimate(flops=20_000_000_000, bytes_accessed=100_000_000, transcendentals=0)
VMEM_LIMIT = 24 * 1024 * 1024
HIGH_LIMIT = 56 * 1024 * 1024


def layer_list(skip_axis, strips):
    layers = []
    for f, width in enumerate(WIDTHS):
        unused = skip_axis is not None and f - skip_axis in VECTORS
        layers += [(f, d) for d in range(width - 1 if unused else width)]
    return layers + [(FIELDS + i, 0) for i in range(strips)]


def low_layers(axis, strips):
    return layer_list(axis, strips)


def high_layers(strips):
    return layer_list(None, strips)


def corner_rows(halo_sign, strips):
    out = []
    furthest = 0 if halo_sign < 0 else 1
    known_x = high_layers(0) if halo_sign < 0 else low_layers(0, 0)
    for f, width in enumerate(WIDTHS + (STEPS,) * strips):
        for d in range(width):
            if f < FIELDS and (f, d) not in known_x:
                continue
            for side in (-1, 1):
                reach = width - d
                if f >= FIELDS or side == halo_sign or any(
                    f in (v, v + 1, v + 2) and f != v + furthest for v in VECTORS
                ):
                    reach -= 1
                known = high_layers(0) if side < 0 else low_layers(1, 0)
                out += [
                    (f, d, side, e)
                    for e in range(reach)
                    if f >= FIELDS or (f, e) in known
                ]
    return out


def corner_shape(halo_sign, strips, depth):
    return (-(-len(corner_rows(halo_sign, strips)) // 8) * 8, depth)


def share_lanes(layers):
    lane = lax.broadcasted_iota(jnp.int32, layers[0].shape, 1)
    out = layers[0]
    for d in range(1, STEPS):
        turned = pltpu.roll(layers[d], LAYER_BASES[d], 1)
        out = jnp.where(lane >= LAYER_BASES[d], turned, out)
    return out


def layer_of_shared(shared, d):
    depth = shared.shape[1]
    return pltpu.roll(shared, depth - LAYER_BASES[d], 1) if d else shared


def inverse_permittivity(classes):
    inverse = jnp.zeros(classes.shape, jnp.float32)
    for number, epsilon in enumerate(CLASS_PERMITTIVITY):
        inverse = jnp.where(classes == number, 1.0 / epsilon, inverse)
    return inverse


def halves(value):
    high = value.astype(jnp.bfloat16)
    low = (value - high.astype(jnp.float32)).astype(jnp.bfloat16)
    return high, low


def write_one_hots(index, row_hot, depth_hot, rows, depth):
    fold = depth // FOLDS
    shift = depth.bit_length() - 1
    buckets, slots = index.shape
    live = index < rows * depth
    part = lax.shift_right_logical(lax.bitwise_and(index, depth - 1), fold.bit_length() - 1)
    row = lax.shift_right_logical(index, shift) + part * rows
    row = jnp.where(live, row, -1)
    deep = lax.bitwise_and(index, fold - 1)
    rows_at = lax.broadcasted_iota(jnp.int32, (FOLDS * rows, slots), 0)
    deep_at = lax.broadcasted_iota(jnp.int32, (fold, slots), 0)
    for b in range(buckets):
        span = slice(b * slots, (b + 1) * slots)
        row_hot[:, span] = jnp.where(rows_at == row[b : b + 1], 1.0, 0.0).astype(jnp.bfloat16)
        depth_hot[:, span] = jnp.where(deep_at == deep[b : b + 1], 1.0, 0.0).astype(jnp.bfloat16)


def cell_halves(cells):
    parts = []
    for block in cells:
        turned = block.T
        fold = turned.shape[0] // FOLDS
        turned = [turned[i * fold : (i + 1) * fold] for i in range(FOLDS)]
        parts += halves(jnp.concatenate(turned, axis=1))
    return jnp.concatenate(parts, axis=0)


def gather_cells(left, index, row_hot, depth):
    buckets, slots = index.shape
    fold = depth // FOLDS
    size = 2 * fold
    samples = [[], [], []]
    group = 2 if buckets % 2 == 0 else 1
    place_at = lax.broadcasted_iota(jnp.int32, (size, slots), 0)
    place_at = lax.bitwise_and(place_at, fold - 1)
    for start in range(0, buckets, group):
        span = slice(start * slots, (start + group) * slots)
        picked = jnp.dot(left, row_hot[:, span], preferred_element_type=jnp.float32)
        for b in range(start, start + group):
            hit = place_at == lax.bitwise_and(index[b : b + 1], fold - 1)
            lanes = slice((b - start) * slots, (b - start + 1) * slots)
            for c in range(3):
                part = picked[c * size : (c + 1) * size, lanes]
                samples[c].append(jnp.sum(jnp.where(hit, part, 0.0), axis=0, keepdims=True))
    return [jnp.concatenate(rows, axis=0) for rows in samples]


def flat_row(value):
    buckets = value.shape[0]
    return jnp.concatenate([value[b : b + 1] for b in range(buckets)], axis=1)


def scatter_cells(values, row_hot, depth_hot, rows, group=4):
    hot = row_hot[...]
    deep = depth_hot[...]
    fold = deep.shape[0]
    out = []
    for start in range(0, len(values), group):
        some = [halves(flat_row(value)) for value in values[start : start + group]]
        total = 0.0
        for part in range(2):
            spread = jnp.concatenate([deep * pair[part] for pair in some], axis=0)
            total = total + lax.dot_general(
                spread, hot, (((1,), (1,)), ((), ())), preferred_element_type=jnp.float32
            )
        for i in range(len(some)):
            block = total[i * fold : (i + 1) * fold]
            block = [block[:, j * rows : (j + 1) * rows] for j in range(FOLDS)]
            out.append(jnp.concatenate(block, axis=0).T)
    return out


def emitter_constants(arrived):
    freq, dephase, strength, pumping = [arrived[:, f, :] for f in range(8, 12)]
    damping = 0.5 * TIME_STEP * dephase
    stiffness = freq * TIME_STEP * (freq * TIME_STEP)
    scale = 1.0 + damping
    keep = (2.0 - stiffness) / scale
    back = (1.0 - damping) / scale
    drive = strength * (TIME_STEP * TIME_STEP) / scale
    share = WORK_SHARE / freq
    return keep, back, drive, share, pumping


def bloch_step(sample, current, previous, upper, pumped, constants):
    keep, back, drive, share, pumping = constants
    lower = 1.0 - upper - pumped
    push = drive * (lower - upper)
    advanced = [keep * c - back * p + push * s for c, p, s in zip(current, previous, sample)]
    work = sum(s * (a - p) for s, a, p in zip(sample, advanced, previous)) / (2.0 * TIME_STEP)
    pumped_next = pumped + TIME_STEP * (pumping * lower - PUMP_DECAY * pumped)
    upper_next = upper + TIME_STEP * (
        PUMP_DECAY * pumped - UPPER_DECAY * upper + share * work
    )
    return advanced, current, upper_next, pumped_next


def pack_kernel(
    electric, classes, index, polar, popul, freq, dephase, strength, pumping, out, base, left
):
    for i in range(2):
        for c in range(3):
            out[:, 3 * i + c, :] = polar[i, c, 0]
    for i in range(2):
        out[:, 6 + i, :] = popul[i, 0]
    for f, source in enumerate((freq, dephase, strength, pumping)):
        out[:, 8 + f, :] = source[0]
    out[:, 12, :] = index[0].astype(jnp.float32)
    _, nx, ny, depth = electric.shape
    rows = nx * ny
    for c in range(3):
        base[c] = electric[c].reshape(rows, depth)
    base[3] = inverse_permittivity(classes[...].reshape(rows, depth)) * -(TIME_STEP**2)
    left[...] = cell_halves([base[c] for c in range(3)])


def source_of(base, coefs, strip, f):
    if f < GRID:
        return base.at[f]
    return coefs.at[f - GRID] if f < FIELDS else strip.at[f - FIELDS]


def first_kernel(arrived, base, left, coefs, states, row_hot, depth_hot, *strip):
    _, rows, depth = base.shape
    index = arrived[:, 12, :].astype(jnp.int32)
    write_one_hots(index, row_hot, depth_hot, rows, depth)
    sample = gather_cells(left[...], index, row_hot, depth)
    constants = emitter_constants(arrived)
    keep, back, drive, share, pumping = constants
    start = [arrived[:, c, :] for c in range(3)]
    before = [arrived[:, 3 + c, :] for c in range(3)]
    now, _, upper, pumped = bloch_step(
        sample, start, before, arrived[:, 6, :], arrived[:, 7, :], constants
    )
    for c in range(3):
        states[c] = now[c]
        states[3 + c] = start[c]
    states[6] = upper
    states[7] = pumped
    lower = 1.0 - upper - pumped
    push = drive * (lower - upper)
    pumped_after = pumped + TIME_STEP * (pumping * lower - PUMP_DECAY * pumped)
    upper_free = upper + TIME_STEP * (PUMP_DECAY * pumped - UPPER_DECAY * upper)
    free = [keep * n - back * s for n, s in zip(now, start)]
    values = [n - s for n, s in zip(now, start)]
    values += [f - n for f, n in zip(free, now)]
    values.append(push)
    values += [(keep - 1.0) * f - back * n for f, n in zip(free, now)]
    values.append((keep - 1.0) * push)
    values.append(drive * (1.0 - pumped_after - 2.0 * upper_free))
    values += [-drive * share * (f - s) for f, s in zip(free, start)]
    values.append(-drive * share * push)
    values = [value * (1.0 / TIME_STEP**2) for value in values]
    for number, block in enumerate(scatter_cells(values, row_hot, depth_hot, rows)):
        coefs[number] = block
    lane = lax.broadcasted_iota(jnp.int32, (rows, depth), 1)
    strips = len(strip)
    for i in range(strips):
        top = 1 - i if strips > 1 else jnp.where(lax.axis_index("gz") == 0, 1, 0)
        packed = jnp.zeros((rows, depth), jnp.float32)
        for f, width in enumerate(WIDTHS):
            at = LANE_BASES[f]
            turned = pltpu.roll(source_of(base, coefs, None, f)[...], at + width * top, 1)
            packed = jnp.where((lane >= at) & (lane < at + width), turned, packed)
        strip[i][0] = packed


def join_kernel(first, second, out):
    out[0] = first[0]
    out[1] = second[0]


def faces_kernel(nx, ny, base, coefs, strip, y_low, y_high, x_low, x_high):
    strips = strip.shape[0]
    for face, layers, sign, axis in (
        (y_low, low_layers(1, strips), -1, 1),
        (y_high, high_layers(strips), 1, 1),
        (x_low, low_layers(0, strips), -1, 0),
        (x_high, high_layers(strips), 1, 0),
    ):

        def layer(f, d):
            source = source_of(base, coefs, strip, f)
            at = d if sign < 0 else (nx, ny)[axis] - 1 - d
            if axis == 1:
                return source[pl.ds(at, nx, stride=ny), :]
            return source[at * ny : (at + 1) * ny, :]

        for at, (f, d) in enumerate(layers):
            count = nx if axis == 1 else ny
            if f < FIELDS:
                value = layer(f, d)
            else:
                value = share_lanes([layer(f, i) for i in range(STEPS)])
            face[at * count : (at + 1) * count, :] = value


def corners_kernel(nx, strips, halo_low, halo_high, low, high):
    for face, sign in ((low, -1), (high, 1)):
        for row, (f, d, side, e) in enumerate(corner_rows(-sign, strips)):
            x = d if sign < 0 else nx - 1 - d
            halo = halo_low if side < 0 else halo_high
            layers = high_layers(strips) if side < 0 else low_layers(1, strips)
            at = layers.index((f, e if f < FIELDS else 0))
            value = halo[at * nx + x : at * nx + x + 1, :]
            face[row : row + 1, :] = value if f < FIELDS else layer_of_shared(value, e)


def place(cells, wide, wide_strip, f):
    if f < 3:
        return cells.at[f]
    return wide.at[f - 3] if f < FIELDS else wide_strip.at[f - FIELDS]


def spread_strip(cells, wide, wide_strip, x, y, count, fields):
    strips, _, _, depth = wide_strip.shape
    values = [wide_strip[i, x, y : y + count] for i in range(strips)]
    upper = lax.broadcasted_iota(jnp.int32, (count, depth), 1) >= depth // 2
    low = lax.axis_index("gz") > 0
    for f in fields:
        at, width = LANE_BASES[f], WIDTHS[f]
        if strips == 1:
            shift = lax.bitwise_and(depth - at - jnp.where(low, width, 0), depth - 1)
            value = pltpu.roll(values[0], shift, 1)
            if f < GRID:
                value = jnp.where(upper == low, value, 0.0)
        else:
            value = jnp.where(
                upper,
                pltpu.roll(values[0], (depth - at - width) % depth, 1),
                pltpu.roll(values[1], (depth - at) % depth, 1),
            )
        place(cells, wide, wide_strip, f)[x, y : y + count, depth : 2 * depth] = value


def assemble_kernel(
    base, coefs, strip, y_low, y_high, cells, wide, wide_strip, field, snaps
):
    _, ex, ey, ez = cells.shape
    nx, ny, depth = ex - 2 * STEPS, ey - 2 * STEPS, ez // 2
    strips = strip.shape[0]
    for f in range(FIELDS + strips):
        source = source_of(base, coefs, strip, f)
        target = place(cells, wide, wide_strip, f)
        target[STEPS : STEPS + nx, 0:ny, 0:depth] = source[...].reshape(nx, ny, depth)
        target[STEPS : STEPS + nx, ny:ey, 0:depth] = jnp.zeros((nx, 2 * STEPS, depth), jnp.float32)
    for halo, layers, sign in (
        (y_low, high_layers(strips), -1),
        (y_high, low_layers(1, strips), 1),
    ):
        for at, (f, first) in enumerate(layers):
            target = place(cells, wide, wide_strip, f)
            rows = halo[at * nx : (at + 1) * nx, :]
            for d in range(STEPS) if f >= FIELDS else (first,):
                y = ey - 1 - d if sign < 0 else ny + d
                value = rows if f < FIELDS else layer_of_shared(rows, d)
                for x in range(nx):
                    target[STEPS + x, y : y + 1, 0:depth] = value[x : x + 1]
    for x in range(STEPS, STEPS + nx):
        spread_strip(cells, wide, wide_strip, x, 0, ey, range(FIELDS))
    inside = inside_mask(ey, ez)
    for step in range(1, STEPS):
        for x in range(STEPS + step - 1, STEPS + nx - step):
            advance_magnetic(cells, field, inside, step, x)
            if x >= STEPS + step:
                advance_electric(cells, wide, field, snaps, step, x)


def side_slabs(nx):
    for d in range(STEPS):
        fields = [f for f in range(FIELDS) if WIDTHS[f] > d]
        yield STEPS - 1 - d, fields
        yield STEPS + nx + d, fields


def sides_kernel(x_low, x_high, _cells, _wide, _strip, cells, wide, wide_strip):
    _, ex, ey, ez = cells.shape
    nx, ny, depth = ex - 2 * STEPS, ey - 2 * STEPS, ez // 2
    strips = wide_strip.shape[0]
    for halo, layers, sign in (
        (x_low, high_layers(strips), -1),
        (x_high, low_layers(0, strips), 1),
    ):
        for at, (f, first) in enumerate(layers):
            rows = halo[at * ny : (at + 1) * ny, :]
            for d in range(STEPS) if f >= FIELDS else (first,):
                x = STEPS - 1 - d if sign < 0 else STEPS + nx + d
                value = rows if f < FIELDS else layer_of_shared(rows, d)
                place(cells, wide, wide_strip, f)[x, 0:ny, 0:depth] = value
    for x, fields in side_slabs(nx):
        for f in (*fields, *range(FIELDS, FIELDS + strips)):
            target = place(cells, wide, wide_strip, f)
            target[x, ny:ey, :] = jnp.zeros((2 * STEPS, target.shape[2]), jnp.float32)
        spread_strip(cells, wide, wide_strip, x, 0, ny, fields)


def rolls(ey, ez):
    return (
        lambda v: pltpu.roll(v, ey - 1, 0),
        lambda v: pltpu.roll(v, ez - 1, 1),
        lambda v: pltpu.roll(v, 1, 0),
        lambda v: pltpu.roll(v, 1, 1),
    )


def inside_mask(ey, ez):
    row_at = lax.broadcasted_iota(jnp.int32, (ey, ez), 0)
    lane_at = lax.broadcasted_iota(jnp.int32, (ey, ez), 1)
    outside = ((row_at >= ey - STEPS) & (lax.axis_index("gy") == 0)) | (
        (lane_at >= ez - STEPS) & (lax.axis_index("gz") == 0)
    )
    return jnp.where(outside, 0.0, 1.0)


def advance_magnetic(cells, field, inside, step, x):
    _, _, ey, ez = cells.shape
    up_y, up_z, _, _ = rolls(ey, ez)
    e0, e1, e2 = cells[0, x], cells[1, x], cells[2, x]
    f1, f2 = cells[1, x + 1], cells[2, x + 1]
    curl = (
        (up_y(e2) - e2) - (up_z(e1) - e1),
        (up_z(e0) - e0) - (f2 - e2),
        (f1 - e1) - (up_y(e0) - e0),
    )
    mask = inside
    if x < STEPS:
        mask = inside * jnp.where(lax.axis_index("gx") == 0, 0.0, 1.0)
    for c in range(3):
        change = curl[c] * mask
        field[c, x] = field[c, x] + change if step > 1 else change


def backward_curl(field, x):
    _, _, ey, ez = field.shape
    _, _, down_y, down_z = rolls(ey, ez)
    m0, m1, m2 = field[0, x], field[1, x], field[2, x]
    l1, l2 = field[1, x - 1], field[2, x - 1]
    return (
        (m2 - down_y(m2)) - (m1 - down_z(m1)),
        (m0 - down_z(m0)) - (m2 - l2),
        (m1 - l1) - (m0 - down_y(m0)),
    )


def advance_electric(cells, wide, field, snaps, step, x):
    curl = backward_curl(field, x)
    old = [cells[c, x] for c in range(3)]
    if step == 2:
        gain = wide[7, x]
        source = [wide[4 + c, x] + gain * old[c] for c in range(3)]
        if STEPS - 2 < x < wide.shape[1] - STEPS + 1:
            ratio = wide[11, x]
            for c in range(3):
                wide[8 + c, x] = wide[8 + c, x] + ratio * old[c]
            square = old[0] * old[0] + old[1] * old[1] + old[2] * old[2]
            wide[12, x] = (
                wide[12, x]
                + (wide[13, x] * old[0] + wide[14, x] * old[1] + wide[15, x] * old[2])
                + wide[16, x] * square
            )
    elif step == 3:
        gain = wide[12, x]
        source = [wide[8 + c, x] + gain * old[c] for c in range(3)]
    else:
        source = [wide[1 + c, x] for c in range(3)]
    scale = wide[0, x]
    _, rows, depth = snaps.shape
    ny = cells.shape[2] - 2 * STEPS
    at = (x - STEPS) * ny
    for c in range(3):
        new = old[c] + scale * (curl[c] + source[c])
        cells[c, x] = new
        if 0 <= at < rows:
            snaps[(step - 1) * 3 + c, at : at + ny, :] = new[0:ny, 0:depth]


def steps_kernel(
    c_low, c_high, _cells, _wide, _field, _snaps, wide_strip, row_hot, depth_hot,
    arrived, states, cells, wide, field, snaps, result, changes,
):
    _, ex, ey, ez = wide.shape
    nx, ny, depth = ex - 2 * STEPS, ey - 2 * STEPS, ez // 2
    rows = nx * ny
    for corner, sign in ((c_low, -1), (c_high, 1)):
        for row, (f, d, side, e) in enumerate(corner_rows(sign, wide_strip.shape[0])):
            x = STEPS - 1 - d if sign < 0 else STEPS + nx + d
            y = ey - 1 - e if side < 0 else ny + e
            place(cells, wide, wide_strip, f)[x, y : y + 1, 0:depth] = corner[row : row + 1, :]
    for x, fields in side_slabs(nx):
        fields = [f for f in fields if WIDTHS[f] > 1]
        spread_strip(cells, wide, wide_strip, x, ny, 2 * STEPS, fields)
    inside = inside_mask(ey, ez)
    index = arrived[:, 12, :].astype(jnp.int32)
    constants = emitter_constants(arrived)
    current = [states[c] for c in range(3)]
    previous = [states[3 + c] for c in range(3)]
    upper = states[6]
    pumped = states[7]
    for step in range(1, STEPS + 1):
        if step > 1:
            own = [snaps[(step - 2) * 3 + c] for c in range(3)]
            sample = gather_cells(cell_halves(own), index, row_hot, depth)
            advanced, previous, upper, pumped = bloch_step(
                sample, current, previous, upper, pumped, constants
            )
            if step == STEPS:
                change = [
                    (a - c) * (1.0 / TIME_STEP**2) for a, c in zip(advanced, current)
                ]
            current = advanced
        if step < STEPS:
            done = range(STEPS + step, STEPS + nx - step)
            for x in range(step - 1, ex - step):
                if x not in done and x + 1 not in done:
                    advance_magnetic(cells, field, inside, step, x)
                if x not in done and x >= step:
                    advance_electric(cells, wide, field, snaps, step, x)
    for c in range(3):
        result[:, c, :] = current[c]
        result[:, 3 + c, :] = previous[c]
    result[:, 6, :] = upper
    result[:, 7, :] = pumped
    for c in range(3):
        changes[c] = change[c]


def last_kernel(cells, base, field, changes, row_hot, depth_hot, electric, magnetic):
    _, nx, ny, depth = electric.shape
    rows = nx * ny
    ey, ez = cells.shape[2:]
    sources = scatter_cells([changes[c] for c in range(3)], row_hot, depth_hot, rows)
    inside = inside_mask(ey, ez)
    advance_magnetic(cells, field, inside, STEPS, STEPS - 1)
    for x in range(STEPS, STEPS + nx):
        advance_magnetic(cells, field, inside, STEPS, x)
        curl = backward_curl(field, x)
        span = slice((x - STEPS) * ny, (x - STEPS + 1) * ny)
        scale = base[3, span]
        for c in range(3):
            own = curl[c][0:ny, 0:depth] + sources[c][span]
            electric[c, x - STEPS] = cells[c, x, 0:ny, 0:depth] + scale * own
            magnetic[c, x - STEPS] = field[c, x, 0:ny, 0:depth] * -TIME_STEP


def unpack_kernel(home, polar, popul):
    for i in range(2):
        for c in range(3):
            polar[i, c, 0] = home[:, 3 * i + c, :]
        popul[i, 0] = home[:, 6 + i, :]


def call(kernel, outs, final=(), aliases=None, limit=VMEM_LIMIT, cost=None):
    shapes = [pltpu.VMEM(s[:-1], s[-1]) if isinstance(s[-1], type) else pltpu.VMEM(s, jnp.float32) for s in outs]
    shapes += [jax.ShapeDtypeStruct(s, jnp.float32) for s in final]
    return pl.pallas_call(
        kernel,
        out_shape=shapes,
        input_output_aliases=aliases or {},
        cost_estimate=cost,
        compiler_params=pltpu.CompilerParams(vmem_limit_bytes=limit),
    )


def near(*values):
    return [pltpu.with_memory_space_constraint(v, pltpu.VMEM) for v in values]


def shifted(value, axis, step):
    count = lax.axis_size(axis)
    pairs = [(i, i + step) for i in range(count) if 0 <= i + step < count]
    return lax.ppermute(value, axis, pairs)


def shards(
    electric, permittivity_class, cell_index, polarization, populations,
    resonance, dephasing, coupling, pump_rate,
):
    _, nx, ny, depth = electric.shape
    rows = nx * ny
    _, buckets, slots = cell_index.shape
    ex, ey, ez = nx + 2 * STEPS, ny + 2 * STEPS, 2 * depth
    hots = [
        (FOLDS * rows, buckets * slots, jnp.bfloat16),
        (depth // FOLDS, buckets * slots, jnp.bfloat16),
    ]
    packed, base, left = near(
        *call(
            pack_kernel,
            [
                (buckets, 13, slots),
                (GRID, rows, depth),
                (6 * depth // FOLDS, FOLDS * rows, jnp.bfloat16),
            ],
            limit=HIGH_LIMIT,
        )(
            electric, permittivity_class, cell_index, polarization, populations,
            resonance, dephasing, coupling, pump_rate,
        )
    )
    arrived = lax.all_to_all(packed, ("gy", "gz"), split_axis=0, concat_axis=0, tiled=True)
    (arrived,) = near(arrived)
    strips = 1 if lax.axis_size("gz") == 2 else 2
    coefs, states, row_hot, depth_hot, *strip = near(
        *call(
            first_kernel,
            [
                (FIELDS - GRID, rows, depth),
                (8, buckets, slots),
                *hots,
                *[(1, rows, depth)] * strips,
            ],
        )(arrived, base, left)
    )
    if strips == 1:
        (strip,) = near(lax.ppermute(strip[0], "gz", [(0, 1), (1, 0)]))
    else:
        strip = near(shifted(strip[0], "gz", 1), shifted(strip[1], "gz", -1))
        (strip,) = near(*call(join_kernel, [(strips, rows, depth)])(*strip))
    high = len(high_layers(strips))
    faces = call(
        functools.partial(faces_kernel, nx, ny),
        [
            (len(low_layers(1, strips)) * nx, depth),
            (high * nx, depth),
            (len(low_layers(0, strips)) * ny, depth),
            (high * ny, depth),
        ],
    )(base, coefs, strip)
    y_low, y_high = near(shifted(faces[1], "gy", 1), shifted(faces[0], "gy", -1))
    x_low, x_high = near(shifted(faces[3], "gx", 1), shifted(faces[2], "gx", -1))
    low, high = call(
        functools.partial(corners_kernel, nx, strips),
        [corner_shape(1, strips, depth), corner_shape(-1, strips, depth)],
        cost=LONG,
    )(y_low, y_high)
    c_low, c_high = near(shifted(high, "gx", 1), shifted(low, "gx", -1))
    state = near(
        *call(
            assemble_kernel,
            [
                (3, ex, ey, ez),
                (FIELDS - 3, ex, ey, ez),
                (strips, ex, ey, depth),
                (3, ex, ey, ez),
                (3 * (STEPS - 1), rows, depth),
            ],
        )(base, coefs, strip, y_low, y_high)
    )
    cells, wide, wide_strip, field, snaps = state
    cells, wide, wide_strip = near(
        *call(
            sides_kernel,
            [cells.shape, wide.shape, wide_strip.shape],
            aliases={2: 0, 3: 1, 4: 2},
        )(x_low, x_high, cells, wide, wide_strip)
    )
    cells, _, field, _, result, changes = near(
        *call(
            steps_kernel,
            [
                cells.shape,
                wide.shape,
                field.shape,
                snaps.shape,
                (buckets, 8, slots),
                (3, buckets, slots),
            ],
            aliases={2: 0, 3: 1, 4: 2, 5: 3},
        )(c_low, c_high, cells, wide, field, snaps, wide_strip, row_hot, depth_hot, arrived, states)
    )
    home = lax.all_to_all(result, ("gy", "gz"), split_axis=0, concat_axis=0, tiled=True)
    electric, magnetic = call(last_kernel, [], [electric.shape, electric.shape])(
        cells, base, field, changes, row_hot, depth_hot
    )
    polar_out, popul_out = call(unpack_kernel, [], [polarization.shape, populations.shape])(
        *near(home)
    )
    return (electric, magnetic, polar_out, popul_out)


def solution(mesh):
    owners = P("gx", ("gy", "gz"), None)
    return jax.shard_map(
        shards,
        mesh=mesh,
        in_specs=(
            P(None, "gx", "gy", "gz"),
            P("gx", "gy", "gz"),
            owners,
            P(None, None, "gx", ("gy", "gz"), None),
            P(None, "gx", ("gy", "gz"), None),
            owners,
            owners,
            owners,
            owners,
        ),
        out_specs=(
            P(None, "gx", "gy", "gz"),
            P(None, "gx", "gy", "gz"),
            P(None, None, "gx", ("gy", "gz"), None),
            P(None, "gx", ("gy", "gz"), None),
        ),
        check_vma=False,
    )
```

```python
import functools

import jax
import jax.numpy as jnp
from jax import lax
from jax.experimental import pallas as pl
from jax.experimental.pallas import tpu as pltpu
from jax.sharding import PartitionSpec as P

STEPS = 4
TIME_STEP = 0.5
PUMP_DECAY = 0.2
UPPER_DECAY = 0.02
WORK_SHARE = 0.05
CLASS_PERMITTIVITY = (1.0, 2.1, 6.0, 12.25)

WIDTHS = (STEPS,) * 3 + (STEPS - 1,) * 4 + (STEPS - 2,) * 4 + (STEPS - 3,) * 9
FIELDS = len(WIDTHS)
GRID = 4
VECTORS = (0, 4, 7, 11)
LANE_BASES = tuple(sum(WIDTHS[:i]) for i in range(FIELDS))
LAYER_LANES = tuple(sum(w for w in WIDTHS if w > d) for d in range(STEPS))
LAYER_BASES = tuple(sum(LAYER_LANES[:d]) for d in range(STEPS + 1))
FOLDS = 2
LONG = pl.CostEstimate(flops=20_000_000_000, bytes_accessed=100_000_000, transcendentals=0)
VMEM_LIMIT = 24 * 1024 * 1024
HIGH_LIMIT = 56 * 1024 * 1024


def layer_list(skip_axis, strips):
    layers = []
    for f, width in enumerate(WIDTHS):
        unused = skip_axis is not None and f - skip_axis in VECTORS
        layers += [(f, d) for d in range(width - 1 if unused else width)]
    return layers + [(FIELDS + i, 0) for i in range(strips)]


def low_layers(axis, strips):
    return layer_list(axis, strips)


def high_layers(strips):
    return layer_list(None, strips)


def corner_rows(halo_sign, strips):
    out = []
    furthest = 0 if halo_sign < 0 else 1
    known_x = high_layers(0) if halo_sign < 0 else low_layers(0, 0)
    for f, width in enumerate(WIDTHS + (STEPS,) * strips):
        for d in range(width):
            if f < FIELDS and (f, d) not in known_x:
                continue
            for side in (-1, 1):
                reach = width - d
                if f >= FIELDS or side == halo_sign or any(
                    f in (v, v + 1, v + 2) and f != v + furthest for v in VECTORS
                ):
                    reach -= 1
                known = high_layers(0) if side < 0 else low_layers(1, 0)
                out += [
                    (f, d, side, e)
                    for e in range(reach)
                    if f >= FIELDS or (f, e) in known
                ]
    return out


def corner_shape(halo_sign, strips, depth):
    return (-(-len(corner_rows(halo_sign, strips)) // 8) * 8, depth)


def share_lanes(layers):
    lane = lax.broadcasted_iota(jnp.int32, layers[0].shape, 1)
    out = layers[0]
    for d in range(1, STEPS):
        turned = pltpu.roll(layers[d], LAYER_BASES[d], 1)
        out = jnp.where(lane >= LAYER_BASES[d], turned, out)
    return out


def layer_of_shared(shared, d):
    depth = shared.shape[1]
    return pltpu.roll(shared, depth - LAYER_BASES[d], 1) if d else shared


def inverse_permittivity(classes):
    inverse = jnp.zeros(classes.shape, jnp.float32)
    for number, epsilon in enumerate(CLASS_PERMITTIVITY):
        inverse = jnp.where(classes == number, 1.0 / epsilon, inverse)
    return inverse


def halves(value):
    high = value.astype(jnp.bfloat16)
    low = (value - high.astype(jnp.float32)).astype(jnp.bfloat16)
    return high, low


def write_one_hots(index, row_hot, depth_hot, rows, depth):
    fold = depth // FOLDS
    shift = depth.bit_length() - 1
    buckets, slots = index.shape
    live = index < rows * depth
    part = lax.shift_right_logical(lax.bitwise_and(index, depth - 1), fold.bit_length() - 1)
    row = lax.shift_right_logical(index, shift) + part * rows
    row = jnp.where(live, row, -1)
    deep = lax.bitwise_and(index, fold - 1)
    rows_at = lax.broadcasted_iota(jnp.int32, (FOLDS * rows, slots), 0)
    deep_at = lax.broadcasted_iota(jnp.int32, (fold, slots), 0)
    for b in range(buckets):
        span = slice(b * slots, (b + 1) * slots)
        row_hot[:, span] = jnp.where(rows_at == row[b : b + 1], 1.0, 0.0).astype(jnp.bfloat16)
        depth_hot[:, span] = jnp.where(deep_at == deep[b : b + 1], 1.0, 0.0).astype(jnp.bfloat16)


def cell_halves(cells):
    parts = []
    for block in cells:
        turned = block.T
        fold = turned.shape[0] // FOLDS
        turned = [turned[i * fold : (i + 1) * fold] for i in range(FOLDS)]
        parts += halves(jnp.concatenate(turned, axis=1))
    return jnp.concatenate(parts, axis=0)


def gather_cells(left, index, row_hot, depth):
    buckets, slots = index.shape
    fold = depth // FOLDS
    size = 2 * fold
    samples = [[], [], []]
    group = 2 if buckets % 2 == 0 else 1
    place_at = lax.broadcasted_iota(jnp.int32, (size, slots), 0)
    place_at = lax.bitwise_and(place_at, fold - 1)
    for start in range(0, buckets, group):
        span = slice(start * slots, (start + group) * slots)
        picked = jnp.dot(left, row_hot[:, span], preferred_element_type=jnp.float32)
        for b in range(start, start + group):
            hit = place_at == lax.bitwise_and(index[b : b + 1], fold - 1)
            lanes = slice((b - start) * slots, (b - start + 1) * slots)
            for c in range(3):
                part = picked[c * size : (c + 1) * size, lanes]
                samples[c].append(jnp.sum(jnp.where(hit, part, 0.0), axis=0, keepdims=True))
    return [jnp.concatenate(rows, axis=0) for rows in samples]


def flat_row(value):
    buckets = value.shape[0]
    return jnp.concatenate([value[b : b + 1] for b in range(buckets)], axis=1)


def scatter_cells(values, row_hot, depth_hot, rows, group=4):
    hot = row_hot[...]
    deep = depth_hot[...]
    fold = deep.shape[0]
    out = []
    for start in range(0, len(values), group):
        some = [halves(flat_row(value)) for value in values[start : start + group]]
        total = 0.0
        for part in range(2):
            spread = jnp.concatenate([deep * pair[part] for pair in some], axis=0)
            total = total + lax.dot_general(
                spread, hot, (((1,), (1,)), ((), ())), preferred_element_type=jnp.float32
            )
        for i in range(len(some)):
            block = total[i * fold : (i + 1) * fold]
            block = [block[:, j * rows : (j + 1) * rows] for j in range(FOLDS)]
            out.append(jnp.concatenate(block, axis=0).T)
    return out


def emitter_constants(arrived):
    freq, dephase, strength, pumping = [arrived[:, f, :] for f in range(8, 12)]
    damping = 0.5 * TIME_STEP * dephase
    stiffness = freq * TIME_STEP * (freq * TIME_STEP)
    scale = 1.0 + damping
    keep = (2.0 - stiffness) / scale
    back = (1.0 - damping) / scale
    drive = strength * (TIME_STEP * TIME_STEP) / scale
    share = WORK_SHARE / freq
    return keep, back, drive, share, pumping


def bloch_step(sample, current, previous, upper, pumped, constants):
    keep, back, drive, share, pumping = constants
    lower = 1.0 - upper - pumped
    push = drive * (lower - upper)
    advanced = [keep * c - back * p + push * s for c, p, s in zip(current, previous, sample)]
    work = sum(s * (a - p) for s, a, p in zip(sample, advanced, previous)) / (2.0 * TIME_STEP)
    pumped_next = pumped + TIME_STEP * (pumping * lower - PUMP_DECAY * pumped)
    upper_next = upper + TIME_STEP * (
        PUMP_DECAY * pumped - UPPER_DECAY * upper + share * work
    )
    return advanced, current, upper_next, pumped_next


def pack_kernel(
    electric, classes, index, polar, popul, freq, dephase, strength, pumping, out, base, left
):
    for i in range(2):
        for c in range(3):
            out[:, 3 * i + c, :] = polar[i, c, 0]
    for i in range(2):
        out[:, 6 + i, :] = popul[i, 0]
    for f, source in enumerate((freq, dephase, strength, pumping)):
        out[:, 8 + f, :] = source[0]
    out[:, 12, :] = index[0].astype(jnp.float32)
    _, nx, ny, depth = electric.shape
    rows = nx * ny
    for c in range(3):
        base[c] = electric[c].reshape(rows, depth)
    base[3] = inverse_permittivity(classes[...].reshape(rows, depth)) * -(TIME_STEP**2)
    left[...] = cell_halves([base[c] for c in range(3)])


def source_of(base, coefs, strip, f):
    if f < GRID:
        return base.at[f]
    return coefs.at[f - GRID] if f < FIELDS else strip.at[f - FIELDS]


def first_kernel(arrived, base, left, coefs, states, row_hot, depth_hot, *strip):
    _, rows, depth = base.shape
    index = arrived[:, 12, :].astype(jnp.int32)
    write_one_hots(index, row_hot, depth_hot, rows, depth)
    sample = gather_cells(left[...], index, row_hot, depth)
    constants = emitter_constants(arrived)
    keep, back, drive, share, pumping = constants
    start = [arrived[:, c, :] for c in range(3)]
    before = [arrived[:, 3 + c, :] for c in range(3)]
    now, _, upper, pumped = bloch_step(
        sample, start, before, arrived[:, 6, :], arrived[:, 7, :], constants
    )
    for c in range(3):
        states[c] = now[c]
        states[3 + c] = start[c]
    states[6] = upper
    states[7] = pumped
    lower = 1.0 - upper - pumped
    push = drive * (lower - upper)
    pumped_after = pumped + TIME_STEP * (pumping * lower - PUMP_DECAY * pumped)
    upper_free = upper + TIME_STEP * (PUMP_DECAY * pumped - UPPER_DECAY * upper)
    free = [keep * n - back * s for n, s in zip(now, start)]
    values = [n - s for n, s in zip(now, start)]
    values += [f - n for f, n in zip(free, now)]
    values.append(push)
    values += [(keep - 1.0) * f - back * n for f, n in zip(free, now)]
    values.append((keep - 1.0) * push)
    values.append(drive * (1.0 - pumped_after - 2.0 * upper_free))
    values += [-drive * share * (f - s) for f, s in zip(free, start)]
    values.append(-drive * share * push)
    values = [value * (1.0 / TIME_STEP**2) for value in values]
    for number, block in enumerate(scatter_cells(values, row_hot, depth_hot, rows)):
        coefs[number] = block
    lane = lax.broadcasted_iota(jnp.int32, (rows, depth), 1)
    strips = len(strip)
    for i in range(strips):
        top = 1 - i if strips > 1 else jnp.where(lax.axis_index("gz") == 0, 1, 0)
        packed = jnp.zeros((rows, depth), jnp.float32)
        for f, width in enumerate(WIDTHS):
            at = LANE_BASES[f]
            turned = pltpu.roll(source_of(base, coefs, None, f)[...], at + width * top, 1)
            packed = jnp.where((lane >= at) & (lane < at + width), turned, packed)
        strip[i][0] = packed


def join_kernel(first, second, out):
    out[0] = first[0]
    out[1] = second[0]


def face_plans(strips, y_low, y_high, x_low, x_high):
    return (
        (y_low, low_layers(1, strips), -1, 1),
        (y_high, high_layers(strips), 1, 1),
        (x_low, low_layers(0, strips), -1, 0),
        (x_high, high_layers(strips), 1, 0),
    )


def face_layer(source, nx, ny, axis, sign, d):
    at = d if sign < 0 else (nx, ny)[axis] - 1 - d
    if axis == 1:
        return source[pl.ds(at, nx, stride=ny), :]
    return source[at * ny : (at + 1) * ny, :]


def faces_kernel(nx, ny, strips, base, coefs, *faces):
    for face, layers, sign, axis in face_plans(strips, *faces):
        count = nx if axis == 1 else ny
        for at, (f, d) in enumerate(layers):
            if f < FIELDS:
                source = source_of(base, coefs, None, f)
                face[at * count : (at + 1) * count, :] = face_layer(source, nx, ny, axis, sign, d)


def face_strips_kernel(nx, ny, strip, *faces):
    strips = strip.shape[0]
    for face, layers, sign, axis in face_plans(strips, *faces[4:]):
        count = nx if axis == 1 else ny
        for at, (f, _) in enumerate(layers):
            if f >= FIELDS:
                source = strip.at[f - FIELDS]
                value = share_lanes(
                    [face_layer(source, nx, ny, axis, sign, d) for d in range(STEPS)]
                )
                face[at * count : (at + 1) * count, :] = value


def corners_kernel(nx, strips, halo_low, halo_high, low, high):
    for face, sign in ((low, -1), (high, 1)):
        for row, (f, d, side, e) in enumerate(corner_rows(-sign, strips)):
            x = d if sign < 0 else nx - 1 - d
            halo = halo_low if side < 0 else halo_high
            layers = high_layers(strips) if side < 0 else low_layers(1, strips)
            at = layers.index((f, e if f < FIELDS else 0))
            value = halo[at * nx + x : at * nx + x + 1, :]
            face[row : row + 1, :] = value if f < FIELDS else layer_of_shared(value, e)


def place(cells, wide, wide_strip, f):
    if f < 3:
        return cells.at[f]
    return wide.at[f - 3] if f < FIELDS else wide_strip.at[f - FIELDS]


def spread_strip(cells, wide, wide_strip, x, y, count, fields):
    strips, _, _, depth = wide_strip.shape
    values = [wide_strip[i, x, y : y + count] for i in range(strips)]
    upper = lax.broadcasted_iota(jnp.int32, (count, depth), 1) >= depth // 2
    low = lax.axis_index("gz") > 0
    for f in fields:
        at, width = LANE_BASES[f], WIDTHS[f]
        if strips == 1:
            shift = lax.bitwise_and(depth - at - jnp.where(low, width, 0), depth - 1)
            value = pltpu.roll(values[0], shift, 1)
            if f < GRID:
                value = jnp.where(upper == low, value, 0.0)
        else:
            value = jnp.where(
                upper,
                pltpu.roll(values[0], (depth - at - width) % depth, 1),
                pltpu.roll(values[1], (depth - at) % depth, 1),
            )
        place(cells, wide, wide_strip, f)[x, y : y + count, depth : 2 * depth] = value


def assemble_kernel(
    base, coefs, strip, y_low, y_high, cells, wide, wide_strip, field, snaps
):
    _, ex, ey, ez = cells.shape
    nx, ny, depth = ex - 2 * STEPS, ey - 2 * STEPS, ez // 2
    strips = strip.shape[0]
    for f in range(FIELDS + strips):
        source = source_of(base, coefs, strip, f)
        target = place(cells, wide, wide_strip, f)
        target[STEPS : STEPS + nx, 0:ny, 0:depth] = source[...].reshape(nx, ny, depth)
        target[STEPS : STEPS + nx, ny:ey, 0:depth] = jnp.zeros((nx, 2 * STEPS, depth), jnp.float32)
    for halo, layers, sign in (
        (y_low, high_layers(strips), -1),
        (y_high, low_layers(1, strips), 1),
    ):
        for at, (f, first) in enumerate(layers):
            target = place(cells, wide, wide_strip, f)
            rows = halo[at * nx : (at + 1) * nx, :]
            for d in range(STEPS) if f >= FIELDS else (first,):
                y = ey - 1 - d if sign < 0 else ny + d
                value = rows if f < FIELDS else layer_of_shared(rows, d)
                for x in range(nx):
                    target[STEPS + x, y : y + 1, 0:depth] = value[x : x + 1]
    for x in range(STEPS, STEPS + nx):
        spread_strip(cells, wide, wide_strip, x, 0, ey, range(FIELDS))
    inside = inside_mask(ey, ez)
    for step in range(1, STEPS):
        for x in range(STEPS + step - 1, STEPS + nx - step):
            advance_magnetic(cells, field, inside, step, x)
            if x >= STEPS + step:
                advance_electric(cells, wide, field, snaps, step, x)


def side_slabs(nx):
    for d in range(STEPS):
        fields = [f for f in range(FIELDS) if WIDTHS[f] > d]
        yield STEPS - 1 - d, fields
        yield STEPS + nx + d, fields


def sides_kernel(x_low, x_high, _cells, _wide, _strip, cells, wide, wide_strip):
    _, ex, ey, ez = cells.shape
    nx, ny, depth = ex - 2 * STEPS, ey - 2 * STEPS, ez // 2
    strips = wide_strip.shape[0]
    for halo, layers, sign in (
        (x_low, high_layers(strips), -1),
        (x_high, low_layers(0, strips), 1),
    ):
        for at, (f, first) in enumerate(layers):
            rows = halo[at * ny : (at + 1) * ny, :]
            for d in range(STEPS) if f >= FIELDS else (first,):
                x = STEPS - 1 - d if sign < 0 else STEPS + nx + d
                value = rows if f < FIELDS else layer_of_shared(rows, d)
                place(cells, wide, wide_strip, f)[x, 0:ny, 0:depth] = value
    for x, fields in side_slabs(nx):
        for f in (*fields, *range(FIELDS, FIELDS + strips)):
            target = place(cells, wide, wide_strip, f)
            target[x, ny:ey, :] = jnp.zeros((2 * STEPS, target.shape[2]), jnp.float32)
        spread_strip(cells, wide, wide_strip, x, 0, ny, fields)


def rolls(ey, ez):
    return (
        lambda v: pltpu.roll(v, ey - 1, 0),
        lambda v: pltpu.roll(v, ez - 1, 1),
        lambda v: pltpu.roll(v, 1, 0),
        lambda v: pltpu.roll(v, 1, 1),
    )


def inside_mask(ey, ez):
    row_at = lax.broadcasted_iota(jnp.int32, (ey, ez), 0)
    lane_at = lax.broadcasted_iota(jnp.int32, (ey, ez), 1)
    outside = ((row_at >= ey - STEPS) & (lax.axis_index("gy") == 0)) | (
        (lane_at >= ez - STEPS) & (lax.axis_index("gz") == 0)
    )
    return jnp.where(outside, 0.0, 1.0)


def advance_magnetic(cells, field, inside, step, x):
    _, _, ey, ez = cells.shape
    up_y, up_z, _, _ = rolls(ey, ez)
    e0, e1, e2 = cells[0, x], cells[1, x], cells[2, x]
    f1, f2 = cells[1, x + 1], cells[2, x + 1]
    curl = (
        (up_y(e2) - e2) - (up_z(e1) - e1),
        (up_z(e0) - e0) - (f2 - e2),
        (f1 - e1) - (up_y(e0) - e0),
    )
    mask = inside
    if x < STEPS:
        mask = inside * jnp.where(lax.axis_index("gx") == 0, 0.0, 1.0)
    for c in range(3):
        change = curl[c] * mask
        field[c, x] = field[c, x] + change if step > 1 else change


def backward_curl(field, x):
    _, _, ey, ez = field.shape
    _, _, down_y, down_z = rolls(ey, ez)
    m0, m1, m2 = field[0, x], field[1, x], field[2, x]
    l1, l2 = field[1, x - 1], field[2, x - 1]
    return (
        (m2 - down_y(m2)) - (m1 - down_z(m1)),
        (m0 - down_z(m0)) - (m2 - l2),
        (m1 - l1) - (m0 - down_y(m0)),
    )


def advance_electric(cells, wide, field, snaps, step, x):
    curl = backward_curl(field, x)
    old = [cells[c, x] for c in range(3)]
    if step == 2:
        gain = wide[7, x]
        source = [wide[4 + c, x] + gain * old[c] for c in range(3)]
        if STEPS - 2 < x < wide.shape[1] - STEPS + 1:
            ratio = wide[11, x]
            for c in range(3):
                wide[8 + c, x] = wide[8 + c, x] + ratio * old[c]
            square = old[0] * old[0] + old[1] * old[1] + old[2] * old[2]
            wide[12, x] = (
                wide[12, x]
                + (wide[13, x] * old[0] + wide[14, x] * old[1] + wide[15, x] * old[2])
                + wide[16, x] * square
            )
    elif step == 3:
        gain = wide[12, x]
        source = [wide[8 + c, x] + gain * old[c] for c in range(3)]
    else:
        source = [wide[1 + c, x] for c in range(3)]
    scale = wide[0, x]
    _, rows, depth = snaps.shape
    ny = cells.shape[2] - 2 * STEPS
    at = (x - STEPS) * ny
    for c in range(3):
        new = old[c] + scale * (curl[c] + source[c])
        cells[c, x] = new
        if 0 <= at < rows:
            snaps[(step - 1) * 3 + c, at : at + ny, :] = new[0:ny, 0:depth]


def steps_kernel(
    c_low, c_high, _cells, _wide, _field, _snaps, wide_strip, row_hot, depth_hot,
    arrived, states, cells, wide, field, snaps, result, changes,
):
    _, ex, ey, ez = wide.shape
    nx, ny, depth = ex - 2 * STEPS, ey - 2 * STEPS, ez // 2
    rows = nx * ny
    for corner, sign in ((c_low, -1), (c_high, 1)):
        for row, (f, d, side, e) in enumerate(corner_rows(sign, wide_strip.shape[0])):
            x = STEPS - 1 - d if sign < 0 else STEPS + nx + d
            y = ey - 1 - e if side < 0 else ny + e
            place(cells, wide, wide_strip, f)[x, y : y + 1, 0:depth] = corner[row : row + 1, :]
    for x, fields in side_slabs(nx):
        fields = [f for f in fields if WIDTHS[f] > 1]
        spread_strip(cells, wide, wide_strip, x, ny, 2 * STEPS, fields)
    inside = inside_mask(ey, ez)
    index = arrived[:, 12, :].astype(jnp.int32)
    constants = emitter_constants(arrived)
    current = [states[c] for c in range(3)]
    previous = [states[3 + c] for c in range(3)]
    upper = states[6]
    pumped = states[7]
    for step in range(1, STEPS + 1):
        if step > 1:
            own = [snaps[(step - 2) * 3 + c] for c in range(3)]
            sample = gather_cells(cell_halves(own), index, row_hot, depth)
            advanced, previous, upper, pumped = bloch_step(
                sample, current, previous, upper, pumped, constants
            )
            if step == STEPS:
                change = [
                    (a - c) * (1.0 / TIME_STEP**2) for a, c in zip(advanced, current)
                ]
            current = advanced
        if step < STEPS:
            done = range(STEPS + step, STEPS + nx - step)
            for x in range(step - 1, ex - step):
                if x not in done and x + 1 not in done:
                    advance_magnetic(cells, field, inside, step, x)
                if x not in done and x >= step:
                    advance_electric(cells, wide, field, snaps, step, x)
    for c in range(3):
        result[:, c, :] = current[c]
        result[:, 3 + c, :] = previous[c]
    result[:, 6, :] = upper
    result[:, 7, :] = pumped
    for c in range(3):
        changes[c] = change[c]


def last_kernel(cells, base, field, changes, row_hot, depth_hot, electric, magnetic):
    _, nx, ny, depth = electric.shape
    rows = nx * ny
    ey, ez = cells.shape[2:]
    sources = scatter_cells([changes[c] for c in range(3)], row_hot, depth_hot, rows)
    inside = inside_mask(ey, ez)
    advance_magnetic(cells, field, inside, STEPS, STEPS - 1)
    for x in range(STEPS, STEPS + nx):
        advance_magnetic(cells, field, inside, STEPS, x)
        curl = backward_curl(field, x)
        span = slice((x - STEPS) * ny, (x - STEPS + 1) * ny)
        scale = base[3, span]
        for c in range(3):
            own = curl[c][0:ny, 0:depth] + sources[c][span]
            electric[c, x - STEPS] = cells[c, x, 0:ny, 0:depth] + scale * own
            magnetic[c, x - STEPS] = field[c, x, 0:ny, 0:depth] * -TIME_STEP


def unpack_kernel(home, polar, popul):
    for i in range(2):
        for c in range(3):
            polar[i, c, 0] = home[:, 3 * i + c, :]
        popul[i, 0] = home[:, 6 + i, :]


def call(kernel, outs, final=(), aliases=None, limit=VMEM_LIMIT, cost=None):
    shapes = [pltpu.VMEM(s[:-1], s[-1]) if isinstance(s[-1], type) else pltpu.VMEM(s, jnp.float32) for s in outs]
    shapes += [jax.ShapeDtypeStruct(s, jnp.float32) for s in final]
    return pl.pallas_call(
        kernel,
        out_shape=shapes,
        input_output_aliases=aliases or {},
        cost_estimate=cost,
        compiler_params=pltpu.CompilerParams(vmem_limit_bytes=limit),
    )


def near(*values):
    return [pltpu.with_memory_space_constraint(v, pltpu.VMEM) for v in values]


def shifted(value, axis, step):
    count = lax.axis_size(axis)
    pairs = [(i, i + step) for i in range(count) if 0 <= i + step < count]
    return lax.ppermute(value, axis, pairs)


def shards(
    electric, permittivity_class, cell_index, polarization, populations,
    resonance, dephasing, coupling, pump_rate,
):
    _, nx, ny, depth = electric.shape
    rows = nx * ny
    _, buckets, slots = cell_index.shape
    ex, ey, ez = nx + 2 * STEPS, ny + 2 * STEPS, 2 * depth
    hots = [
        (FOLDS * rows, buckets * slots, jnp.bfloat16),
        (depth // FOLDS, buckets * slots, jnp.bfloat16),
    ]
    packed, base, left = near(
        *call(
            pack_kernel,
            [
                (buckets, 13, slots),
                (GRID, rows, depth),
                (6 * depth // FOLDS, FOLDS * rows, jnp.bfloat16),
            ],
            limit=HIGH_LIMIT,
        )(
            electric, permittivity_class, cell_index, polarization, populations,
            resonance, dephasing, coupling, pump_rate,
        )
    )
    arrived = lax.all_to_all(packed, ("gy", "gz"), split_axis=0, concat_axis=0, tiled=True)
    (arrived,) = near(arrived)
    strips = 1 if lax.axis_size("gz") == 2 else 2
    coefs, states, row_hot, depth_hot, *strip = near(
        *call(
            first_kernel,
            [
                (FIELDS - GRID, rows, depth),
                (8, buckets, slots),
                *hots,
                *[(1, rows, depth)] * strips,
            ],
        )(arrived, base, left)
    )
    high = len(high_layers(strips))
    shapes = [
        (len(low_layers(1, strips)) * nx, depth),
        (high * nx, depth),
        (len(low_layers(0, strips)) * ny, depth),
        (high * ny, depth),
    ]
    faces = near(*call(functools.partial(faces_kernel, nx, ny, strips), shapes)(base, coefs))
    if strips == 1:
        (strip,) = near(lax.ppermute(strip[0], "gz", [(0, 1), (1, 0)]))
    else:
        strip = near(shifted(strip[0], "gz", 1), shifted(strip[1], "gz", -1))
        (strip,) = near(*call(join_kernel, [(strips, rows, depth)])(*strip))
    faces = call(
        functools.partial(face_strips_kernel, nx, ny),
        shapes,
        aliases={1: 0, 2: 1, 3: 2, 4: 3},
    )(strip, *faces)
    y_low, y_high = near(shifted(faces[1], "gy", 1), shifted(faces[0], "gy", -1))
    x_low, x_high = near(shifted(faces[3], "gx", 1), shifted(faces[2], "gx", -1))
    low, high = call(
        functools.partial(corners_kernel, nx, strips),
        [corner_shape(1, strips, depth), corner_shape(-1, strips, depth)],
        cost=LONG,
    )(y_low, y_high)
    c_low, c_high = near(shifted(high, "gx", 1), shifted(low, "gx", -1))
    state = near(
        *call(
            assemble_kernel,
            [
                (3, ex, ey, ez),
                (FIELDS - 3, ex, ey, ez),
                (strips, ex, ey, depth),
                (3, ex, ey, ez),
                (3 * (STEPS - 1), rows, depth),
            ],
        )(base, coefs, strip, y_low, y_high)
    )
    cells, wide, wide_strip, field, snaps = state
    cells, wide, wide_strip = near(
        *call(
            sides_kernel,
            [cells.shape, wide.shape, wide_strip.shape],
            aliases={2: 0, 3: 1, 4: 2},
        )(x_low, x_high, cells, wide, wide_strip)
    )
    cells, _, field, _, result, changes = near(
        *call(
            steps_kernel,
            [
                cells.shape,
                wide.shape,
                field.shape,
                snaps.shape,
                (buckets, 8, slots),
                (3, buckets, slots),
            ],
            aliases={2: 0, 3: 1, 4: 2, 5: 3},
        )(c_low, c_high, cells, wide, field, snaps, wide_strip, row_hot, depth_hot, arrived, states)
    )
    home = lax.all_to_all(result, ("gy", "gz"), split_axis=0, concat_axis=0, tiled=True)
    electric, magnetic = call(last_kernel, [], [electric.shape, electric.shape])(
        cells, base, field, changes, row_hot, depth_hot
    )
    polar_out, popul_out = call(unpack_kernel, [], [polarization.shape, populations.shape])(
        *near(home)
    )
    return (electric, magnetic, polar_out, popul_out)


def solution(mesh):
    owners = P("gx", ("gy", "gz"), None)
    return jax.shard_map(
        shards,
        mesh=mesh,
        in_specs=(
            P(None, "gx", "gy", "gz"),
            P("gx", "gy", "gz"),
            owners,
            P(None, None, "gx", ("gy", "gz"), None),
            P(None, "gx", ("gy", "gz"), None),
            owners,
            owners,
            owners,
            owners,
        ),
        out_specs=(
            P(None, "gx", "gy", "gz"),
            P(None, "gx", "gy", "gz"),
            P(None, None, "gx", ("gy", "gz"), None),
            P(None, "gx", ("gy", "gz"), None),
        ),
        check_vma=False,
    )
```

```python
import functools

import jax
import jax.numpy as jnp
from jax import lax
from jax.experimental import pallas as pl
from jax.experimental.pallas import tpu as pltpu
from jax.sharding import PartitionSpec as P

STEPS = 4
TIME_STEP = 0.5
PUMP_DECAY = 0.2
UPPER_DECAY = 0.02
WORK_SHARE = 0.05
CLASS_PERMITTIVITY = (1.0, 2.1, 6.0, 12.25)

WIDTHS = (STEPS,) * 3 + (STEPS - 1,) * 4 + (STEPS - 2,) * 4 + (STEPS - 3,) * 9
FIELDS = len(WIDTHS)
GRID = 4
VECTORS = (0, 4, 7, 11)
LANE_BASES = tuple(sum(WIDTHS[:i]) for i in range(FIELDS))
LAYER_LANES = tuple(sum(w for w in WIDTHS if w > d) for d in range(STEPS))
LAYER_BASES = tuple(sum(LAYER_LANES[:d]) for d in range(STEPS + 1))
FOLDS = 2
LONG = pl.CostEstimate(flops=20_000_000_000, bytes_accessed=100_000_000, transcendentals=0)
VMEM_LIMIT = 24 * 1024 * 1024
HIGH_LIMIT = 56 * 1024 * 1024


def layer_list(skip_axis, strips):
    layers = []
    for f, width in enumerate(WIDTHS):
        unused = skip_axis is not None and f - skip_axis in VECTORS
        layers += [(f, d) for d in range(width - 1 if unused else width)]
    return layers + [(FIELDS + i, 0) for i in range(strips)]


def low_layers(axis, strips):
    return layer_list(axis, strips)


def high_layers(strips):
    return layer_list(None, strips)


def corner_rows(halo_sign, strips):
    out = []
    furthest = 0 if halo_sign < 0 else 1
    known_x = high_layers(0) if halo_sign < 0 else low_layers(0, 0)
    for f, width in enumerate(WIDTHS + (STEPS,) * strips):
        for d in range(width):
            if f < FIELDS and (f, d) not in known_x:
                continue
            for side in (-1, 1):
                reach = width - d
                if f >= FIELDS or side == halo_sign or any(
                    f in (v, v + 1, v + 2) and f != v + furthest for v in VECTORS
                ):
                    reach -= 1
                known = high_layers(0) if side < 0 else low_layers(1, 0)
                out += [
                    (f, d, side, e)
                    for e in range(reach)
                    if f >= FIELDS or (f, e) in known
                ]
    return out


def corner_shape(halo_sign, strips, depth):
    return (-(-len(corner_rows(halo_sign, strips)) // 8) * 8, depth)


def share_lanes(layers):
    lane = lax.broadcasted_iota(jnp.int32, layers[0].shape, 1)
    out = layers[0]
    for d in range(1, STEPS):
        turned = pltpu.roll(layers[d], LAYER_BASES[d], 1)
        out = jnp.where(lane >= LAYER_BASES[d], turned, out)
    return out


def layer_of_shared(shared, d):
    depth = shared.shape[1]
    return pltpu.roll(shared, depth - LAYER_BASES[d], 1) if d else shared


def inverse_permittivity(classes):
    inverse = jnp.zeros(classes.shape, jnp.float32)
    for number, epsilon in enumerate(CLASS_PERMITTIVITY):
        inverse = jnp.where(classes == number, 1.0 / epsilon, inverse)
    return inverse


def halves(value):
    high = value.astype(jnp.bfloat16)
    low = (value - high.astype(jnp.float32)).astype(jnp.bfloat16)
    return high, low


def write_one_hots(index, row_hot, depth_hot, rows, depth):
    fold = depth // FOLDS
    shift = depth.bit_length() - 1
    buckets, slots = index.shape
    live = index < rows * depth
    part = lax.shift_right_logical(lax.bitwise_and(index, depth - 1), fold.bit_length() - 1)
    row = lax.shift_right_logical(index, shift) + part * rows
    row = jnp.where(live, row, -1)
    deep = lax.bitwise_and(index, fold - 1)
    rows_at = lax.broadcasted_iota(jnp.int32, (FOLDS * rows, slots), 0)
    deep_at = lax.broadcasted_iota(jnp.int32, (fold, slots), 0)
    for b in range(buckets):
        span = slice(b * slots, (b + 1) * slots)
        row_hot[:, span] = jnp.where(rows_at == row[b : b + 1], 1.0, 0.0).astype(jnp.bfloat16)
        depth_hot[:, span] = jnp.where(deep_at == deep[b : b + 1], 1.0, 0.0).astype(jnp.bfloat16)


def cell_halves(cells):
    parts = []
    for block in cells:
        turned = block.T
        fold = turned.shape[0] // FOLDS
        turned = [turned[i * fold : (i + 1) * fold] for i in range(FOLDS)]
        parts += halves(jnp.concatenate(turned, axis=1))
    return jnp.concatenate(parts, axis=0)


def gather_cells(left, index, row_hot, depth):
    buckets, slots = index.shape
    fold = depth // FOLDS
    size = 2 * fold
    samples = [[], [], []]
    group = 2 if buckets % 2 == 0 else 1
    place_at = lax.broadcasted_iota(jnp.int32, (size, slots), 0)
    place_at = lax.bitwise_and(place_at, fold - 1)
    for start in range(0, buckets, group):
        span = slice(start * slots, (start + group) * slots)
        picked = jnp.dot(left, row_hot[:, span], preferred_element_type=jnp.float32)
        for b in range(start, start + group):
            hit = place_at == lax.bitwise_and(index[b : b + 1], fold - 1)
            lanes = slice((b - start) * slots, (b - start + 1) * slots)
            for c in range(3):
                part = picked[c * size : (c + 1) * size, lanes]
                samples[c].append(jnp.sum(jnp.where(hit, part, 0.0), axis=0, keepdims=True))
    return [jnp.concatenate(rows, axis=0) for rows in samples]


def flat_row(value):
    buckets = value.shape[0]
    return jnp.concatenate([value[b : b + 1] for b in range(buckets)], axis=1)


def scatter_cells(values, row_hot, depth_hot, rows, group=4):
    hot = row_hot[...]
    deep = depth_hot[...]
    fold = deep.shape[0]
    out = []
    for start in range(0, len(values), group):
        some = [halves(flat_row(value)) for value in values[start : start + group]]
        total = 0.0
        for part in range(2):
            spread = jnp.concatenate([deep * pair[part] for pair in some], axis=0)
            total = total + lax.dot_general(
                spread, hot, (((1,), (1,)), ((), ())), preferred_element_type=jnp.float32
            )
        for i in range(len(some)):
            block = total[i * fold : (i + 1) * fold]
            block = [block[:, j * rows : (j + 1) * rows] for j in range(FOLDS)]
            out.append(jnp.concatenate(block, axis=0).T)
    return out


def emitter_constants(arrived):
    freq, dephase, strength, pumping = [arrived[:, f, :] for f in range(8, 12)]
    damping = 0.5 * TIME_STEP * dephase
    stiffness = freq * TIME_STEP * (freq * TIME_STEP)
    scale = 1.0 + damping
    keep = (2.0 - stiffness) / scale
    back = (1.0 - damping) / scale
    drive = strength * (TIME_STEP * TIME_STEP) / scale
    share = WORK_SHARE / freq
    return keep, back, drive, share, pumping


def bloch_step(sample, current, previous, upper, pumped, constants):
    keep, back, drive, share, pumping = constants
    lower = 1.0 - upper - pumped
    push = drive * (lower - upper)
    advanced = [keep * c - back * p + push * s for c, p, s in zip(current, previous, sample)]
    work = sum(s * (a - p) for s, a, p in zip(sample, advanced, previous)) / (2.0 * TIME_STEP)
    pumped_next = pumped + TIME_STEP * (pumping * lower - PUMP_DECAY * pumped)
    upper_next = upper + TIME_STEP * (
        PUMP_DECAY * pumped - UPPER_DECAY * upper + share * work
    )
    return advanced, current, upper_next, pumped_next


def pack_kernel(
    electric, classes, index, polar, popul, freq, dephase, strength, pumping, out, base, left
):
    for i in range(2):
        for c in range(3):
            out[:, 3 * i + c, :] = polar[i, c, 0]
    for i in range(2):
        out[:, 6 + i, :] = popul[i, 0]
    for f, source in enumerate((freq, dephase, strength, pumping)):
        out[:, 8 + f, :] = source[0]
    out[:, 12, :] = index[0].astype(jnp.float32)
    _, nx, ny, depth = electric.shape
    rows = nx * ny
    for c in range(3):
        base[c] = electric[c].reshape(rows, depth)
    base[3] = inverse_permittivity(classes[...].reshape(rows, depth)) * -(TIME_STEP**2)
    left[...] = cell_halves([base[c] for c in range(3)])


def source_of(base, coefs, strip, f):
    if f < GRID:
        return base.at[f]
    return coefs.at[f - GRID] if f < FIELDS else strip.at[f - FIELDS]


def first_kernel(arrived, base, left, coefs, states, row_hot, depth_hot, *strip):
    _, rows, depth = base.shape
    index = arrived[:, 12, :].astype(jnp.int32)
    write_one_hots(index, row_hot, depth_hot, rows, depth)
    sample = gather_cells(left[...], index, row_hot, depth)
    constants = emitter_constants(arrived)
    keep, back, drive, share, pumping = constants
    start = [arrived[:, c, :] for c in range(3)]
    before = [arrived[:, 3 + c, :] for c in range(3)]
    now, _, upper, pumped = bloch_step(
        sample, start, before, arrived[:, 6, :], arrived[:, 7, :], constants
    )
    for c in range(3):
        states[c] = now[c]
        states[3 + c] = start[c]
    states[6] = upper
    states[7] = pumped
    lower = 1.0 - upper - pumped
    push = drive * (lower - upper)
    pumped_after = pumped + TIME_STEP * (pumping * lower - PUMP_DECAY * pumped)
    upper_free = upper + TIME_STEP * (PUMP_DECAY * pumped - UPPER_DECAY * upper)
    free = [keep * n - back * s for n, s in zip(now, start)]
    values = [n - s for n, s in zip(now, start)]
    values += [f - n for f, n in zip(free, now)]
    values.append(push)
    values += [(keep - 1.0) * f - back * n for f, n in zip(free, now)]
    values.append((keep - 1.0) * push)
    values.append(drive * (1.0 - pumped_after - 2.0 * upper_free))
    values += [-drive * share * (f - s) for f, s in zip(free, start)]
    values.append(-drive * share * push)
    values = [value * (1.0 / TIME_STEP**2) for value in values]
    for number, block in enumerate(scatter_cells(values, row_hot, depth_hot, rows)):
        coefs[number] = block
    lane = lax.broadcasted_iota(jnp.int32, (rows, depth), 1)
    strips = len(strip)
    for i in range(strips):
        top = 1 - i if strips > 1 else jnp.where(lax.axis_index("gz") == 0, 1, 0)
        packed = jnp.zeros((rows, depth), jnp.float32)
        for f, width in enumerate(WIDTHS):
            at = LANE_BASES[f]
            turned = pltpu.roll(source_of(base, coefs, None, f)[...], at + width * top, 1)
            packed = jnp.where((lane >= at) & (lane < at + width), turned, packed)
        strip[i][0] = packed


def join_kernel(first, second, out):
    out[0] = first[0]
    out[1] = second[0]


def face_plans(strips, y_low, y_high, x_low, x_high):
    return (
        (y_low, low_layers(1, strips), -1, 1),
        (y_high, high_layers(strips), 1, 1),
        (x_low, low_layers(0, strips), -1, 0),
        (x_high, high_layers(strips), 1, 0),
    )


def face_layer(source, nx, ny, axis, sign, d):
    at = d if sign < 0 else (nx, ny)[axis] - 1 - d
    if axis == 1:
        return source[pl.ds(at, nx, stride=ny), :]
    return source[at * ny : (at + 1) * ny, :]


def faces_kernel(nx, ny, strips, base, coefs, *faces):
    for face, layers, sign, axis in face_plans(strips, *faces):
        count = nx if axis == 1 else ny
        for at, (f, d) in enumerate(layers):
            if f < FIELDS:
                source = source_of(base, coefs, None, f)
                face[at * count : (at + 1) * count, :] = face_layer(source, nx, ny, axis, sign, d)


def face_strips_kernel(nx, ny, strip, *faces):
    strips = strip.shape[0]
    for face, layers, sign, axis in face_plans(strips, *faces[4:]):
        count = nx if axis == 1 else ny
        for at, (f, _) in enumerate(layers):
            if f >= FIELDS:
                source = strip.at[f - FIELDS]
                value = share_lanes(
                    [face_layer(source, nx, ny, axis, sign, d) for d in range(STEPS)]
                )
                face[at * count : (at + 1) * count, :] = value


def corners_kernel(nx, strips, halo_low, halo_high, low, high):
    for face, sign in ((low, -1), (high, 1)):
        for row, (f, d, side, e) in enumerate(corner_rows(-sign, strips)):
            x = d if sign < 0 else nx - 1 - d
            halo = halo_low if side < 0 else halo_high
            layers = high_layers(strips) if side < 0 else low_layers(1, strips)
            at = layers.index((f, e if f < FIELDS else 0))
            value = halo[at * nx + x : at * nx + x + 1, :]
            face[row : row + 1, :] = value if f < FIELDS else layer_of_shared(value, e)


def place(cells, wide, wide_strip, f):
    if f < 3:
        return cells.at[f]
    return wide.at[f - 3] if f < FIELDS else wide_strip.at[f - FIELDS]


def spread_strip(cells, wide, wide_strip, x, y, count, fields):
    strips, _, _, depth = wide_strip.shape
    values = [wide_strip[i, x, y : y + count] for i in range(strips)]
    upper = lax.broadcasted_iota(jnp.int32, (count, depth), 1) >= depth // 2
    low = lax.axis_index("gz") > 0
    for f in fields:
        at, width = LANE_BASES[f], WIDTHS[f]
        if strips == 1:
            shift = lax.bitwise_and(depth - at - jnp.where(low, width, 0), depth - 1)
            value = pltpu.roll(values[0], shift, 1)
            if f < GRID:
                value = jnp.where(upper == low, value, 0.0)
        else:
            value = jnp.where(
                upper,
                pltpu.roll(values[0], (depth - at - width) % depth, 1),
                pltpu.roll(values[1], (depth - at) % depth, 1),
            )
        place(cells, wide, wide_strip, f)[x, y : y + count, depth : 2 * depth] = value


def assemble_kernel(
    base, coefs, strip, y_low, y_high, cells, wide, wide_strip, field, snaps
):
    _, ex, ey, ez = cells.shape
    nx, ny, depth = ex - 2 * STEPS, ey - 2 * STEPS, ez // 2
    strips = strip.shape[0]
    for f in range(FIELDS + strips):
        source = source_of(base, coefs, strip, f)
        target = place(cells, wide, wide_strip, f)
        target[STEPS : STEPS + nx, 0:ny, 0:depth] = source[...].reshape(nx, ny, depth)
        target[STEPS : STEPS + nx, ny:ey, 0:depth] = jnp.zeros((nx, 2 * STEPS, depth), jnp.float32)
    for halo, layers, sign in (
        (y_low, high_layers(strips), -1),
        (y_high, low_layers(1, strips), 1),
    ):
        for at, (f, first) in enumerate(layers):
            target = place(cells, wide, wide_strip, f)
            rows = halo[at * nx : (at + 1) * nx, :]
            for d in range(STEPS) if f >= FIELDS else (first,):
                y = ey - 1 - d if sign < 0 else ny + d
                value = rows if f < FIELDS else layer_of_shared(rows, d)
                for x in range(nx):
                    target[STEPS + x, y : y + 1, 0:depth] = value[x : x + 1]
    for x in range(STEPS, STEPS + nx):
        spread_strip(cells, wide, wide_strip, x, 0, ey, range(FIELDS))
    inside = inside_mask(ey, ez)
    for step in range(1, STEPS):
        for x in range(STEPS + step - 1, STEPS + nx - step):
            advance_magnetic(cells, field, inside, step, x)
            if x >= STEPS + step:
                advance_electric(cells, wide, field, snaps, step, x)


def side_slabs(nx):
    for d in range(STEPS):
        fields = [f for f in range(FIELDS) if WIDTHS[f] > d]
        yield STEPS - 1 - d, fields
        yield STEPS + nx + d, fields


def sides_kernel(x_low, x_high, _cells, _wide, _strip, cells, wide, wide_strip):
    _, ex, ey, ez = cells.shape
    nx, ny, depth = ex - 2 * STEPS, ey - 2 * STEPS, ez // 2
    strips = wide_strip.shape[0]
    for halo, layers, sign in (
        (x_low, high_layers(strips), -1),
        (x_high, low_layers(0, strips), 1),
    ):
        for at, (f, first) in enumerate(layers):
            rows = halo[at * ny : (at + 1) * ny, :]
            for d in range(STEPS) if f >= FIELDS else (first,):
                x = STEPS - 1 - d if sign < 0 else STEPS + nx + d
                value = rows if f < FIELDS else layer_of_shared(rows, d)
                place(cells, wide, wide_strip, f)[x, 0:ny, 0:depth] = value
    for x, fields in side_slabs(nx):
        for f in (*fields, *range(FIELDS, FIELDS + strips)):
            target = place(cells, wide, wide_strip, f)
            target[x, ny:ey, :] = jnp.zeros((2 * STEPS, target.shape[2]), jnp.float32)
        spread_strip(cells, wide, wide_strip, x, 0, ny, fields)


def rolls(ey, ez):
    return (
        lambda v: pltpu.roll(v, ey - 1, 0),
        lambda v: pltpu.roll(v, ez - 1, 1),
        lambda v: pltpu.roll(v, 1, 0),
        lambda v: pltpu.roll(v, 1, 1),
    )


def inside_mask(ey, ez):
    row_at = lax.broadcasted_iota(jnp.int32, (ey, ez), 0)
    lane_at = lax.broadcasted_iota(jnp.int32, (ey, ez), 1)
    outside = ((row_at >= ey - STEPS) & (lax.axis_index("gy") == 0)) | (
        (lane_at >= ez - STEPS) & (lax.axis_index("gz") == 0)
    )
    return jnp.where(outside, 0.0, 1.0)


def advance_magnetic(cells, field, inside, step, x):
    _, _, ey, ez = cells.shape
    up_y, up_z, _, _ = rolls(ey, ez)
    e0, e1, e2 = cells[0, x], cells[1, x], cells[2, x]
    f1, f2 = cells[1, x + 1], cells[2, x + 1]
    curl = (
        (up_y(e2) - e2) - (up_z(e1) - e1),
        (up_z(e0) - e0) - (f2 - e2),
        (f1 - e1) - (up_y(e0) - e0),
    )
    mask = inside
    if x < STEPS:
        mask = inside * jnp.where(lax.axis_index("gx") == 0, 0.0, 1.0)
    for c in range(3):
        change = curl[c] * mask
        field[c, x] = field[c, x] + change if step > 1 else change


def backward_curl(field, x):
    _, _, ey, ez = field.shape
    _, _, down_y, down_z = rolls(ey, ez)
    m0, m1, m2 = field[0, x], field[1, x], field[2, x]
    l1, l2 = field[1, x - 1], field[2, x - 1]
    return (
        (m2 - down_y(m2)) - (m1 - down_z(m1)),
        (m0 - down_z(m0)) - (m2 - l2),
        (m1 - l1) - (m0 - down_y(m0)),
    )


def advance_electric(cells, wide, field, snaps, step, x):
    curl = backward_curl(field, x)
    old = [cells[c, x] for c in range(3)]
    if step == 2:
        gain = wide[7, x]
        source = [wide[4 + c, x] + gain * old[c] for c in range(3)]
        if STEPS - 2 < x < wide.shape[1] - STEPS + 1:
            ratio = wide[11, x]
            for c in range(3):
                wide[8 + c, x] = wide[8 + c, x] + ratio * old[c]
            square = old[0] * old[0] + old[1] * old[1] + old[2] * old[2]
            wide[12, x] = (
                wide[12, x]
                + (wide[13, x] * old[0] + wide[14, x] * old[1] + wide[15, x] * old[2])
                + wide[16, x] * square
            )
    elif step == 3:
        gain = wide[12, x]
        source = [wide[8 + c, x] + gain * old[c] for c in range(3)]
    else:
        source = [wide[1 + c, x] for c in range(3)]
    scale = wide[0, x]
    _, rows, depth = snaps.shape
    ny = cells.shape[2] - 2 * STEPS
    at = (x - STEPS) * ny
    for c in range(3):
        new = old[c] + scale * (curl[c] + source[c])
        cells[c, x] = new
        if 0 <= at < rows:
            snaps[(step - 1) * 3 + c, at : at + ny, :] = new[0:ny, 0:depth]


def steps_kernel(
    c_low, c_high, _cells, _wide, _field, _snaps, wide_strip, row_hot, depth_hot,
    arrived, states, cells, wide, field, snaps, result, changes, edges,
):
    _, ex, ey, ez = wide.shape
    nx, ny, depth = ex - 2 * STEPS, ey - 2 * STEPS, ez // 2
    rows = nx * ny
    for corner, sign in ((c_low, -1), (c_high, 1)):
        for row, (f, d, side, e) in enumerate(corner_rows(sign, wide_strip.shape[0])):
            x = STEPS - 1 - d if sign < 0 else STEPS + nx + d
            y = ey - 1 - e if side < 0 else ny + e
            place(cells, wide, wide_strip, f)[x, y : y + 1, 0:depth] = corner[row : row + 1, :]
    for x, fields in side_slabs(nx):
        fields = [f for f in fields if WIDTHS[f] > 1]
        spread_strip(cells, wide, wide_strip, x, ny, 2 * STEPS, fields)
    inside = inside_mask(ey, ez)
    index = arrived[:, 12, :].astype(jnp.int32)
    constants = emitter_constants(arrived)
    current = [states[c] for c in range(3)]
    previous = [states[3 + c] for c in range(3)]
    upper = states[6]
    pumped = states[7]
    for step in range(1, STEPS + 1):
        if step > 1:
            own = [snaps[(step - 2) * 3 + c] for c in range(3)]
            sample = gather_cells(cell_halves(own), index, row_hot, depth)
            advanced, previous, upper, pumped = bloch_step(
                sample, current, previous, upper, pumped, constants
            )
            if step == STEPS:
                change = [
                    (a - c) * (1.0 / TIME_STEP**2) for a, c in zip(advanced, current)
                ]
            current = advanced
        if step < STEPS:
            done = range(STEPS + step, STEPS + nx - step)
            spare = step == STEPS - 1
            for x in range(step - 1 + spare, ex - step - spare):
                if x not in done and x + 1 not in done:
                    advance_magnetic(cells, field, inside, step, x)
                if x not in done and x >= step + spare:
                    advance_electric(cells, wide, field, snaps, step, x)
    for c in range(3):
        result[:, c, :] = current[c]
        result[:, 3 + c, :] = previous[c]
    result[:, 6, :] = upper
    result[:, 7, :] = pumped
    for c in range(3):
        changes[c] = change[c]
    for i, x in enumerate((STEPS - 1, STEPS + nx)):
        for c in range(3):
            edges[i, c] = wide[8 + c, x] + wide[12, x] * cells[c, x]
        edges[i, 3] = wide[0, x]


def last_kernel(cells, base, field, changes, edges, row_hot, depth_hot, electric, magnetic):
    _, nx, ny, depth = electric.shape
    rows = nx * ny
    ey, ez = cells.shape[2:]
    sources = scatter_cells([changes[c] for c in range(3)], row_hot, depth_hot, rows)
    inside = inside_mask(ey, ez)
    for x in (STEPS - 2, STEPS + nx):
        advance_magnetic(cells, field, inside, STEPS - 1, x)
    for i, x in enumerate((STEPS - 1, STEPS + nx)):
        curl = backward_curl(field, x)
        for c in range(3):
            cells[c, x] = cells[c, x] + edges[i, 3] * (curl[c] + edges[i, c])
    advance_magnetic(cells, field, inside, STEPS, STEPS - 1)
    for x in range(STEPS, STEPS + nx):
        advance_magnetic(cells, field, inside, STEPS, x)
        curl = backward_curl(field, x)
        span = slice((x - STEPS) * ny, (x - STEPS + 1) * ny)
        scale = base[3, span]
        for c in range(3):
            own = curl[c][0:ny, 0:depth] + sources[c][span]
            electric[c, x - STEPS] = cells[c, x, 0:ny, 0:depth] + scale * own
            magnetic[c, x - STEPS] = field[c, x, 0:ny, 0:depth] * -TIME_STEP


def unpack_kernel(home, polar, popul):
    for i in range(2):
        for c in range(3):
            polar[i, c, 0] = home[:, 3 * i + c, :]
        popul[i, 0] = home[:, 6 + i, :]


def call(kernel, outs, final=(), aliases=None, limit=VMEM_LIMIT, cost=None):
    shapes = [pltpu.VMEM(s[:-1], s[-1]) if isinstance(s[-1], type) else pltpu.VMEM(s, jnp.float32) for s in outs]
    shapes += [jax.ShapeDtypeStruct(s, jnp.float32) for s in final]
    return pl.pallas_call(
        kernel,
        out_shape=shapes,
        input_output_aliases=aliases or {},
        cost_estimate=cost,
        compiler_params=pltpu.CompilerParams(vmem_limit_bytes=limit),
    )


def near(*values):
    return [pltpu.with_memory_space_constraint(v, pltpu.VMEM) for v in values]


def shifted(value, axis, step):
    count = lax.axis_size(axis)
    pairs = [(i, i + step) for i in range(count) if 0 <= i + step < count]
    return lax.ppermute(value, axis, pairs)


def shards(
    electric, permittivity_class, cell_index, polarization, populations,
    resonance, dephasing, coupling, pump_rate,
):
    _, nx, ny, depth = electric.shape
    rows = nx * ny
    _, buckets, slots = cell_index.shape
    ex, ey, ez = nx + 2 * STEPS, ny + 2 * STEPS, 2 * depth
    hots = [
        (FOLDS * rows, buckets * slots, jnp.bfloat16),
        (depth // FOLDS, buckets * slots, jnp.bfloat16),
    ]
    packed, base, left = near(
        *call(
            pack_kernel,
            [
                (buckets, 13, slots),
                (GRID, rows, depth),
                (6 * depth // FOLDS, FOLDS * rows, jnp.bfloat16),
            ],
            limit=HIGH_LIMIT,
        )(
            electric, permittivity_class, cell_index, polarization, populations,
            resonance, dephasing, coupling, pump_rate,
        )
    )
    arrived = lax.all_to_all(packed, ("gy", "gz"), split_axis=0, concat_axis=0, tiled=True)
    (arrived,) = near(arrived)
    strips = 1 if lax.axis_size("gz") == 2 else 2
    coefs, states, row_hot, depth_hot, *strip = near(
        *call(
            first_kernel,
            [
                (FIELDS - GRID, rows, depth),
                (8, buckets, slots),
                *hots,
                *[(1, rows, depth)] * strips,
            ],
        )(arrived, base, left)
    )
    high = len(high_layers(strips))
    shapes = [
        (len(low_layers(1, strips)) * nx, depth),
        (high * nx, depth),
        (len(low_layers(0, strips)) * ny, depth),
        (high * ny, depth),
    ]
    faces = near(*call(functools.partial(faces_kernel, nx, ny, strips), shapes)(base, coefs))
    if strips == 1:
        (strip,) = near(lax.ppermute(strip[0], "gz", [(0, 1), (1, 0)]))
    else:
        strip = near(shifted(strip[0], "gz", 1), shifted(strip[1], "gz", -1))
        (strip,) = near(*call(join_kernel, [(strips, rows, depth)])(*strip))
    faces = call(
        functools.partial(face_strips_kernel, nx, ny),
        shapes,
        aliases={1: 0, 2: 1, 3: 2, 4: 3},
    )(strip, *faces)
    y_low, y_high = near(shifted(faces[1], "gy", 1), shifted(faces[0], "gy", -1))
    x_low, x_high = near(shifted(faces[3], "gx", 1), shifted(faces[2], "gx", -1))
    low, high = call(
        functools.partial(corners_kernel, nx, strips),
        [corner_shape(1, strips, depth), corner_shape(-1, strips, depth)],
        cost=LONG,
    )(y_low, y_high)
    c_low, c_high = near(shifted(high, "gx", 1), shifted(low, "gx", -1))
    state = near(
        *call(
            assemble_kernel,
            [
                (3, ex, ey, ez),
                (FIELDS - 3, ex, ey, ez),
                (strips, ex, ey, depth),
                (3, ex, ey, ez),
                (3 * (STEPS - 1), rows, depth),
            ],
        )(base, coefs, strip, y_low, y_high)
    )
    cells, wide, wide_strip, field, snaps = state
    cells, wide, wide_strip = near(
        *call(
            sides_kernel,
            [cells.shape, wide.shape, wide_strip.shape],
            aliases={2: 0, 3: 1, 4: 2},
        )(x_low, x_high, cells, wide, wide_strip)
    )
    cells, _, field, _, result, changes, edges = near(
        *call(
            steps_kernel,
            [
                cells.shape,
                wide.shape,
                field.shape,
                snaps.shape,
                (buckets, 8, slots),
                (3, buckets, slots),
                (2, 4, ey, ez),
            ],
            aliases={2: 0, 3: 1, 4: 2, 5: 3},
        )(c_low, c_high, cells, wide, field, snaps, wide_strip, row_hot, depth_hot, arrived, states)
    )
    home = lax.all_to_all(result, ("gy", "gz"), split_axis=0, concat_axis=0, tiled=True)
    electric, magnetic = call(last_kernel, [], [electric.shape, electric.shape])(
        cells, base, field, changes, edges, row_hot, depth_hot
    )
    polar_out, popul_out = call(unpack_kernel, [], [polarization.shape, populations.shape])(
        *near(home)
    )
    return (electric, magnetic, polar_out, popul_out)


def solution(mesh):
    owners = P("gx", ("gy", "gz"), None)
    return jax.shard_map(
        shards,
        mesh=mesh,
        in_specs=(
            P(None, "gx", "gy", "gz"),
            P("gx", "gy", "gz"),
            owners,
            P(None, None, "gx", ("gy", "gz"), None),
            P(None, "gx", ("gy", "gz"), None),
            owners,
            owners,
            owners,
            owners,
        ),
        out_specs=(
            P(None, "gx", "gy", "gz"),
            P(None, "gx", "gy", "gz"),
            P(None, None, "gx", ("gy", "gz"), None),
            P(None, "gx", ("gy", "gz"), None),
        ),
        check_vma=False,
    )
```
